32 devices in a mesh: batch: 4 (over y, x), seq: 8 (over z, core).
Axes of the slice: x: 2, y: 2, z: 4, core: 2. Of those that a mesh axis runs over, the one named last changes fastest.
Arguments:
- tokens: float32 [4, 4096, 768], P('batch', 'seq'), may hold values from -6 to 6
- lengths: int32 [4, 3], P('batch'), may hold values from 1 to 30, as said below
- cotangent: float32 [4, 4096, 768], P('batch', 'seq'), may hold values from -6 to 6
- norm_gain: float32 [768, 2], replicated, may hold values from 0.5 to 1.5
- norm_shift: float32 [768, 2], replicated, may hold values from -3 to 3
- alpha_logit: float32 [768, 16], replicated, may hold values from -1 to 1
- delta_logit: float32 [768, 16], replicated, may hold values from -10 to -3
- ema_beta: float32 [768, 16], replicated, may hold values from -0.005859375 to 0.005859375
- ema_eta: float32 [768, 16], replicated, may hold values from -1.5 to 1.5
- ema_omega: float32 [768], replicated, may hold values from -6 to 6
- w_value: bfloat16 [768, 1536], replicated, may hold values from -0.21875 to 0.21875
- b_value: float32 [1536], replicated, may hold values from -3 to 3
- w_gates: bfloat16 [768, 3200], replicated, may hold values from -0.21875 to 0.21875
- b_gates: float32 [3200], replicated, may hold values from -3 to 3
- query_key: float32 [128, 3], replicated, may hold values from -5 to 5
- position_bias: float32 [128], replicated, may hold values from -5 to 5
- w_output: bfloat16 [1536, 768], replicated, may hold values from -0.625 to 0.625
- b_output: float32 [768], replicated, may hold values from -3 to 3
- w_expand: bfloat16 [768, 1536], replicated, may hold values from -0.21875 to 0.21875
- b_expand: float32 [1536], replicated, may hold values from -3 to 3
- w_shrink: bfloat16 [1536, 768], replicated, may hold values from -0.15625 to 0.15625
- b_shrink: float32 [768], replicated, may hold values from -3 to 3
Outputs:
- out: float32 [4, 4096, 768], P('batch', 'seq')
- grad_tokens: float32 [4, 4096, 768], P('batch', 'seq')
- grad_norm_gain: float32 [768, 2], replicated
- grad_norm_shift: float32 [768, 2], replicated
- grad_alpha_logit: float32 [768, 16], replicated
- grad_delta_logit: float32 [768, 16], replicated
- grad_ema_beta: float32 [768, 16], replicated
- grad_ema_eta: float32 [768, 16], replicated
- grad_ema_omega: float32 [768], replicated
- grad_w_value: float32 [768, 1536], replicated
- grad_b_value: float32 [1536], replicated
- grad_w_gates: float32 [768, 3200], replicated
- grad_b_gates: float32 [3200], replicated
- grad_query_key: float32 [128, 3], replicated
- grad_position_bias: float32 [128], replicated
- grad_w_output: float32 [1536, 768], replicated
- grad_b_output: float32 [768], replicated
- grad_w_expand: float32 [768, 1536], replicated
- grad_b_expand: float32 [1536], replicated
- grad_w_shrink: float32 [1536, 768], replicated
- grad_b_shrink: float32 [768], replicated
The draws below stay inside these ranges and needn't reach their ends.
Inputs may be any that keep to these rules, and one draw needn't show every extreme that they name: `lengths`: each row packs three documents, measured in groups of 128 tokens, that sum to 32; the first and the last each have 1 to 4 groups.
All inputs are finite; a program needn't handle non-finite values.
Results may differ from the reference program's by a relative error of at most 0.0003.
Values sent between devices are 32-bit elements; how exact they have to be, the bound alone decides.
A program may use at most 384 MiB of HBM per device.

```python
import math
import jax
import jax.numpy as jnp
from jax import lax

D = 768
NDIM = 16
ZD = 128
HV = 1536
FF = 1536
GROUP = 128
GROUPS_DEV = 4
ROWS = 4
ROW_LEN = 4096
ROW_GROUPS = 32
GATES = 3200


def draw_lengths(key, part):
    key = jax.random.fold_in(key, 7)
    lead_key, trail_key = jax.random.split(key)
    leading = jax.random.randint(lead_key, (ROWS, 1), 1, GROUPS_DEV + 1)
    trailing = jax.random.randint(trail_key, (ROWS, 1), 1, GROUPS_DEV + 1)
    leading = leading.at[0, 0].set(1)
    trailing = trailing.at[0, 0].set(1)
    return jnp.concatenate([leading, ROW_GROUPS - leading - trailing, trailing], axis=1).astype(jnp.int32)


def level_of(rng, shape, shards, smallest, largest):
    loudness, own = 1.0, jax.random.fold_in(rng, 6)
    for position, shards_of in shards:
        heights = jnp.exp(jax.random.uniform(jax.random.fold_in(own, position), (shards_of,), jnp.float32, smallest / len(shards), largest / len(shards)))
        loudness = loudness * jnp.repeat(heights, shape[position] // shards_of).reshape([-1 if axis == position else 1 for axis in range(len(shape))])
    return loudness


def bell_draw(own_key, shape, width, limit, shards=(), kind=jnp.bfloat16):
    result = width * jax.random.normal(own_key, shape, jnp.float32)
    if shards:
        result = result * level_of(own_key, shape, shards, -0.22, 0.18)
    return jnp.clip(result, -limit, limit).astype(kind)


def setup_inputs(seed: int = 0) -> dict:
    keys = jax.random.split(jax.random.key(seed), 23)
    return {
        "tokens": bell_draw(keys[0], (ROWS, ROW_LEN, D), 1.0, 6.0, ((0, 4), (1, 8)), jnp.float32),
        "lengths": draw_lengths(jax.random.fold_in(keys[22], 71), 0),
        "cotangent": bell_draw(keys[2], (ROWS, ROW_LEN, D), 1.0, 6.0, ((0, 4), (1, 8)), jnp.float32),
        "norm_gain": jnp.clip(1.0 + 0.1 * jax.random.normal(keys[3], (D, 2), jnp.float32), 0.5, 1.5),
        "norm_shift": bell_draw(keys[4], (D, 2), 0.5, 3.0, (), jnp.float32),
        "alpha_logit": jnp.clip(jax.random.uniform(keys[5], (D, NDIM), jnp.float32, -1.0, 1.0), -1.0, 1.0),
        "delta_logit": jnp.clip(jax.random.uniform(keys[6], (D, NDIM), jnp.float32, -10.0, -3.0), -10.0, -3.0),
        "ema_beta": bell_draw(keys[7], (D, NDIM), (4.0 / ROW_LEN), 0.005859375, (), jnp.float32),
        "ema_eta": bell_draw(keys[8], (D, NDIM), 0.25, 1.5, (), jnp.float32),
        "ema_omega": bell_draw(keys[9], (D,), 1.0, 6.0, (), jnp.float32),
        "w_value": bell_draw(keys[10], (D, HV), D ** -0.5, 0.21875),
        "b_value": bell_draw(keys[11], (HV,), 0.5, 3.0, (), jnp.float32),
        "w_gates": bell_draw(keys[12], (D, GATES), D ** -0.5, 0.21875),
        "b_gates": bell_draw(keys[13], (GATES,), 0.5, 3.0, (), jnp.float32),
        "query_key": bell_draw(keys[14], (ZD, 3), 1.0, 5.0, (), jnp.float32),
        "position_bias": bell_draw(keys[15], (GROUP,), 1.0, 5.0, (), jnp.float32),
        "w_output": bell_draw(keys[16], (HV, D), (HV // 16) ** -0.5, 0.625),
        "b_output": bell_draw(keys[17], (D,), 0.5, 3.0, (), jnp.float32),
        "w_expand": bell_draw(keys[18], (D, FF), D ** -0.5, 0.21875),
        "b_expand": bell_draw(keys[19], (FF,), 0.5, 3.0, (), jnp.float32),
        "w_shrink": bell_draw(keys[20], (FF, D), FF ** -0.5, 0.15625),
        "b_shrink": bell_draw(keys[21], (D,), 0.5, 3.0, (), jnp.float32),
    }


highest = lax.Precision.HIGHEST

@jax.custom_vjp
def low(v):
    return lax.optimization_barrier(v.astype(jnp.bfloat16)).astype(jnp.float32)

@jax.custom_vjp
def low_back(v):
    return v

def low_keep(v):
    return (low(v), None)

def low_pass(kept, grad):
    return (grad,)

def back_keep(v):
    return (v, None)

def back_low(kept, grad):
    return (low(grad),)
low.defvjp(low_keep, low_pass)
low_back.defvjp(back_keep, back_low)

def matmul(left_side, right_side):
    return jnp.dot(left_side, right_side, precision=highest, preferred_element_type=jnp.float32)

def layer_norm(inputs, gain_row, shift_row):
    centre = inputs - lax.optimization_barrier(jnp.mean(inputs, axis=-1, keepdims=True))
    spread = lax.optimization_barrier(jnp.mean(centre * centre, axis=-1, keepdims=True))
    return centre * lax.rsqrt(spread + 1e-05) * gain_row + shift_row

def group_keep(lengths, group_ids):
    first_end = lengths[0]
    second_end = lengths[0] + lengths[1]
    starts = (group_ids == 0) | (group_ids == first_end) | (group_ids == second_end)
    return 1.0 - starts.astype(jnp.float32)

def ema_tables(params, group_len):
    rate_in = jax.nn.sigmoid(params['alpha_logit']).T
    damping = jax.nn.sigmoid(params['delta_logit']).T
    inflow = rate_in * params['ema_beta'].T
    log_decay = jnp.log1p(-rate_in * damping)
    offsets = jnp.arange(group_len).astype(jnp.float32)
    powers = jnp.exp(offsets[:, None, None] * log_decay[None])
    mixing = params['ema_eta'].T
    lag_kernel = lax.optimization_barrier(jnp.sum(powers * (mixing * inflow)[None], axis=1))
    row_index = jnp.arange(group_len)
    lag_grid = row_index[:, None] - row_index[None, :]
    toeplitz = jnp.where((lag_grid >= 0)[:, :, None], lag_kernel[jnp.clip(lag_grid, 0, group_len - 1)], 0.0)
    end_weight = powers[::-1] * inflow[None]
    read_weight = powers * jnp.exp(log_decay)[None] * mixing[None]
    group_decay = jnp.exp(group_len * log_decay)
    return (toeplitz, end_weight, read_weight, group_decay, log_decay)

def group_states(entries, keep_mask, group_decay, initial):

    def advance(running, element):
        fresh_entry, keep_one = element
        entering = keep_one * running
        return (group_decay * entering + fresh_entry, entering)
    final_state, entering = lax.scan(advance, initial, (entries, keep_mask))
    return (entering, final_state)

def group_attention(queries, key_rows, values, position_bias, group_len):
    row_count, shared_dim = queries.shape
    blocks = row_count // group_len
    row_index = jnp.arange(group_len)
    lag_grid = row_index[:, None] - row_index[None, :]
    bias_table = position_bias[jnp.clip(lag_grid, 0, group_len - 1)]
    scores = jnp.einsum('cid,cjd->cij', queries.reshape(blocks, group_len, shared_dim), key_rows.reshape(blocks, group_len, shared_dim), precision=highest) / math.sqrt(shared_dim) + bias_table[None]
    scores = jnp.where((lag_grid >= 0)[None], scores, -1e+30)
    weights = jax.nn.softmax(scores, axis=-1)
    attended = jnp.einsum('cij,cjv->civ', weights, values.reshape(blocks, group_len, values.shape[1]), precision=highest)
    return attended.reshape(row_count, values.shape[1])

def gated_mixer(params, tokens, keep_mask, carry_ema):
    group_len = params['position_bias'].shape[0]
    row_count, feature_dim = tokens.shape
    shared_dim = params['query_key'].shape[0]
    value_dim = params['w_value'].shape[1]
    normed = layer_norm(tokens, params['norm_gain'][:, 0], params['norm_shift'][:, 0])
    values = jax.nn.silu(matmul(normed, params['w_value']) + params['b_value'])
    tables = ema_tables(params, group_len)
    blocks = normed.reshape(row_count // group_len, group_len, feature_dim)
    within = jnp.einsum('tsd,csd->ctd', tables[0], blocks, precision=highest)
    entries = jnp.einsum('csd,snd->cnd', blocks, tables[1], precision=highest)
    states = group_states(entries, keep_mask, tables[3], jnp.zeros_like(tables[3]))
    between = jnp.einsum('cnd,tnd->ctd', states[0], tables[2], precision=highest)
    smoothed = (within + between).reshape(row_count, feature_dim) + carry_ema
    mixed = jax.nn.silu(smoothed + params['ema_omega'] * normed)
    gate_input = matmul(mixed, params['w_gates']) + params['b_gates']
    update = jax.nn.sigmoid(gate_input[:, :feature_dim])
    shared = jax.nn.silu(gate_input[:, feature_dim:feature_dim + shared_dim])
    reset_gate = jax.nn.silu(gate_input[:, feature_dim + shared_dim:feature_dim + shared_dim + value_dim])
    candidate = gate_input[:, feature_dim + shared_dim + value_dim:]
    queries = shared * params['query_key'][:, 0] + params['query_key'][:, 2]
    key_rows = shared * params['query_key'][:, 1]
    attended = group_attention(queries, key_rows, values, params['position_bias'], group_len)
    hidden = jax.nn.silu(candidate + matmul(attended * reset_gate, params['w_output']) + params['b_output'])
    return tokens + update * (hidden - tokens)

def feed_forward(params, tokens):
    normed = layer_norm(tokens, params['norm_gain'][:, 1], params['norm_shift'][:, 1])
    inner_act = jax.nn.silu(matmul(normed, params['w_expand']) + params['b_expand'])
    return tokens + matmul(inner_act, params['w_shrink']) + params['b_shrink']

def row_forward(params, tokens, lengths):
    group_len = params['position_bias'].shape[0]
    keep_mask = group_keep(lengths, jnp.arange(tokens.shape[0] // group_len))
    middle = gated_mixer(params, tokens, keep_mask, jnp.zeros_like(tokens))
    return feed_forward(params, middle)

def reference(tokens, lengths, cotangent, norm_gain, norm_shift, alpha_logit, delta_logit, ema_beta, ema_eta, ema_omega, w_value, b_value, w_gates, b_gates, query_key, position_bias, w_output, b_output, w_expand, b_expand, w_shrink, b_shrink):
    params = dict(norm_gain=norm_gain.astype(jnp.float32), norm_shift=norm_shift.astype(jnp.float32), alpha_logit=alpha_logit.astype(jnp.float32), delta_logit=delta_logit.astype(jnp.float32), ema_beta=ema_beta.astype(jnp.float32), ema_eta=ema_eta.astype(jnp.float32), ema_omega=ema_omega.astype(jnp.float32), w_value=w_value.astype(jnp.float32), b_value=b_value.astype(jnp.float32), w_gates=w_gates.astype(jnp.float32), b_gates=b_gates.astype(jnp.float32), query_key=query_key.astype(jnp.float32), position_bias=position_bias.astype(jnp.float32), w_output=w_output.astype(jnp.float32), b_output=b_output.astype(jnp.float32), w_expand=w_expand.astype(jnp.float32), b_expand=b_expand.astype(jnp.float32), w_shrink=w_shrink.astype(jnp.float32), b_shrink=b_shrink.astype(jnp.float32))
    row_step = jax.checkpoint(row_forward)

    def whole_layer(params_in, tokens_in):
        return lax.map(lambda row_pair: row_step(params_in, row_pair[0], row_pair[1]), (tokens_in, lengths))
    output, pullback = jax.vjp(whole_layer, params, tokens.astype(jnp.float32))
    grads, grad_tokens = pullback(cotangent.astype(jnp.float32))
    return (output, grad_tokens, grads['norm_gain'], grads['norm_shift'], grads['alpha_logit'], grads['delta_logit'], grads['ema_beta'], grads['ema_eta'], grads['ema_omega'], grads['w_value'], grads['b_value'], grads['w_gates'], grads['b_gates'], grads['query_key'], grads['position_bias'], grads['w_output'], grads['b_output'], grads['w_expand'], grads['b_expand'], grads['w_shrink'], grads['b_shrink'])
```

```python
import functools
import math
import typing

import jax
import jax.numpy as jnp
from jax import lax
from jax.experimental import pallas as pl
from jax.experimental.pallas import tpu as pltpu
from jax.sharding import PartitionSpec as P

f32 = jnp.float32
bf16 = jnp.bfloat16
MESH = pl.DeviceIdType.MESH

SEG = 8
LANES = 128
TILE = 256

NN = (((1,), (0,)), ((), ()))
NT = (((1,), (1,)), ((), ()))


def split(value):
    high = value.astype(bf16)
    return high, (value - high.astype(f32)).astype(bf16)


def dot(a, b, dims=NN):
    return lax.dot_general(a, b, dims, preferred_element_type=f32)


def dot3(a, b, dims=NN):
    a_high, a_low = a
    b_high, b_low = b
    return dot(a_high, b_high, dims) + (dot(a_high, b_low, dims) + dot(a_low, b_high, dims))


def sigmoid(value):
    return 1.0 / (1.0 + jnp.exp(-value))


def silu(value):
    return value * sigmoid(value)


def dsilu(value):
    s = sigmoid(value)
    return s * (1.0 + value * (1.0 - s))


def row_get(ref, part):
    return jnp.concatenate([ref[d, part, :] for d in range(ref.shape[0])], axis=-1)


def row_set(ref, part, value):
    for d in range(ref.shape[0]):
        ref[d, part, :] = value[:, d * LANES : (d + 1) * LANES]


def col_get(ref, i, size=TILE):
    n = size // LANES
    return jnp.concatenate([ref[i * n + k] for k in range(n)], axis=-1)


def col_set(ref, i, value):
    n = value.shape[1] // LANES
    for k in range(n):
        ref[i * n + k] = value[:, k * LANES : (k + 1) * LANES]


def at(i, size):
    return pl.ds(pl.multiple_of(i * size, size), size)


def off(start, i, size):
    return pl.ds(pl.multiple_of(start + i * size, LANES), size)


class Refs(typing.NamedTuple):
    x: typing.Any
    cot: typing.Any
    sk: typing.Any
    pk: typing.Any
    kf: typing.Any
    tables: typing.Any
    gains: typing.Any
    w_value: typing.Any
    w_gates: typing.Any
    w_output: typing.Any
    w_expand: typing.Any
    w_shrink: typing.Any
    b_value: typing.Any
    b_gates: typing.Any
    b_expand: typing.Any
    qk: typing.Any
    bias_row: typing.Any
    out: typing.Any
    dx: typing.Any
    dw_value: typing.Any
    dw_gates: typing.Any
    dw_output: typing.Any
    dw_expand: typing.Any
    dw_shrink: typing.Any
    s768: typing.Any
    s_value: typing.Any
    s_expand: typing.Any
    s_gates: typing.Any
    s_small: typing.Any
    wv: typing.Any
    wg: typing.Any
    wo: typing.Any
    we: typing.Any
    ws: typing.Any
    normed: typing.Any
    vpre: typing.Any
    gate: typing.Any
    att: typing.Any
    hpre: typing.Any
    mid: typing.Any
    epre: typing.Any
    mpre: typing.Any
    dnorm: typing.Any
    probs: typing.Any
    lh: typing.Any
    ll: typing.Any
    th: typing.Any
    tl: typing.Any
    stage: typing.Any
    ends: typing.Any
    starts: typing.Any
    e_recv: typing.Any
    f_recv: typing.Any
    history: typing.Any
    wsem: typing.Any
    ssem: typing.Any
    send: typing.Any
    recv: typing.Any
    send2: typing.Any
    recv2: typing.Any


def kernel(seq, *refs):
    r = Refs(*refs)
    rows, width = r.x.shape
    seg_len = rows // SEG
    me_b, me = lax.axis_index("batch"), lax.axis_index("seq")
    nstate = 16
    hv = r.vpre.shape[1]
    ff = r.epre.shape[1]
    zd = r.qk.shape[1]
    group = r.probs.shape[1]
    groups = rows // group
    reset0 = width + zd
    cand0 = reset0 + hv
    scale = 1.0 / math.sqrt(zd)

    weights = [
        pltpu.make_async_copy(a, b, r.wsem.at[i])
        for i, (a, b) in enumerate(
            [
                (r.w_value, r.wv),
                (r.w_gates, r.wg),
                (r.w_output, r.wo),
                (r.w_expand, r.we),
                (r.w_shrink, r.ws),
            ]
        )
    ]
    for copy in weights:
        copy.start()

    barrier = pltpu.get_barrier_semaphore()

    def greet(k, _):
        pl.semaphore_signal(
            barrier, inc=1, device_id=(me_b, lax.rem(me + k, seq)), device_id_type=MESH
        )
        return 0

    lax.fori_loop(1, seq, greet, 0)

    gain0, shift0, gain1, shift1, omega, b_output, b_shrink = (
        r.gains[i : i + 1, :] for i in range(7)
    )
    decay, coef, dec_seg, dec_all = (r.tables.at[i] for i in range(4))

    def zero_small(i):
        r.s768[i : i + 1, :] = jnp.zeros((1, width), f32)

    for i in range(7):
        zero_small(i)

    def add768(i, value, cols=slice(None)):
        r.s768[i : i + 1, cols] += jnp.sum(value, axis=0, keepdims=True)

    RC = 32

    def norm_stats(value):
        centre = value - jnp.mean(value, axis=-1, keepdims=True)
        inv = lax.rsqrt(jnp.mean(centre * centre, axis=-1, keepdims=True) + 1e-05)
        return centre * inv, inv

    def norm_back(grad, n, inv):
        return inv * (
            grad
            - jnp.mean(grad, axis=-1, keepdims=True)
            - n * jnp.mean(grad * n, axis=-1, keepdims=True)
        )

    @pl.loop(0, rows // RC)
    def _(i):
        part = at(i, RC)
        n, _inv = norm_stats(r.x[part, :])
        value = n * gain0 + shift0
        row_set(r.normed, part, value)
        r.lh[part, :width], r.ll[part, :width] = split(value)

    def seg_rows(t):
        return pl.ds(t, SEG, stride=seg_len)

    def rows_of(ref, count, cols):
        return [jnp.broadcast_to(ref[n : n + 1, cols], (SEG, LANES)) for n in count]

    def end_states(source, reverse, target):
        @pl.loop(0, width // LANES)
        def _(d):
            cols = at(d, LANES)
            dec = rows_of(decay, range(nstate), cols)

            def turn(t, state):
                at_t = seg_len - 1 - t if reverse else t
                value = source[d, seg_rows(at_t), :]
                return tuple(a * s + value for a, s in zip(dec, state))

            zero = jnp.zeros((SEG, LANES), f32)
            state = lax.fori_loop(0, seg_len, turn, (zero,) * nstate, unroll=8)
            for n in range(nstate):
                target[d, n * SEG : (n + 1) * SEG, :] = state[n]

    def seg_of(k):
        return pl.ds(k, nstate, stride=SEG)

    def exchange(buffer, send_sem, recv_sem):
        def copy_to(k):
            peer = lax.rem(me + k, seq)
            return pltpu.make_async_remote_copy(
                src_ref=buffer.at[me],
                dst_ref=buffer.at[me],
                send_sem=send_sem.at[k],
                recv_sem=recv_sem.at[me],
                device_id=(me_b, peer),
                device_id_type=MESH,
            )

        def copy_from(k):
            peer = lax.rem(me + k, seq)
            return pltpu.make_async_remote_copy(
                src_ref=buffer.at[me],
                dst_ref=buffer.at[peer],
                send_sem=send_sem.at[k],
                recv_sem=recv_sem.at[peer],
                device_id=(me_b, peer),
                device_id_type=MESH,
            )

        def start():
            def one(k, _):
                copy_to(k).start()
                return 0

            lax.fori_loop(1, seq, one, 0)

        def wait():
            def one(k, _):
                copy_to(k).wait_send()
                copy_from(k).wait_recv()
                return 0

            lax.fori_loop(1, seq, one, 0)

        return start, wait

    end_states(r.normed, False, r.ends)
    total = jnp.zeros((nstate, width), f32)
    for k in range(SEG):
        total = r.sk[k] * total * dec_seg[...] + row_get(r.ends, seg_of(k))
    r.e_recv[me] = total
    pl.semaphore_wait(barrier, seq - 1)
    start_e, wait_e = exchange(r.e_recv, r.send, r.recv)
    start_e()

    weights[0].wait()

    @pl.loop(0, hv // TILE)
    def _(i):
        c = at(i, TILE)
        w = r.wv[:, c]
        r.vpre[:, c] = (
            dot(r.lh[:, :width], w) + dot(r.ll[:, :width], w) + r.b_value[:, c]
        )

    wait_e()

    def carry_step(k, carried):
        new = dec_all[...] * (r.pk[k] * carried) + r.e_recv[k]
        return jnp.where(k < me, new, carried)

    state = lax.fori_loop(0, seq, carry_step, jnp.zeros((nstate, width), f32))
    for k in range(SEG):
        state = r.sk[k] * state
        row_set(r.starts, seg_of(k), state)
        if k < SEG - 1:
            state = dec_seg[...] * state + row_get(r.ends, seg_of(k))

    @pl.loop(0, width // LANES)
    def _(d):
        cols = at(d, LANES)
        dec = rows_of(decay, range(nstate), cols)
        mix = rows_of(coef, range(nstate), cols)

        def turn(t, state):
            value = r.normed[d, seg_rows(t), :]
            state = tuple(a * s + value for a, s in zip(dec, state))
            terms = [m * s for m, s in zip(mix, state)]
            while len(terms) > 1:
                terms = [a + b for a, b in zip(terms[::2], terms[1::2])]
            r.mpre[d, seg_rows(t), :] = terms[0]
            return state

        first = tuple(r.starts[d, n * SEG : (n + 1) * SEG, :] for n in range(nstate))
        lax.fori_loop(0, seg_len, turn, first, unroll=4)

    @pl.loop(0, rows // RC)
    def _(i):
        part = at(i, RC)
        value = row_get(r.mpre, part) + omega * row_get(r.normed, part)
        row_set(r.mpre, part, value)
        r.lh[part, :width], r.ll[part, :width] = split(silu(value))

    weights[1].wait()

    def gate_tile(c):
        w = r.wg[:, c]
        r.gate[:, c] = (
            dot(r.lh[:, :width], w) + dot(r.ll[:, :width], w) + r.b_gates[:, c]
        )

    @pl.loop(0, width // TILE)
    def _(i):
        gate_tile(at(i, TILE))

    gate_tile(pl.ds(width, zd))

    @pl.loop(0, (hv + width) // TILE)
    def _(i):
        gate_tile(off(reset0, i, TILE))

    lag = lax.broadcasted_iota(jnp.int32, (group, group), 0) - lax.broadcasted_iota(
        jnp.int32, (group, group), 1
    )
    row_id = lax.broadcasted_iota(jnp.int32, (group, group), 0)
    causal = lag >= 0
    table = jnp.broadcast_to(r.bias_row[...], (group, group))
    for b in range(group.bit_length() - 1):
        moved = pltpu.roll(table, 1 << b, 1)
        table = jnp.where((row_id & (1 << b)) != 0, moved, table)
    q_gain, k_gain, q_shift = (r.qk[i : i + 1, :] for i in range(3))
    r.starts[0] = table

    @pl.loop(0, groups)
    def _(g):
        part = at(g, group)
        shared = silu(r.gate[part, width:reset0])
        q = split(shared * q_gain + q_shift)
        k = split(shared * k_gain)
        scores = dot3(q, k, NT) * scale + r.starts[0]
        scores = jnp.where(causal, scores, -1e30)
        p = jnp.exp(scores - jnp.max(scores, axis=-1, keepdims=True))
        p = p / jnp.sum(p, axis=-1, keepdims=True)
        r.probs[part, :] = p
        p = split(p)

        @pl.loop(0, hv // TILE)
        def _(i):
            c = at(i, TILE)
            v = split(silu(r.vpre[part, c]))
            attended = dot3(p, v)
            r.att[part, c] = attended
            gated = attended * silu(r.gate[part, off(reset0, i, TILE)])
            r.lh[part, c], r.ll[part, c] = split(gated)

    weights[2].wait()

    @pl.loop(0, width // TILE)
    def _(i):
        c = at(i, TILE)
        w = r.wo[:, c]
        value = (
            dot(r.lh[...], w)
            + dot(r.ll[...], w)
            + (r.gate[:, off(cand0, i, TILE)] + r.gains[5:6, c])
        )
        r.hpre[:, c] = value
        x = r.x[:, c]
        r.mid[:, c] = x + sigmoid(r.gate[:, c]) * (silu(value) - x)

    @pl.loop(0, rows // RC)
    def _(i):
        part = at(i, RC)
        n, _inv = norm_stats(r.mid[part, :])
        r.lh[part, :width], r.ll[part, :width] = split(n * gain1 + shift1)

    weights[3].wait()

    @pl.loop(0, ff // TILE)
    def _(i):
        c = at(i, TILE)
        w = r.we[:, c]
        r.epre[:, c] = (
            dot(r.lh[:, :width], w) + dot(r.ll[:, :width], w) + r.b_expand[:, c]
        )

    @pl.loop(0, ff // TILE)
    def _(i):
        c = at(i, TILE)
        r.lh[:, c], r.ll[:, c] = split(silu(r.epre[:, c]))

    weights[4].wait()

    @pl.loop(0, width // TILE)
    def _(i):
        c = at(i, TILE)
        w = r.ws[:, c]
        r.out[:, c] = r.mid[:, c] + (
            dot(r.lh[...], w) + dot(r.ll[...], w) + r.gains[6:7, c]
        )

    def transposed(source, count):
        @pl.loop(0, count // LANES)
        def _(i):
            value = source(i, at(i, LANES)).T
            here = at(i, LANES)
            r.th[here, :], r.tl[here, :] = split(value)

    def weight_grad(count, grad, target, tiles, first=0):
        def copy(i, slot):
            return pltpu.make_async_copy(
                r.stage.at[slot, pl.ds(0, count), :],
                target.at[:, off(first, i, TILE)],
                r.ssem.at[slot],
            )

        @pl.loop(0, tiles)
        def _(i):
            slot = lax.rem(i, 2)

            @pl.when(i >= 2)
            def _():
                copy(i - 2, slot).wait()

            g_high, g_low = split(grad(i))
            for k in range(count // TILE):
                here = slice(k * TILE, (k + 1) * TILE)
                a_high, a_low = r.th[here, :], r.tl[here, :]
                r.stage[slot, here, :] = dot3((a_high, a_low), (g_high, g_low))
            copy(i, slot).start()

        for i in range(max(tiles - 2, 0), tiles):
            copy(i, i % 2).wait()

    transposed(lambda i, c: silu(r.epre[:, c]), ff)
    weight_grad(ff, lambda i: r.cot[:, at(i, TILE)], r.dw_shrink, width // TILE)

    @pl.loop(0, rows // RC)
    def _(i):
        part = at(i, RC)
        value = r.cot[part, :]
        add768(6, value)
        r.lh[part, :width], r.ll[part, :width] = split(value)

    @pl.loop(0, ff // TILE)
    def _(i):
        c = at(i, TILE)
        w = r.ws[c, :]
        value = (dot(r.lh[:, :width], w, NT) + dot(r.ll[:, :width], w, NT)) * dsilu(
            r.epre[:, c]
        )
        r.epre[:, c] = value
        r.s_expand[:, c] = jnp.sum(value, axis=0, keepdims=True)

    @pl.loop(0, ff // TILE)
    def _(i):
        c = at(i, TILE)
        r.lh[:, c], r.ll[:, c] = split(r.epre[:, c])

    @pl.loop(0, rows // RC)
    def _(i):
        part = at(i, RC)
        n, _inv = norm_stats(r.mid[part, :])
        row_set(r.dnorm, part, n * gain1 + shift1)

    transposed(lambda i, c: r.dnorm[i], width)
    weight_grad(width, lambda i: r.epre[:, at(i, TILE)], r.dw_expand, ff // TILE)

    @pl.loop(0, width // TILE)
    def _(i):
        c = at(i, TILE)
        w = r.we[c, :]
        r.dx[:, c] = dot(r.lh[...], w, NT) + dot(r.ll[...], w, NT)

    @pl.loop(0, rows // RC)
    def _(i):
        part = at(i, RC)
        grad = r.dx[part, :]
        n, inv = norm_stats(r.mid[part, :])
        add768(2, grad * n)
        add768(3, grad)
        dmid = r.cot[part, :] + norm_back(grad * gain1, n, inv)
        update = sigmoid(r.gate[part, :width])
        pre = r.hpre[part, :]
        x = r.x[part, :]
        dhpre = dmid * update * dsilu(pre)
        r.dx[part, :] = dmid * (1.0 - update)
        dupdate = dmid * (silu(pre) - x) * (update * (1.0 - update))
        r.gate[part, :width] = dupdate
        r.gate[part, cand0:] = dhpre
        r.lh[part, :width], r.ll[part, :width] = split(dhpre)
        r.s_gates[:, :width] = (
            jnp.where(i == 0, 0.0, r.s_gates[:, :width])
            + jnp.sum(dupdate, axis=0, keepdims=True)
        )
        add768(5, dhpre)

    transposed(lambda i, c: r.att[:, c] * silu(r.gate[:, off(reset0, i, LANES)]), hv)
    weight_grad(hv, lambda i: r.gate[:, off(cand0, i, TILE)], r.dw_output, width // TILE)

    @pl.loop(0, hv // TILE)
    def _(i):
        c = at(i, TILE)
        w = r.wo[c, :]
        gated = dot(r.lh[:, :width], w, NT) + dot(r.ll[:, :width], w, NT)
        here = off(reset0, i, TILE)
        pre = r.gate[:, here]
        dreset = gated * r.att[:, c] * dsilu(pre)
        r.att[:, c] = gated * silu(pre)
        r.gate[:, here] = dreset
        r.s_gates[:, here] = jnp.sum(dreset, axis=0, keepdims=True)

    r.s_small[...] = jnp.zeros_like(r.s_small)
    r.starts[0] = jnp.zeros((group, group), f32)

    @pl.loop(0, groups)
    def _(g):
        part = at(g, group)
        p = r.probs[part, :]
        p_t = split(p.T)

        def value_tile(i, dp):
            c = at(i, TILE)
            pre = r.vpre[part, c]
            d_att = split(r.att[part, c])
            r.vpre[part, c] = dot3(p_t, d_att) * dsilu(pre)
            return dp + dot3(d_att, split(silu(pre)), NT)

        dp = lax.fori_loop(0, hv // TILE, value_tile, jnp.zeros((group, group), f32))
        ds = p * (dp - jnp.sum(dp * p, axis=-1, keepdims=True))
        r.starts[0] += ds
        ds = ds * scale
        pre = r.gate[part, width:reset0]
        shared = silu(pre)
        dq = dot3(split(ds), split(shared * k_gain))
        dk = dot3(split(ds.T), split(shared * q_gain + q_shift))
        for n, value in enumerate((dq * shared, dk * shared, dq)):
            r.s_small[n : n + 1, :] += jnp.sum(value, axis=0, keepdims=True)
        r.gate[part, width:reset0] = (dq * q_gain + dk * k_gain) * dsilu(pre)

    diagonals = r.starts[0]
    for b in range(group.bit_length() - 1):
        moved = pltpu.roll(diagonals, group - (1 << b), 1)
        diagonals = jnp.where((row_id & (1 << b)) != 0, moved, diagonals)
    r.s_small[3:4, :] = jnp.sum(diagonals, axis=0, keepdims=True)
    r.s_gates[:, width:reset0] = jnp.sum(r.gate[:, width:reset0], axis=0, keepdims=True)
    r.s_gates[:, cand0:] = r.s768[5:6, :]

    @pl.loop(0, hv // TILE)
    def _(i):
        c = at(i, TILE)
        value = r.vpre[:, c]
        r.s_value[:, c] = jnp.sum(value, axis=0, keepdims=True)
        r.lh[:, c], r.ll[:, c] = split(value)

    @pl.loop(0, width // TILE)
    def _(i):
        c = at(i, TILE)
        w = r.wv[c, :]
        col_set(r.dnorm, i, dot(r.lh[...], w, NT) + dot(r.ll[...], w, NT))

    transposed(lambda i, c: r.normed[i], width)
    weight_grad(width, lambda i: r.vpre[:, at(i, TILE)], r.dw_value, hv // TILE)

    transposed(lambda i, c: silu(r.mpre[i]), width)
    weight_grad(width, lambda i: r.gate[:, at(i, TILE)], r.dw_gates, width // TILE)
    weight_grad(
        width,
        lambda i: r.gate[:, off(reset0, i, TILE)],
        r.dw_gates,
        (hv + width) // TILE,
        reset0,
    )
    g_high, g_low = split(r.gate[:, width:reset0])
    for k in range(width // TILE):
        here = slice(k * TILE, (k + 1) * TILE)
        r.stage[0, here, :zd] = dot3((r.th[here, :], r.tl[here, :]), (g_high, g_low))
    shared_copy = pltpu.make_async_copy(
        r.stage.at[0, pl.ds(0, width), pl.ds(0, zd)],
        r.dw_gates.at[:, pl.ds(width, zd)],
        r.ssem.at[0],
    )
    shared_copy.start()

    def gate_section(start, size, first, last):
        @pl.loop(0, size // LANES)
        def _(i):
            c = at(i, LANES)
            r.lh[:, c], r.ll[:, c] = split(r.gate[:, off(start, i, LANES)])

        @pl.loop(0, width // TILE)
        def _(i):
            c = at(i, TILE)
            w = r.wg[c, start : start + size]
            value = dot(r.lh[:, :size], w, NT) + dot(r.ll[:, :size], w, NT)
            if not first:
                value += r.att[:, c]
            if last:
                value = value * dsilu(col_get(r.mpre, i))
                col_set(r.mpre, i, value)
                add768(4, value * col_get(r.normed, i), c)
                col_set(r.dnorm, i, col_get(r.dnorm, i) + r.gains[4:5, c] * value)
            else:
                r.att[:, c] = value

    shared_copy.wait()
    gate_section(0, reset0, True, False)
    gate_section(reset0, hv, False, False)
    gate_section(cand0, width, False, True)

    end_states(r.mpre, True, r.ends)
    adj = jnp.zeros((nstate, width), f32)
    for k in reversed(range(SEG)):
        if k < SEG - 1:
            adj = dec_seg[...] * (r.sk[k + 1] * adj)
        adj = adj + row_get(r.ends, seg_of(k))
    r.f_recv[me] = adj
    start_f, wait_f = exchange(r.f_recv, r.send2, r.recv2)
    start_f()

    state = lax.fori_loop(0, seq, carry_step, jnp.zeros((nstate, width), f32))
    wait_f()

    def adj_step(j, carried):
        k = seq - 1 - j
        new = r.kf[k] * r.f_recv[k] + dec_all[...] * (r.pk[k] * carried)
        return jnp.where(k > me, new, carried)

    adj = lax.fori_loop(0, seq, adj_step, jnp.zeros((nstate, width), f32))
    for k in reversed(range(SEG)):
        fresh = row_get(r.ends, seg_of(k))
        row_set(r.ends, seg_of(k), adj)
        if k > 0:
            adj = r.sk[k] * (dec_seg[...] * adj + fresh)

    end_states(r.normed, False, r.starts)
    for k in range(SEG):
        state = r.sk[k] * state
        fresh = row_get(r.starts, seg_of(k))
        row_set(r.starts, seg_of(k), state)
        state = dec_seg[...] * state + fresh

    half = nstate // 2
    for h in range(2):
        states = range(h * half, (h + 1) * half)

        @pl.loop(0, width // LANES)
        def _(d):
            cols = at(d, LANES)
            dec = rows_of(decay, states, cols)
            mix = rows_of(coef, states, cols)

            def ahead(t, state):
                value = r.normed[d, seg_rows(t), :]
                for n in range(half):
                    r.history[t, n * SEG : (n + 1) * SEG, :] = state[n]
                return tuple(a * s + value for a, s in zip(dec, state))

            first = tuple(r.starts[d, n * SEG : (n + 1) * SEG, :] for n in states)
            lax.fori_loop(0, seg_len, ahead, first, unroll=4)

            def back(j, carried):
                t = seg_len - 1 - j
                adj, p_sum, q_sum = carried
                grad = r.mpre[d, seg_rows(t), :]
                value = r.normed[d, seg_rows(t), :]
                adj = tuple(a * s + grad for a, s in zip(dec, adj))
                p_sum = tuple(p + a * value for p, a in zip(p_sum, adj))
                q_sum = tuple(
                    q + a * r.history[t, n * SEG : (n + 1) * SEG, :]
                    for n, (q, a) in enumerate(zip(q_sum, adj))
                )
                terms = [m * a for m, a in zip(mix, adj)]
                while len(terms) > 1:
                    terms = [a + b for a, b in zip(terms[::2], terms[1::2])]
                r.dnorm[d, seg_rows(t), :] += terms[0]
                return adj, p_sum, q_sum

            zero = (jnp.zeros((SEG, LANES), f32),) * half
            last = tuple(r.ends[d, n * SEG : (n + 1) * SEG, :] for n in states)
            _adj, p_sum, q_sum = lax.fori_loop(0, seg_len, back, (last, zero, zero), unroll=4)
            for n in range(half):
                row = 8 + h * half + n
                r.s768[row : row + 1, cols] = jnp.sum(p_sum[n], axis=0, keepdims=True)
                row = row + nstate
                r.s768[row : row + 1, cols] = jnp.sum(q_sum[n], axis=0, keepdims=True)

    @pl.loop(0, rows // RC)
    def _(i):
        part = at(i, RC)
        grad = row_get(r.dnorm, part)
        n, inv = norm_stats(r.x[part, :])
        add768(0, grad * n)
        add768(1, grad)
        r.dx[part, :] += norm_back(grad * gain0, n, inv)

    zero_small(7)


def layer(x, cot, sk, pk, kf, tables, gains, weights, biases, qk, bias_row, seq):
    rows, width = x.shape
    w_value, w_gates, w_output, w_expand, w_shrink = weights
    hv, gates, ff = w_value.shape[1], w_gates.shape[1], w_expand.shape[1]
    zd, group = qk.shape[1], bias_row.shape[1]
    nstate = tables.shape[1]
    vmem = pl.BlockSpec(memory_space=pltpu.VMEM)
    smem = pl.BlockSpec(memory_space=pltpu.SMEM)
    hbm = pl.BlockSpec(memory_space=pl.ANY)

    def shape(*dims, kind=f32):
        return jax.ShapeDtypeStruct(dims, kind)

    return pl.pallas_call(
        functools.partial(kernel, seq),
        out_shape=(
            shape(rows, width),
            shape(rows, width),
            shape(width, hv),
            shape(width, gates),
            shape(hv, width),
            shape(width, ff),
            shape(ff, width),
            shape(8 + 2 * nstate, width),
            shape(1, hv),
            shape(1, ff),
            shape(1, gates),
            shape(8, zd),
        ),
        in_specs=[vmem, vmem, smem, smem, smem, vmem, vmem] + [hbm] * 5 + [vmem] * 5,
        out_specs=(vmem, vmem, hbm, hbm, hbm, hbm, hbm, vmem, vmem, vmem, vmem, vmem),
        scratch_shapes=[
            pltpu.VMEM(w_value.shape, bf16),
            pltpu.VMEM(w_gates.shape, bf16),
            pltpu.VMEM(w_output.shape, bf16),
            pltpu.VMEM(w_expand.shape, bf16),
            pltpu.VMEM(w_shrink.shape, bf16),
            pltpu.VMEM((width // LANES, rows, LANES), f32),
            pltpu.VMEM((rows, hv), f32),
            pltpu.VMEM((rows, gates), f32),
            pltpu.VMEM((rows, hv), f32),
            pltpu.VMEM((rows, width), f32),
            pltpu.VMEM((rows, width), f32),
            pltpu.VMEM((rows, ff), f32),
            pltpu.VMEM((width // LANES, rows, LANES), f32),
            pltpu.VMEM((width // LANES, rows, LANES), f32),
            pltpu.VMEM((rows, group), f32),
            pltpu.VMEM((rows, max(hv, ff)), bf16),
            pltpu.VMEM((rows, max(hv, ff)), bf16),
            pltpu.VMEM((max(hv, ff), rows), bf16),
            pltpu.VMEM((max(hv, ff), rows), bf16),
            pltpu.VMEM((2, max(hv, ff), TILE), f32),
            pltpu.VMEM((width // LANES, nstate * SEG, LANES), f32),
            pltpu.VMEM((width // LANES, nstate * SEG, LANES), f32),
            pltpu.VMEM((seq, nstate, width), f32),
            pltpu.VMEM((seq, nstate, width), f32),
            pltpu.VMEM((rows // SEG, nstate // 2 * SEG, LANES), f32),
            pltpu.SemaphoreType.DMA((5,)),
            pltpu.SemaphoreType.DMA((2,)),
            pltpu.SemaphoreType.DMA((seq,)),
            pltpu.SemaphoreType.DMA((seq,)),
            pltpu.SemaphoreType.DMA((seq,)),
            pltpu.SemaphoreType.DMA((seq,)),
        ],
        compiler_params=pltpu.CompilerParams(
            collective_id=0, has_side_effects=True, vmem_limit_bytes=63 << 20
        ),
        cost_estimate=pl.CostEstimate(
            flops=52_000_000_000, bytes_accessed=60_000_000, transcendentals=20_000_000
        ),
    )(
        x, cot, sk, pk, kf, tables, gains, *weights, *biases, qk, bias_row
    )


def shards(
    seq,
    tokens,
    lengths,
    cotangent,
    norm_gain,
    norm_shift,
    alpha_logit,
    delta_logit,
    ema_beta,
    ema_eta,
    ema_omega,
    w_value,
    b_value,
    w_gates,
    b_gates,
    query_key,
    position_bias,
    w_output,
    b_output,
    w_expand,
    b_expand,
    w_shrink,
    b_shrink,
):
    rows, width = tokens.shape[1:]
    group = position_bias.shape[0]
    blocks = rows // group
    me = lax.axis_index("seq")

    alpha = jax.nn.sigmoid(alpha_logit).T
    damping = jax.nn.sigmoid(delta_logit).T
    beta, eta = ema_beta.T, ema_eta.T
    inflow = alpha * beta
    log_decay = jnp.log1p(-alpha * damping)
    tables = jnp.stack(
        [
            jnp.exp(log_decay),
            inflow * eta,
            jnp.exp((rows // SEG) * log_decay),
            jnp.exp(rows * log_decay),
        ]
    )
    ids = jnp.arange(seq * blocks)
    first_end = lengths[0, 0]
    second_end = first_end + lengths[0, 1]
    keep = 1.0 - ((ids == 0) | (ids == first_end) | (ids == second_end)).astype(f32)
    keep = keep.reshape(seq, blocks)
    mine = lax.dynamic_index_in_dim(keep, me, 0, keepdims=False)
    sk = jnp.ones((blocks, SEG // blocks), f32).at[:, 0].set(mine).reshape(SEG)
    gains = jnp.stack(
        [
            norm_gain[:, 0],
            norm_shift[:, 0],
            norm_gain[:, 1],
            norm_shift[:, 1],
            ema_omega,
            b_output,
            b_shrink,
            jnp.zeros_like(b_shrink),
        ]
    )
    outs = layer(
        tokens[0],
        cotangent[0],
        sk,
        jnp.prod(keep, axis=1),
        keep[:, 0],
        tables,
        gains,
        (w_value, w_gates, w_output, w_expand, w_shrink),
        (b_value[None], b_gates[None], b_expand[None]),
        query_key.T,
        jnp.roll(position_bias[::-1], 1)[None],
        seq,
    )
    output, grad_tokens = outs[:2]
    summed = lax.psum(outs[2:], ("batch", "seq"))
    dw_value, dw_gates, dw_output, dw_expand, dw_shrink, s768, s_value, s_expand, s_gates, small = (
        summed
    )
    nstate = alpha.shape[0]
    p_sum, q_sum = s768[8 : 8 + nstate], s768[8 + nstate : 8 + 2 * nstate]
    d_inflow = eta * p_sum
    d_eta = inflow * p_sum
    d_decay = eta * inflow * q_sum
    d_alpha = d_inflow * beta - d_decay * damping
    return (
        output[None],
        grad_tokens[None],
        jnp.stack([s768[0], s768[2]], axis=1),
        jnp.stack([s768[1], s768[3]], axis=1),
        (d_alpha * alpha * (1.0 - alpha)).T,
        (-d_decay * alpha * damping * (1.0 - damping)).T,
        (d_inflow * alpha).T,
        d_eta.T,
        s768[4],
        dw_value,
        s_value[0],
        dw_gates,
        s_gates[0],
        small[:3].T,
        jnp.roll(small[3][::-1], 1),
        dw_output,
        s768[5],
        dw_expand,
        s_expand[0],
        dw_shrink,
        s768[6],
    )


def solution(mesh):
    token_spec = P("batch", "seq", None)
    return jax.shard_map(
        functools.partial(shards, mesh.shape["seq"]),
        mesh=mesh,
        in_specs=(token_spec, P("batch", None), token_spec) + (P(),) * 19,
        out_specs=(token_spec, token_spec) + (P(),) * 19,
        check_vma=False,
    )
```

```python
import functools
import math
import typing

import jax
import jax.numpy as jnp
from jax import lax
from jax.experimental import pallas as pl
from jax.experimental.pallas import tpu as pltpu
from jax.sharding import PartitionSpec as P

f32 = jnp.float32
bf16 = jnp.bfloat16
MESH = pl.DeviceIdType.MESH

SEG = 8
LANES = 128
TILE = 256

NN = (((1,), (0,)), ((), ()))
NT = (((1,), (1,)), ((), ()))


def split(value):
    high = value.astype(bf16)
    return high, (value - high.astype(f32)).astype(bf16)


def dot(a, b, dims=NN):
    return lax.dot_general(a, b, dims, preferred_element_type=f32)


def dot3(a, b, dims=NN):
    a_high, a_low = a
    b_high, b_low = b
    return dot(a_high, b_high, dims) + (dot(a_high, b_low, dims) + dot(a_low, b_high, dims))


def sigmoid(value):
    return 1.0 / (1.0 + jnp.exp(-value))


def silu(value):
    return value * sigmoid(value)


def dsilu(value):
    s = sigmoid(value)
    return s * (1.0 + value * (1.0 - s))


def row_get(ref, part):
    return jnp.concatenate([ref[d, part, :] for d in range(ref.shape[0])], axis=-1)


def row_set(ref, part, value):
    for d in range(ref.shape[0]):
        ref[d, part, :] = value[:, d * LANES : (d + 1) * LANES]


def col_get(ref, i, size=TILE):
    n = size // LANES
    return jnp.concatenate([ref[i * n + k] for k in range(n)], axis=-1)


def col_set(ref, i, value):
    n = value.shape[1] // LANES
    for k in range(n):
        ref[i * n + k] = value[:, k * LANES : (k + 1) * LANES]


def at(i, size):
    return pl.ds(pl.multiple_of(i * size, size), size)


def off(start, i, size):
    return pl.ds(pl.multiple_of(start + i * size, LANES), size)


def bit_of(bit):
    name, step = bit
    return lax.rem(lax.div(lax.axis_index(name), step), 2)


def partner(bit):
    name, step = bit
    where = {"batch": lax.axis_index("batch"), "seq": lax.axis_index("seq")}
    where[name] = where[name] + step * (1 - 2 * bit_of(bit))
    return (where["batch"], where["seq"])


HALVINGS = 5
BLOCK = 768
TILES = 2


def slot_count(seq):
    return 8 if seq <= 16 else 4


def bits_of(batch, seq):
    chips = [("batch", 1 << k) for k in range(batch.bit_length() - 1)]
    line = [("seq", 1 << k) for k in range(1, seq.bit_length() - 1)]
    return ("seq", 1), chips, line


def stage_orders(batch, seq):
    core, chips, line = bits_of(batch, seq)
    flipped = chips[::-1]
    return (
        [core] + chips + line,
        [core] + flipped + line,
        [core] + line + chips,
        [core] + line + flipped,
    )


def stage_rows(count):
    return [BLOCK >> (min(s, HALVINGS - 1) + 1) for s in range(count)]


class Reducer:
    def __init__(self, orders, slots, kinds, subs, tile, red, gathered, sems):
        self.slots = slots
        self.orders, self.kinds, self.subs = orders, kinds, subs
        self.tile, self.red, self.gathered = tile, red, gathered
        self.send, self.recv, self.credit, self.local, self.gsend, self.grecv = sems
        self.stages = len(orders[0])
        self.halvings = min(HALVINGS, self.stages)
        self.rows = stage_rows(self.stages)
        self.jobs = len(subs)
        self.first = [sum(subs[:j]) for j in range(self.jobs)]
        self.now = 0.0
        self.free = {}
        self.due = {}
        self.done = [-1] * self.jobs

    def order(self, j):
        return self.orders[self.kinds[j]]

    def part(self, ref, slot, j, start, size):
        if not isinstance(start, int):
            start = pl.multiple_of(start, 8)
        return ref.at[slot, pl.ds(0, self.subs[j]), pl.ds(start, size), :]

    def held(self, j, s):
        if s < 0:
            return self.tile, j % TILES, BLOCK
        return self.red[s], j % self.slots, self.rows[s]

    def keep_start(self, j, s):
        return bit_of(self.order(j)[s]) * self.rows[s] if s < self.halvings else 0

    def give_start(self, j, s):
        return (1 - bit_of(self.order(j)[s])) * self.rows[s] if s < self.halvings else 0

    def scatter_copy(self, j, s):
        ref, slot, _rows = self.held(j, s - 1)
        into, into_slot, rows = self.held(j, s)
        return pltpu.make_async_remote_copy(
            src_ref=self.part(ref, slot, j, self.give_start(j, s), rows),
            dst_ref=self.part(into, into_slot, j, 0, rows),
            send_sem=self.send.at[s, into_slot],
            recv_sem=self.recv.at[s, into_slot],
            device_id=partner(self.order(j)[s]),
            device_id_type=MESH,
        )

    def owned(self, j, s, flip=False):
        start = 0
        for t in range(s + 1):
            bit = bit_of(self.order(j)[t])
            if flip and t == s:
                bit = 1 - bit
            start = start + bit * self.rows[t]
        return self.gathered.at[
            pl.ds(self.first[j], self.subs[j]), pl.ds(pl.multiple_of(start, 8), self.rows[s]), :
        ]

    def final(self, j):
        ref, slot, rows = self.held(j, self.stages - 1)
        return self.part(ref, slot, j, 0, rows)

    def gather_copy(self, j, s, arriving=False):
        last = s == self.halvings - 1
        return pltpu.make_async_remote_copy(
            src_ref=self.final(j) if last else self.owned(j, s),
            dst_ref=self.owned(j, s, flip=arriving),
            send_sem=self.gsend.at[j, s],
            recv_sem=self.grecv.at[j, s],
            device_id=partner(self.order(j)[s]),
            device_id_type=MESH,
        )

    def local_copy(self, j):
        return pltpu.make_async_copy(
            self.final(j), self.owned(j, self.halvings - 1), self.local.at[j]
        )

    def arrival(self, j, s):
        name, step = self.order(j)[s]
        rows = self.rows[s] * self.subs[j]
        size = rows * TILE * 4e-6
        if (name, step) == ("seq", 1):
            link, cost = "core", size / 0.6
        else:
            link = name + (str(step) if name == "batch" else "")
            cost = 2 * size / 0.09 * (step // 2 if name == "seq" else 1)
        start = max(self.now, self.free.get(link, 0.0))
        self.free[link] = start + cost
        return start + cost + 2.0

    def advance(self, us):
        self.now += us

    def set_due(self, j, event, when):
        self.due[j] = (event, when)

    def run(self, j):
        event, when = self.due.pop(j)
        self.now = max(self.now, when)
        n = self.stages
        if event < n:
            s = event
            copy = self.scatter_copy(j, s)
            copy.wait_send()
            copy.wait_recv()
            self.add(j, s)
            if s > 0:
                self.give_credit(j, s - 1)
            if s < n - 1:
                self.start_scatter(j, s + 1)
            else:
                self.local_copy(j).start()
                self.gather_copy(j, self.halvings - 1).start()
                self.set_due(j, event + 1, self.arrival(j, self.halvings - 1))
        else:
            s = self.halvings - 1 - (event - n)
            self.gather_copy(j, s, True).wait_recv()
            if s == self.halvings - 1:
                self.gather_copy(j, s).wait_send()
                self.local_copy(j).wait()
                self.give_credit(j, n - 1)
            if s > 0:
                self.gather_copy(j, s - 1).start()
                self.set_due(j, event + 1, self.arrival(j, s - 1))
        self.done[j] = event
        self.now += 0.5

    def add(self, j, s):
        ref, slot, _rows = self.held(j, s - 1)
        into, into_slot, rows = self.held(j, s)
        start = self.keep_start(j, s)
        step = min(48, rows)

        @pl.loop(0, rows // step)
        def _(i):
            for b in range(self.subs[j]):
                here = pl.ds(pl.multiple_of(start + i * step, 8), step)
                there = pl.ds(pl.multiple_of(i * step, 8), step)
                into[into_slot, b, there, :] += ref[slot, b, here, :]

    def give_credit(self, j, s):
        if j + self.slots < self.jobs:
            pl.semaphore_signal(
                self.credit.at[s, j % self.slots],
                inc=1,
                device_id=partner(self.order(j + self.slots)[s]),
                device_id_type=MESH,
            )

    def start_scatter(self, j, s):
        if j >= self.slots:
            self.reach(j - self.slots, s + 1)
            pl.semaphore_wait(self.credit.at[s, j % self.slots], 1)
        self.scatter_copy(j, s).start()
        self.set_due(j, s, self.arrival(j, s))

    def reach(self, j, event):
        while self.done[j] < event:
            self.run(j)

    def acquire(self, j):
        if j >= TILES:
            self.reach(j - TILES, 0)
        return j % TILES

    def produced(self, j):
        self.start_scatter(j, 0)

    def tick(self, us=0.0):
        self.advance(us)
        while self.due:
            j = min(self.due, key=lambda k: self.due[k][1])
            if self.due[j][1] > self.now:
                break
            self.run(j)

    def drain(self):
        while self.due:
            self.run(min(self.due, key=lambda k: self.due[k][1]))
        for j in range(self.jobs):
            for s in range(self.halvings - 1):
                self.gather_copy(j, s).wait_send()


class Refs(typing.NamedTuple):
    x: typing.Any
    cot: typing.Any
    sk: typing.Any
    pk: typing.Any
    kf: typing.Any
    tables: typing.Any
    gains: typing.Any
    w_value: typing.Any
    w_gates: typing.Any
    w_output: typing.Any
    w_expand: typing.Any
    w_shrink: typing.Any
    b_value: typing.Any
    b_gates: typing.Any
    b_expand: typing.Any
    qk: typing.Any
    bias_row: typing.Any
    out: typing.Any
    dx: typing.Any
    gathered: typing.Any
    wa: typing.Any
    wb: typing.Any
    wg: typing.Any
    normed: typing.Any
    vpre: typing.Any
    gate: typing.Any
    att: typing.Any
    hpre: typing.Any
    mid: typing.Any
    epre: typing.Any
    mpre: typing.Any
    dnorm: typing.Any
    probs: typing.Any
    lh: typing.Any
    ll: typing.Any
    th: typing.Any
    tl: typing.Any
    s768: typing.Any
    s_value: typing.Any
    s_expand: typing.Any
    s_gates: typing.Any
    s_small: typing.Any
    ends: typing.Any
    starts: typing.Any
    e_recv: typing.Any
    f_recv: typing.Any
    wsem: typing.Any
    send: typing.Any
    recv: typing.Any
    send2: typing.Any
    recv2: typing.Any
    tile: typing.Any
    sems: typing.Any
    red: typing.Any


def kernel(batch, seq, plan, *refs):
    n = len(Refs._fields) - 2
    r = Refs(*refs[:n], refs[n : n + 6], refs[n + 6 :])
    rows, width = r.x.shape
    seg_len = rows // SEG
    me_b, me = lax.axis_index("batch"), lax.axis_index("seq")
    nstate = 16
    hv = r.vpre.shape[1]
    ff = r.epre.shape[1]
    zd = r.qk.shape[1]
    group = r.probs.shape[1]
    groups = rows // group
    reset0 = width + zd
    cand0 = reset0 + hv
    scale = 1.0 / math.sqrt(zd)

    sources = (r.w_value, r.w_gates, r.w_output, r.w_expand, r.w_shrink, r.w_output, r.w_value)
    places = (r.wa, r.wg, r.wb, r.wa, r.wb, r.wb, r.wa)
    weights = [
        pltpu.make_async_copy(a, b, r.wsem.at[i]) for i, (a, b) in enumerate(zip(sources, places))
    ]
    for copy in weights[:3]:
        copy.start()

    kinds, subs = plan
    comm = Reducer(
        stage_orders(batch, seq), slot_count(seq), kinds, subs, r.tile, r.red, r.gathered, r.sems
    )
    _core, chips, _line = bits_of(batch, seq)

    barrier = pltpu.get_barrier_semaphore()

    def greet(k, _):
        pl.semaphore_signal(
            barrier, inc=1, device_id=(me_b, lax.rem(me + k, seq)), device_id_type=MESH
        )
        return 0

    lax.fori_loop(1, seq, greet, 0)
    for bit in chips:
        pl.semaphore_signal(barrier, inc=1, device_id=partner(bit), device_id_type=MESH)

    gain0, shift0, gain1, shift1, omega, b_output, b_shrink = (
        r.gains[i : i + 1, :] for i in range(7)
    )
    decay, coef, dec_seg, dec_all = (r.tables.at[i] for i in range(4))

    def zero_small(i):
        r.s768[i : i + 1, :] = jnp.zeros((1, width), f32)

    for i in range(8):
        zero_small(i)

    def add768(i, value, cols=slice(None)):
        r.s768[i : i + 1, cols] += jnp.sum(value, axis=0, keepdims=True)

    RC = 32

    def norm_stats(value):
        centre = value - jnp.mean(value, axis=-1, keepdims=True)
        inv = lax.rsqrt(jnp.mean(centre * centre, axis=-1, keepdims=True) + 1e-05)
        return centre * inv, inv

    def norm_back(grad, n, inv):
        return inv * (
            grad
            - jnp.mean(grad, axis=-1, keepdims=True)
            - n * jnp.mean(grad * n, axis=-1, keepdims=True)
        )

    @pl.loop(0, rows // RC)
    def _(i):
        part = at(i, RC)
        n, _inv = norm_stats(r.x[part, :])
        value = n * gain0 + shift0
        row_set(r.normed, part, value)
        r.lh[part, :width], r.ll[part, :width] = split(value)

    def seg_rows(t):
        return pl.ds(t, SEG, stride=seg_len)

    def rows_of(ref, count, cols):
        return [jnp.broadcast_to(ref[n : n + 1, cols], (SEG, LANES)) for n in count]

    def end_states(source, reverse, target):
        @pl.loop(0, width // LANES)
        def _(d):
            cols = at(d, LANES)
            dec = rows_of(decay, range(nstate), cols)

            def turn(t, state):
                at_t = seg_len - 1 - t if reverse else t
                value = source[d, seg_rows(at_t), :]
                return tuple(a * s + value for a, s in zip(dec, state))

            zero = jnp.zeros((SEG, LANES), f32)
            state = lax.fori_loop(0, seg_len, turn, (zero,) * nstate, unroll=8)
            for n in range(nstate):
                target[d, n * SEG : (n + 1) * SEG, :] = state[n]

    def seg_of(k):
        return pl.ds(k, nstate, stride=SEG)

    def exchange(buffer, send_sem, recv_sem):
        def copy_to(k):
            peer = lax.rem(me + k, seq)
            return pltpu.make_async_remote_copy(
                src_ref=buffer.at[me],
                dst_ref=buffer.at[me],
                send_sem=send_sem.at[k],
                recv_sem=recv_sem.at[me],
                device_id=(me_b, peer),
                device_id_type=MESH,
            )

        def copy_from(k):
            peer = lax.rem(me + k, seq)
            return pltpu.make_async_remote_copy(
                src_ref=buffer.at[me],
                dst_ref=buffer.at[peer],
                send_sem=send_sem.at[k],
                recv_sem=recv_sem.at[peer],
                device_id=(me_b, peer),
                device_id_type=MESH,
            )

        def start():
            def one(k, _):
                copy_to(k).start()
                return 0

            lax.fori_loop(1, seq, one, 0)

        def wait():
            def one(k, _):
                copy_to(k).wait_send()
                copy_from(k).wait_recv()
                return 0

            lax.fori_loop(1, seq, one, 0)

        return start, wait

    end_states(r.normed, False, r.ends)
    total = jnp.zeros((nstate, width), f32)
    for k in range(SEG):
        total = r.sk[k] * total * dec_seg[...] + row_get(r.ends, seg_of(k))
    r.e_recv[me] = total
    pl.semaphore_wait(barrier, seq - 1 + len(chips))
    start_e, wait_e = exchange(r.e_recv, r.send, r.recv)
    start_e()

    weights[0].wait()

    @pl.loop(0, hv // TILE)
    def _(i):
        c = at(i, TILE)
        w = r.wa[:, c]
        r.vpre[:, c] = (
            dot(r.lh[:, :width], w) + dot(r.ll[:, :width], w) + r.b_value[:, c]
        )

    weights[3].start()

    wait_e()

    def carry_step(k, carried):
        new = dec_all[...] * (r.pk[k] * carried) + r.e_recv[k]
        return jnp.where(k < me, new, carried)

    state = lax.fori_loop(0, seq, carry_step, jnp.zeros((nstate, width), f32))
    for k in range(SEG):
        state = r.sk[k] * state
        row_set(r.starts, seg_of(k), state)
        if k < SEG - 1:
            state = dec_seg[...] * state + row_get(r.ends, seg_of(k))

    @pl.loop(0, width // LANES)
    def _(d):
        cols = at(d, LANES)
        dec = rows_of(decay, range(nstate), cols)
        mix = rows_of(coef, range(nstate), cols)

        def turn(t, state):
            value = r.normed[d, seg_rows(t), :]
            state = tuple(a * s + value for a, s in zip(dec, state))
            terms = [m * s for m, s in zip(mix, state)]
            while len(terms) > 1:
                terms = [a + b for a, b in zip(terms[::2], terms[1::2])]
            r.mpre[d, seg_rows(t), :] = terms[0]
            return state

        first = tuple(r.starts[d, n * SEG : (n + 1) * SEG, :] for n in range(nstate))
        lax.fori_loop(0, seg_len, turn, first, unroll=4)

    @pl.loop(0, rows // RC)
    def _(i):
        part = at(i, RC)
        value = row_get(r.mpre, part) + omega * row_get(r.normed, part)
        row_set(r.mpre, part, value)
        r.lh[part, :width], r.ll[part, :width] = split(silu(value))

    weights[1].wait()

    def gate_tile(c):
        w = r.wg[:, c]
        r.gate[:, c] = (
            dot(r.lh[:, :width], w) + dot(r.ll[:, :width], w) + r.b_gates[:, c]
        )

    @pl.loop(0, width // TILE)
    def _(i):
        gate_tile(at(i, TILE))

    gate_tile(pl.ds(width, zd))

    @pl.loop(0, (hv + width) // TILE)
    def _(i):
        gate_tile(off(reset0, i, TILE))

    lag = lax.broadcasted_iota(jnp.int32, (group, group), 0) - lax.broadcasted_iota(
        jnp.int32, (group, group), 1
    )
    row_id = lax.broadcasted_iota(jnp.int32, (group, group), 0)
    causal = lag >= 0
    table = jnp.broadcast_to(r.bias_row[...], (group, group))
    for b in range(group.bit_length() - 1):
        moved = pltpu.roll(table, 1 << b, 1)
        table = jnp.where((row_id & (1 << b)) != 0, moved, table)
    q_gain, k_gain, q_shift = (r.qk[i : i + 1, :] for i in range(3))
    r.starts[0] = table

    @pl.loop(0, groups)
    def _(g):
        part = at(g, group)
        shared = silu(r.gate[part, width:reset0])
        q = split(shared * q_gain + q_shift)
        k = split(shared * k_gain)
        scores = dot3(q, k, NT) * scale + r.starts[0]
        scores = jnp.where(causal, scores, -1e30)
        p = jnp.exp(scores - jnp.max(scores, axis=-1, keepdims=True))
        p = p / jnp.sum(p, axis=-1, keepdims=True)
        r.probs[part, :] = p
        p = split(p)

        @pl.loop(0, hv // TILE)
        def _(i):
            c = at(i, TILE)
            v = split(silu(r.vpre[part, c]))
            attended = dot3(p, v)
            r.att[part, c] = attended
            gated = attended * silu(r.gate[part, off(reset0, i, TILE)])
            r.lh[part, c], r.ll[part, c] = split(gated)

    weights[2].wait()

    @pl.loop(0, width // TILE)
    def _(i):
        c = at(i, TILE)
        w = r.wb[:, c]
        value = (
            dot(r.lh[...], w)
            + dot(r.ll[...], w)
            + (r.gate[:, off(cand0, i, TILE)] + r.gains[5:6, c])
        )
        r.hpre[:, c] = value
        x = r.x[:, c]
        r.mid[:, c] = x + sigmoid(r.gate[:, c]) * (silu(value) - x)

    weights[4].start()

    @pl.loop(0, rows // RC)
    def _(i):
        part = at(i, RC)
        n, _inv = norm_stats(r.mid[part, :])
        r.lh[part, :width], r.ll[part, :width] = split(n * gain1 + shift1)

    weights[3].wait()

    @pl.loop(0, ff // TILE)
    def _(i):
        c = at(i, TILE)
        w = r.wa[:, c]
        r.epre[:, c] = (
            dot(r.lh[:, :width], w) + dot(r.ll[:, :width], w) + r.b_expand[:, c]
        )

    @pl.loop(0, ff // TILE)
    def _(i):
        c = at(i, TILE)
        r.lh[:, c], r.ll[:, c] = split(silu(r.epre[:, c]))

    weights[4].wait()

    @pl.loop(0, width // TILE)
    def _(i):
        c = at(i, TILE)
        w = r.wb[:, c]
        r.out[:, c] = r.mid[:, c] + (
            dot(r.lh[...], w) + dot(r.ll[...], w) + r.gains[6:7, c]
        )

    comm.advance(56.0)

    def transposed(source, count, first=0):
        @pl.loop(0, count // LANES)
        def _(i):
            here = off(first, i, LANES)
            r.th[here, :], r.tl[here, :] = split(source(i, at(i, LANES)).T)

    def products(j, pairs):
        slot = comm.acquire(j)
        for b, (first, grad) in enumerate(pairs):
            g = split(grad)
            cols = grad.shape[1]

            @pl.loop(0, BLOCK // TILE)
            def _(k):
                a = off(first, k, TILE)
                value = dot3((r.th[a, :], r.tl[a, :]), g)
                if cols == TILE:
                    r.tile[slot, b, at(k, TILE), :] = value
                else:
                    r.tile[slot, b, at(k, TILE), :cols] = value

        comm.advance(2.5 * len(pairs))
        return slot

    def tall(j, grad):
        products(j, [(0, grad), (BLOCK, grad)])
        comm.produced(j)
        comm.tick()

    def wide(j, first, left, right):
        products(j, [(first, left), (first, right)])
        comm.produced(j)
        comm.tick()

    def cols_of(ref, i, start=0):
        return ref[:, start + i * TILE : start + (i + 1) * TILE]

    transposed(lambda i, c: silu(r.epre[:, c]), ff)
    comm.advance(4.0)
    for i in range(width // TILE):
        tall(i, cols_of(r.cot, i))

    @pl.loop(0, rows // RC)
    def _(i):
        part = at(i, RC)
        value = r.cot[part, :]
        add768(6, value)
        r.lh[part, :width], r.ll[part, :width] = split(value)

    @pl.loop(0, ff // TILE)
    def _(i):
        c = at(i, TILE)
        w = r.wb[c, :]
        value = (dot(r.lh[:, :width], w, NT) + dot(r.ll[:, :width], w, NT)) * dsilu(
            r.epre[:, c]
        )
        r.epre[:, c] = value
        r.s_expand[:, c] = jnp.sum(value, axis=0, keepdims=True)

    @pl.loop(0, ff // TILE)
    def _(i):
        c = at(i, TILE)
        r.lh[:, c], r.ll[:, c] = split(r.epre[:, c])

    weights[5].start()
    comm.tick(7.0)

    @pl.loop(0, rows // RC)
    def _(i):
        part = at(i, RC)
        n, _inv = norm_stats(r.mid[part, :])
        row_set(r.dnorm, part, n * gain1 + shift1)

    transposed(lambda i, c: r.dnorm[i], width)
    comm.advance(3.0)
    for i in range(ff // (2 * TILE)):
        wide(3 + i, 0, cols_of(r.epre, 2 * i), cols_of(r.epre, 2 * i + 1))

    @pl.loop(0, width // TILE)
    def _(i):
        c = at(i, TILE)
        w = r.wa[c, :]
        r.dx[:, c] = dot(r.lh[...], w, NT) + dot(r.ll[...], w, NT)

    weights[6].start()
    comm.tick(4.0)

    @pl.loop(0, rows // RC)
    def _(i):
        part = at(i, RC)
        grad = r.dx[part, :]
        n, inv = norm_stats(r.mid[part, :])
        add768(2, grad * n)
        add768(3, grad)
        dmid = r.cot[part, :] + norm_back(grad * gain1, n, inv)
        update = sigmoid(r.gate[part, :width])
        pre = r.hpre[part, :]
        x = r.x[part, :]
        dhpre = dmid * update * dsilu(pre)
        r.dx[part, :] = dmid * (1.0 - update)
        dupdate = dmid * (silu(pre) - x) * (update * (1.0 - update))
        r.gate[part, :width] = dupdate
        r.gate[part, cand0:] = dhpre
        r.lh[part, :width], r.ll[part, :width] = split(dhpre)
        r.s_gates[:, :width] = (
            jnp.where(i == 0, 0.0, r.s_gates[:, :width])
            + jnp.sum(dupdate, axis=0, keepdims=True)
        )
        add768(5, dhpre)

    transposed(lambda i, c: r.att[:, c] * silu(r.gate[:, off(reset0, i, LANES)]), hv)
    weights[5].wait()
    comm.tick(9.0)
    for i in range(width // TILE):
        tall(6 + i, cols_of(r.gate, i, cand0))

    @pl.loop(0, hv // TILE)
    def _(i):
        c = at(i, TILE)
        w = r.wb[c, :]
        gated = dot(r.lh[:, :width], w, NT) + dot(r.ll[:, :width], w, NT)
        here = off(reset0, i, TILE)
        pre = r.gate[:, here]
        dreset = gated * r.att[:, c] * dsilu(pre)
        r.att[:, c] = gated * silu(pre)
        r.gate[:, here] = dreset
        r.s_gates[:, here] = jnp.sum(dreset, axis=0, keepdims=True)

    comm.tick(6.0)

    r.s_small[...] = jnp.zeros_like(r.s_small)
    r.starts[0] = jnp.zeros((group, group), f32)

    @pl.loop(0, groups)
    def _(g):
        part = at(g, group)
        p = r.probs[part, :]
        p_t = split(p.T)

        def value_tile(i, dp):
            c = at(i, TILE)
            pre = r.vpre[part, c]
            d_att = split(r.att[part, c])
            r.vpre[part, c] = dot3(p_t, d_att) * dsilu(pre)
            return dp + dot3(d_att, split(silu(pre)), NT)

        dp = lax.fori_loop(0, hv // TILE, value_tile, jnp.zeros((group, group), f32))
        ds = p * (dp - jnp.sum(dp * p, axis=-1, keepdims=True))
        r.starts[0] += ds
        ds = ds * scale
        pre = r.gate[part, width:reset0]
        shared = silu(pre)
        dq = dot3(split(ds), split(shared * k_gain))
        dk = dot3(split(ds.T), split(shared * q_gain + q_shift))
        for n, value in enumerate((dq * shared, dk * shared, dq)):
            r.s_small[n : n + 1, :] += jnp.sum(value, axis=0, keepdims=True)
        r.gate[part, width:reset0] = (dq * q_gain + dk * k_gain) * dsilu(pre)

    diagonals = r.starts[0]
    for b in range(group.bit_length() - 1):
        moved = pltpu.roll(diagonals, group - (1 << b), 1)
        diagonals = jnp.where((row_id & (1 << b)) != 0, moved, diagonals)
    r.s_small[3:4, :] = jnp.sum(diagonals, axis=0, keepdims=True)
    r.s_gates[:, width:reset0] = jnp.sum(r.gate[:, width:reset0], axis=0, keepdims=True)
    r.s_gates[:, cand0:] = r.s768[5:6, :]

    comm.tick(12.0)
    weights[6].wait()

    @pl.loop(0, hv // TILE)
    def _(i):
        c = at(i, TILE)
        value = r.vpre[:, c]
        r.s_value[:, c] = jnp.sum(value, axis=0, keepdims=True)
        r.lh[:, c], r.ll[:, c] = split(value)

    @pl.loop(0, width // TILE)
    def _(i):
        c = at(i, TILE)
        w = r.wa[c, :]
        col_set(r.dnorm, i, dot(r.lh[...], w, NT) + dot(r.ll[...], w, NT))

    transposed(lambda i, c: r.normed[i], width, width)
    transposed(lambda i, c: silu(r.mpre[i]), width)
    comm.tick(10.0)

    def gate_section(start, size, first, last):
        @pl.loop(0, size // LANES)
        def _(i):
            c = at(i, LANES)
            r.lh[:, c], r.ll[:, c] = split(r.gate[:, off(start, i, LANES)])

        @pl.loop(0, width // TILE)
        def _(i):
            c = at(i, TILE)
            w = r.wg[c, start : start + size]
            value = dot(r.lh[:, :size], w, NT) + dot(r.ll[:, :size], w, NT)
            if not first:
                value += r.att[:, c]
            if last:
                value = value * dsilu(col_get(r.mpre, i))
                col_set(r.mpre, i, value)
                add768(4, value * col_get(r.normed, i), c)
                col_set(r.dnorm, i, col_get(r.dnorm, i) + r.gains[4:5, c] * value)
            else:
                r.att[:, c] = value

    gate_section(0, reset0, True, False)
    gate_section(reset0, hv, False, False)
    gate_section(cand0, width, False, True)

    comm.tick(10.0)

    end_states(r.mpre, True, r.ends)
    adj = jnp.zeros((nstate, width), f32)
    for k in reversed(range(SEG)):
        if k < SEG - 1:
            adj = dec_seg[...] * (r.sk[k + 1] * adj)
        adj = adj + row_get(r.ends, seg_of(k))
    r.f_recv[me] = adj
    start_f, wait_f = exchange(r.f_recv, r.send2, r.recv2)
    start_f()

    state = lax.fori_loop(0, seq, carry_step, jnp.zeros((nstate, width), f32))
    wait_f()

    def adj_step(j, carried):
        k = seq - 1 - j
        new = r.kf[k] * r.f_recv[k] + dec_all[...] * (r.pk[k] * carried)
        return jnp.where(k > me, new, carried)

    adj = lax.fori_loop(0, seq, adj_step, jnp.zeros((nstate, width), f32))
    for k in reversed(range(SEG)):
        fresh = row_get(r.ends, seg_of(k))
        row_set(r.ends, seg_of(k), adj)
        if k > 0:
            adj = r.sk[k] * (dec_seg[...] * adj + fresh)

    end_states(r.normed, False, r.starts)
    for k in range(SEG):
        state = r.sk[k] * state
        fresh = row_get(r.starts, seg_of(k))
        row_set(r.starts, seg_of(k), state)
        state = dec_seg[...] * state + fresh

    comm.tick(6.0)
    half = nstate // 2
    for h in range(2):
        states = range(h * half, (h + 1) * half)

        @pl.loop(0, width // LANES)
        def _(d):
            cols = at(d, LANES)
            dec = rows_of(decay, states, cols)
            mix = rows_of(coef, states, cols)

            def ahead(t, state):
                value = r.normed[d, seg_rows(t), :]
                for n in range(half):
                    r.epre[at(t, SEG), n * LANES : (n + 1) * LANES] = state[n]
                return tuple(a * s + value for a, s in zip(dec, state))

            first = tuple(r.starts[d, n * SEG : (n + 1) * SEG, :] for n in states)
            lax.fori_loop(0, seg_len, ahead, first, unroll=4)

            def back(j, carried):
                t = seg_len - 1 - j
                adj, p_sum, q_sum = carried
                grad = r.mpre[d, seg_rows(t), :]
                value = r.normed[d, seg_rows(t), :]
                adj = tuple(a * s + grad for a, s in zip(dec, adj))
                p_sum = tuple(p + a * value for p, a in zip(p_sum, adj))
                q_sum = tuple(
                    q + a * r.epre[at(t, SEG), n * LANES : (n + 1) * LANES]
                    for n, (q, a) in enumerate(zip(q_sum, adj))
                )
                terms = [m * a for m, a in zip(mix, adj)]
                while len(terms) > 1:
                    terms = [a + b for a, b in zip(terms[::2], terms[1::2])]
                r.dnorm[d, seg_rows(t), :] += terms[0]
                return adj, p_sum, q_sum

            zero = (jnp.zeros((SEG, LANES), f32),) * half
            last = tuple(r.ends[d, n * SEG : (n + 1) * SEG, :] for n in states)
            _adj, p_sum, q_sum = lax.fori_loop(0, seg_len, back, (last, zero, zero), unroll=4)
            for n in range(half):
                row = 8 + h * half + n
                r.s768[row : row + 1, cols] = jnp.sum(p_sum[n], axis=0, keepdims=True)
                row = row + nstate
                r.s768[row : row + 1, cols] = jnp.sum(q_sum[n], axis=0, keepdims=True)

        comm.tick(9.0)

    @pl.loop(0, rows // RC)
    def _(i):
        part = at(i, RC)
        grad = row_get(r.dnorm, part)
        n, inv = norm_stats(r.x[part, :])
        add768(0, grad * n)
        add768(1, grad)
        r.dx[part, :] += norm_back(grad * gain0, n, inv)

    comm.tick(3.0)

    for i in range(hv // (2 * TILE)):
        wide(9 + i, width, cols_of(r.vpre, 2 * i), cols_of(r.vpre, 2 * i + 1))
    starts = [i * TILE for i in range(width // TILE)]
    starts += [reset0 + i * TILE for i in range((hv + width) // TILE)]
    for i in range(len(starts) // 2):
        left, right = starts[2 * i : 2 * i + 2]
        wide(12 + i, 0, cols_of(r.gate, 0, left), cols_of(r.gate, 0, right))

    slot = products(comm.jobs - 1, [(0, r.gate[:, width:reset0])])
    r.tile[slot, 0, :, zd:] = jnp.zeros((BLOCK, TILE - zd), f32)
    place = 0

    def put(value):
        nonlocal place
        count = value.shape[0]
        r.tile[slot, 0, place : place + count, zd:] = value
        place += count

    for d in range(width // LANES):
        put(r.s768[:, d * LANES : (d + 1) * LANES])
    put(r.s_small[...])
    for ref in (r.s_value, r.s_expand, r.s_gates):
        for d in range(ref.shape[1] // LANES):
            put(ref[:, d * LANES : (d + 1) * LANES])
    comm.produced(comm.jobs - 1)
    comm.drain()


def layer(x, cot, sk, pk, kf, tables, gains, weights, biases, qk, bias_row, batch, seq):
    rows, width = x.shape
    w_value, w_gates, w_output, w_expand, w_shrink = weights
    hv, gates, ff = w_value.shape[1], w_gates.shape[1], w_expand.shape[1]
    zd, group = qk.shape[1], bias_row.shape[1]
    nstate = tables.shape[1]
    vmem = pl.BlockSpec(memory_space=pltpu.VMEM)
    smem = pl.BlockSpec(memory_space=pltpu.SMEM)
    hbm = pl.BlockSpec(memory_space=pl.ANY)
    subs = [2] * 18 + [1]
    kinds = [(0, 1, 0, 1, 2, 0, 1, 0, 1, 3)[j % 10] for j in range(len(subs))]
    stages, slots = len(stage_orders(batch, seq)[0]), slot_count(seq)

    def shape(*dims, kind=f32):
        return jax.ShapeDtypeStruct(dims, kind)

    return pl.pallas_call(
        functools.partial(kernel, batch, seq, (kinds, subs)),
        out_shape=(shape(rows, width), shape(rows, width), shape(sum(subs), BLOCK, TILE)),
        in_specs=[vmem, vmem, smem, smem, smem, vmem, vmem] + [hbm] * 5 + [vmem] * 5,
        out_specs=(vmem, vmem, hbm),
        scratch_shapes=[
            pltpu.VMEM(w_value.shape, bf16),
            pltpu.VMEM(w_output.shape, bf16),
            pltpu.VMEM(w_gates.shape, bf16),
            pltpu.VMEM((width // LANES, rows, LANES), f32),
            pltpu.VMEM((rows, hv), f32),
            pltpu.VMEM((rows, gates), f32),
            pltpu.VMEM((rows, hv), f32),
            pltpu.VMEM((rows, width), f32),
            pltpu.VMEM((rows, width), f32),
            pltpu.VMEM((rows, ff), f32),
            pltpu.VMEM((width // LANES, rows, LANES), f32),
            pltpu.VMEM((width // LANES, rows, LANES), f32),
            pltpu.VMEM((rows, group), f32),
            pltpu.VMEM((rows, max(hv, ff)), bf16),
            pltpu.VMEM((rows, max(hv, ff)), bf16),
            pltpu.VMEM((max(hv, ff), rows), bf16),
            pltpu.VMEM((max(hv, ff), rows), bf16),
            pltpu.VMEM((8 + 2 * nstate, width), f32),
            pltpu.VMEM((1, hv), f32),
            pltpu.VMEM((1, ff), f32),
            pltpu.VMEM((1, gates), f32),
            pltpu.VMEM((8, zd), f32),
            pltpu.VMEM((width // LANES, nstate * SEG, LANES), f32),
            pltpu.VMEM((width // LANES, nstate * SEG, LANES), f32),
            pltpu.VMEM((seq, nstate, width), f32),
            pltpu.VMEM((seq, nstate, width), f32),
            pltpu.SemaphoreType.DMA((7,)),
            pltpu.SemaphoreType.DMA((seq,)),
            pltpu.SemaphoreType.DMA((seq,)),
            pltpu.SemaphoreType.DMA((seq,)),
            pltpu.SemaphoreType.DMA((seq,)),
            pltpu.VMEM((TILES, 2, BLOCK, TILE), f32),
            pltpu.SemaphoreType.DMA((stages, slots)),
            pltpu.SemaphoreType.DMA((stages, slots)),
            pltpu.SemaphoreType.REGULAR((stages, slots)),
            pltpu.SemaphoreType.DMA((len(subs),)),
            pltpu.SemaphoreType.DMA((len(subs), HALVINGS)),
            pltpu.SemaphoreType.DMA((len(subs), HALVINGS)),
        ]
        + [pltpu.VMEM((slots, 2, count, TILE), f32) for count in stage_rows(stages)],
        compiler_params=pltpu.CompilerParams(
            collective_id=0, has_side_effects=True, vmem_limit_bytes=63 << 20
        ),
        cost_estimate=pl.CostEstimate(
            flops=52_000_000_000, bytes_accessed=60_000_000, transcendentals=20_000_000
        ),
    )(
        x, cot, sk, pk, kf, tables, gains, *weights, *biases, qk, bias_row
    )


def shards(
    batch,
    seq,
    tokens,
    lengths,
    cotangent,
    norm_gain,
    norm_shift,
    alpha_logit,
    delta_logit,
    ema_beta,
    ema_eta,
    ema_omega,
    w_value,
    b_value,
    w_gates,
    b_gates,
    query_key,
    position_bias,
    w_output,
    b_output,
    w_expand,
    b_expand,
    w_shrink,
    b_shrink,
):
    rows, width = tokens.shape[1:]
    group = position_bias.shape[0]
    blocks = rows // group
    me = lax.axis_index("seq")

    alpha = jax.nn.sigmoid(alpha_logit).T
    damping = jax.nn.sigmoid(delta_logit).T
    beta, eta = ema_beta.T, ema_eta.T
    inflow = alpha * beta
    log_decay = jnp.log1p(-alpha * damping)
    tables = jnp.stack(
        [
            jnp.exp(log_decay),
            inflow * eta,
            jnp.exp((rows // SEG) * log_decay),
            jnp.exp(rows * log_decay),
        ]
    )
    ids = jnp.arange(seq * blocks)
    first_end = lengths[0, 0]
    second_end = first_end + lengths[0, 1]
    keep = 1.0 - ((ids == 0) | (ids == first_end) | (ids == second_end)).astype(f32)
    keep = keep.reshape(seq, blocks)
    mine = lax.dynamic_index_in_dim(keep, me, 0, keepdims=False)
    sk = jnp.ones((blocks, SEG // blocks), f32).at[:, 0].set(mine).reshape(SEG)
    gains = jnp.stack(
        [
            norm_gain[:, 0],
            norm_shift[:, 0],
            norm_gain[:, 1],
            norm_shift[:, 1],
            ema_omega,
            b_output,
            b_shrink,
            jnp.zeros_like(b_shrink),
        ]
    )
    outs = layer(
        tokens[0],
        cotangent[0],
        sk,
        jnp.prod(keep, axis=1),
        keep[:, 0],
        tables,
        gains,
        (w_value, w_gates, w_output, w_expand, w_shrink),
        (b_value[None], b_gates[None], b_expand[None]),
        query_key.T,
        jnp.roll(position_bias[::-1], 1)[None],
        batch,
        seq,
    )
    output, grad_tokens, blocks_out = outs

    def tall(first, count):
        parts = blocks_out[first : first + count].reshape(count // 2, 2, BLOCK, TILE)
        return parts.transpose(1, 2, 0, 3).reshape(2 * BLOCK, count // 2 * TILE)

    def wide(first, count):
        return blocks_out[first : first + count].transpose(1, 0, 2).reshape(BLOCK, count * TILE)

    nstate = alpha.shape[0]
    hv, gates, ff = b_value.shape[0], b_gates.shape[0], b_expand.shape[0]
    zd = query_key.shape[0]
    dw_shrink, dw_expand, dw_output, dw_value = tall(0, 6), wide(6, 6), tall(12, 6), wide(18, 6)
    dw_gates = jnp.concatenate(
        [wide(24, width // TILE), blocks_out[36, :, :zd], wide(24 + width // TILE, 9)], axis=1
    )
    rest = blocks_out[36, :, zd:]
    tall_rows = 8 + 2 * nstate
    lanes = width // LANES
    s768 = rest[: lanes * tall_rows].reshape(lanes, tall_rows, LANES)
    s768 = s768.transpose(1, 0, 2).reshape(tall_rows, width)
    place = lanes * tall_rows
    small = rest[place : place + 8]
    place += 8
    sums = []
    for count in (hv, ff, gates):
        sums.append(rest[place : place + count // LANES].reshape(count))
        place += count // LANES
    s_value, s_expand, s_gates = sums
    p_sum, q_sum = s768[8 : 8 + nstate], s768[8 + nstate : 8 + 2 * nstate]
    d_inflow = eta * p_sum
    d_eta = inflow * p_sum
    d_decay = eta * inflow * q_sum
    d_alpha = d_inflow * beta - d_decay * damping
    return (
        output[None],
        grad_tokens[None],
        jnp.stack([s768[0], s768[2]], axis=1),
        jnp.stack([s768[1], s768[3]], axis=1),
        (d_alpha * alpha * (1.0 - alpha)).T,
        (-d_decay * alpha * damping * (1.0 - damping)).T,
        (d_inflow * alpha).T,
        d_eta.T,
        s768[4],
        dw_value,
        s_value,
        dw_gates,
        s_gates,
        small[:3].T,
        jnp.roll(small[3][::-1], 1),
        dw_output,
        s768[5],
        dw_expand,
        s_expand,
        dw_shrink,
        s768[6],
    )


def solution(mesh):
    token_spec = P("batch", "seq", None)
    return jax.shard_map(
        functools.partial(shards, mesh.shape["batch"], mesh.shape["seq"]),
        mesh=mesh,
        in_specs=(token_spec, P("batch", None), token_spec) + (P(),) * 19,
        out_specs=(token_spec, token_spec) + (P(),) * 19,
        check_vma=False,
    )
```

```python
import functools
import math
import typing

import jax
import jax.numpy as jnp
from jax import lax
from jax.experimental import pallas as pl
from jax.experimental.pallas import tpu as pltpu
from jax.sharding import PartitionSpec as P

f32 = jnp.float32
bf16 = jnp.bfloat16
MESH = pl.DeviceIdType.MESH

SEG = 8
LANES = 128
TILE = 256

NN = (((1,), (0,)), ((), ()))
NT = (((1,), (1,)), ((), ()))


def split(value):
    high = value.astype(bf16)
    return high, (value - high.astype(f32)).astype(bf16)


def dot(a, b, dims=NN):
    return lax.dot_general(a, b, dims, preferred_element_type=f32)


def dot3(a, b, dims=NN):
    a_high, a_low = a
    b_high, b_low = b
    return dot(a_high, b_high, dims) + (dot(a_high, b_low, dims) + dot(a_low, b_high, dims))


def sigmoid(value):
    return 1.0 / (1.0 + jnp.exp(-value))


def silu(value):
    return value * sigmoid(value)


def dsilu(value):
    s = sigmoid(value)
    return s * (1.0 + value * (1.0 - s))


def row_get(ref, part):
    return jnp.concatenate([ref[d, part, :] for d in range(ref.shape[0])], axis=-1)


def row_set(ref, part, value):
    for d in range(ref.shape[0]):
        ref[d, part, :] = value[:, d * LANES : (d + 1) * LANES]


def col_get(ref, i, size=TILE):
    n = size // LANES
    return jnp.concatenate([ref[i * n + k] for k in range(n)], axis=-1)


def col_set(ref, i, value):
    n = value.shape[1] // LANES
    for k in range(n):
        ref[i * n + k] = value[:, k * LANES : (k + 1) * LANES]


def at(i, size):
    return pl.ds(pl.multiple_of(i * size, size), size)


def off(start, i, size):
    return pl.ds(pl.multiple_of(start + i * size, LANES), size)


def bit_of(bit):
    name, step = bit
    return lax.rem(lax.div(lax.axis_index(name), step), 2)


def partner(bit):
    name, step = bit
    where = {"batch": lax.axis_index("batch"), "seq": lax.axis_index("seq")}
    where[name] = where[name] + step * (1 - 2 * bit_of(bit))
    return (where["batch"], where["seq"])


HALVINGS = 5
BLOCK = 768
TILES = 2
SERVICE = 0.7
JOBS = 19
KINDS = (0, 1, 0, 1, 2, 0, 1, 0, 1, 3)


def slot_count(seq):
    return 7 if seq <= 16 else 3


def bits_of(batch, seq):
    chips = [("batch", 1 << k) for k in range(batch.bit_length() - 1)]
    line = [("seq", 1 << k) for k in range(1, seq.bit_length() - 1)]
    return ("seq", 1), chips, line


def stage_orders(batch, seq):
    core, chips, line = bits_of(batch, seq)
    flipped = chips[::-1]
    return (
        [core] + chips + line,
        [core] + flipped + line,
        [core] + line + chips,
        [core] + line + flipped,
    )


def stage_rows(count):
    return [BLOCK >> (min(s, HALVINGS - 1) + 1) for s in range(count)]


class Links:
    LATENCY = 1.5
    CORE, LINE = 0.6, 0.0455

    def __init__(self):
        self.now = 0.0
        self.active = {}
        self.arrived = {}

    def uses(self, bit):
        name, step = bit
        if bit == ("seq", 1):
            return (("core", 1),)
        if name == "batch":
            return ((name + str(step), 1),)
        return (("ends", 1),) if step == 2 else (("ends", 1), ("middle", 2))

    def start(self, key, size, bit):
        self.active[key] = [size, self.uses(bit)]

    def rates(self):
        load = {}
        for _size, uses in self.active.values():
            for link, weight in uses:
                load[link] = load.get(link, 0) + weight
        return {
            key: min((self.CORE if link == "core" else self.LINE) / load[link] for link, _w in uses)
            for key, (_size, uses) in self.active.items()
        }

    def forward(self, until=None):
        while self.active:
            rates = self.rates()
            key = min(self.active, key=lambda k: self.active[k][0] / rates[k])
            step = self.active[key][0] / rates[key]
            if until is not None and self.now + step > until:
                step = until - self.now
                key = None
            for k in self.active:
                self.active[k][0] -= step * rates[k]
            self.now += step
            if key is None:
                return
            del self.active[key]
            self.arrived[key] = self.now + self.LATENCY
            if until is None:
                return
        if until is not None:
            self.now = max(self.now, until)


class Reducer:
    def __init__(self, orders, slots, kinds, pieces, tile, red, sems):
        self.slots = slots
        self.orders, self.kinds, self.pieces = orders, kinds, pieces
        self.subs = [max(p[0] for p in job) + 1 for job in pieces]
        self.tile, self.red = tile, red
        self.send, self.recv, self.credit, self.local, self.gsend, self.grecv = sems
        self.stages = len(orders[0])
        self.halvings = min(HALVINGS, self.stages)
        self.rows = stage_rows(self.stages)
        self.jobs = len(pieces)
        self.links = Links()
        self.due = {}
        self.done = [-1] * self.jobs

    def order(self, j):
        return self.orders[self.kinds[j]]

    def part(self, ref, slot, j, start, size):
        if not isinstance(start, int):
            start = pl.multiple_of(start, 8)
        return ref.at[slot, pl.ds(0, self.subs[j]), pl.ds(start, size), :]

    def held(self, j, s):
        if s < 0:
            return self.tile, j % TILES, BLOCK
        return self.red[s], j % self.slots, self.rows[s]

    def keep_start(self, j, s):
        return bit_of(self.order(j)[s]) * self.rows[s] if s < self.halvings else 0

    def give_start(self, j, s):
        return (1 - bit_of(self.order(j)[s])) * self.rows[s] if s < self.halvings else 0

    def scatter_copy(self, j, s):
        ref, slot, _rows = self.held(j, s - 1)
        into, into_slot, rows = self.held(j, s)
        return pltpu.make_async_remote_copy(
            src_ref=self.part(ref, slot, j, self.give_start(j, s), rows),
            dst_ref=self.part(into, into_slot, j, 0, rows),
            send_sem=self.send.at[s, into_slot],
            recv_sem=self.recv.at[s, into_slot],
            device_id=partner(self.order(j)[s]),
            device_id_type=MESH,
        )

    def owned(self, j, s, flip=False):
        start = 0
        for t in range(s + 1):
            bit = bit_of(self.order(j)[t])
            if flip and t == s:
                bit = 1 - bit
            start = start + bit * self.rows[t]
        return [
            target.at[
                pl.ds(pl.multiple_of(row + start, 8), self.rows[s]), pl.ds(col, count)
            ]
            for _block, _from, count, target, row, col in self.pieces[j]
        ]

    def final(self, j):
        ref, slot, rows = self.held(j, self.stages - 1)
        return [
            ref.at[slot, block, pl.ds(0, rows), pl.ds(from_col, count)]
            for block, from_col, count, _target, _row, _col in self.pieces[j]
        ]

    def gather_copies(self, j, s, arriving=False):
        last = s == self.halvings - 1
        sources = self.final(j) if last else self.owned(j, s)
        return [
            pltpu.make_async_remote_copy(
                src_ref=source,
                dst_ref=target,
                send_sem=self.gsend.at[j, s, p],
                recv_sem=self.grecv.at[j, s, p],
                device_id=partner(self.order(j)[s]),
                device_id_type=MESH,
            )
            for p, (source, target) in enumerate(zip(sources, self.owned(j, s, flip=arriving)))
        ]

    def local_copies(self, j):
        pairs = zip(self.final(j), self.owned(j, self.halvings - 1))
        return [
            pltpu.make_async_copy(source, target, self.local.at[j, p])
            for p, (source, target) in enumerate(pairs)
        ]

    def sent(self, j, event, s):
        size = self.rows[s] * self.subs[j] * TILE * 4e-6
        self.links.start((j, event), size, self.order(j)[s])
        self.due[j] = event

    def advance(self, us):
        self.links.forward(self.links.now + us)

    def run(self, j):
        event = self.due.pop(j)
        while (j, event) not in self.links.arrived:
            self.links.forward()
        self.links.forward(max(self.links.now, self.links.arrived.pop((j, event))))
        n = self.stages
        if event < n:
            s = event
            copy = self.scatter_copy(j, s)
            copy.wait_send()
            copy.wait_recv()
            self.add(j, s)
            if s > 0:
                self.give_credit(j, s - 1)
            if s < n - 1:
                self.start_scatter(j, s + 1)
            else:
                for copy in self.local_copies(j) + self.gather_copies(j, self.halvings - 1):
                    copy.start()
                self.sent(j, event + 1, self.halvings - 1)
        else:
            s = self.halvings - 1 - (event - n)
            for copy in self.gather_copies(j, s, True):
                copy.wait_recv()
            if s == self.halvings - 1:
                for copy in self.gather_copies(j, s):
                    copy.wait_send()
                for copy in self.local_copies(j):
                    copy.wait()
                self.give_credit(j, n - 1)
            if s > 0:
                for copy in self.gather_copies(j, s - 1):
                    copy.start()
                self.sent(j, event + 1, s - 1)
        self.done[j] = event
        self.advance(SERVICE)

    def add(self, j, s):
        ref, slot, _rows = self.held(j, s - 1)
        into, into_slot, rows = self.held(j, s)
        start = self.keep_start(j, s)
        step = min(48, rows)

        @pl.loop(0, rows // step)
        def _(i):
            for b in range(self.subs[j]):
                here = pl.ds(pl.multiple_of(start + i * step, 8), step)
                there = pl.ds(pl.multiple_of(i * step, 8), step)
                into[into_slot, b, there, :] += ref[slot, b, here, :]

    def give_credit(self, j, s):
        if j + self.slots < self.jobs:
            pl.semaphore_signal(
                self.credit.at[s, j % self.slots],
                inc=1,
                device_id=partner(self.order(j + self.slots)[s]),
                device_id_type=MESH,
            )

    def start_scatter(self, j, s):
        if j >= self.slots:
            self.reach(j - self.slots, s + 1)
            pl.semaphore_wait(self.credit.at[s, j % self.slots], 1)
        self.scatter_copy(j, s).start()
        self.sent(j, s, s)

    def reach(self, j, event):
        while self.done[j] < event:
            self.run(j)

    def acquire(self, j):
        if j >= TILES:
            self.reach(j - TILES, 0)
        return j % TILES

    def produced(self, j):
        self.start_scatter(j, 0)

    def tick(self, us=0.0):
        self.advance(us)
        while True:
            ready = {k: t for k, t in self.links.arrived.items() if t <= self.links.now}
            if not ready:
                break
            self.run(min(ready, key=ready.get)[0])

    def drain(self):
        while self.due:
            if not self.links.arrived:
                self.links.forward()
            self.run(min(self.links.arrived, key=self.links.arrived.get)[0])
        for j in range(self.jobs):
            for s in range(self.halvings - 1):
                for copy in self.gather_copies(j, s):
                    copy.wait_send()


class Refs(typing.NamedTuple):
    x: typing.Any
    cot: typing.Any
    lengths: typing.Any
    norm_gain: typing.Any
    norm_shift: typing.Any
    alpha: typing.Any
    delta: typing.Any
    beta: typing.Any
    eta: typing.Any
    omega_in: typing.Any
    b_output_in: typing.Any
    b_shrink_in: typing.Any
    b_value_in: typing.Any
    b_gates_in: typing.Any
    b_expand_in: typing.Any
    qk: typing.Any
    bias: typing.Any
    w_value: typing.Any
    w_gates: typing.Any
    w_output: typing.Any
    w_expand: typing.Any
    w_shrink: typing.Any
    out_hbm: typing.Any
    dx_hbm: typing.Any
    dw_value: typing.Any
    dw_gates: typing.Any
    dw_output: typing.Any
    dw_expand: typing.Any
    dw_shrink: typing.Any
    sums: typing.Any
    wa: typing.Any
    wb: typing.Any
    wg: typing.Any
    cot_v: typing.Any
    out: typing.Any
    dx: typing.Any
    tables: typing.Any
    gains: typing.Any
    b_value: typing.Any
    b_gates: typing.Any
    b_expand: typing.Any
    normed: typing.Any
    vpre: typing.Any
    gate: typing.Any
    att: typing.Any
    hpre: typing.Any
    mid: typing.Any
    epre: typing.Any
    mpre: typing.Any
    dnorm: typing.Any
    probs: typing.Any
    square: typing.Any
    lh: typing.Any
    ll: typing.Any
    th: typing.Any
    tl: typing.Any
    s768: typing.Any
    s_value: typing.Any
    s_expand: typing.Any
    s_gates: typing.Any
    s_small: typing.Any
    ends: typing.Any
    starts: typing.Any
    e_recv: typing.Any
    f_recv: typing.Any
    wsem: typing.Any
    osem: typing.Any
    send: typing.Any
    recv: typing.Any
    send2: typing.Any
    recv2: typing.Any
    tile: typing.Any
    sems: typing.Any
    red: typing.Any


def kernel(batch, seq, *refs):
    n = len(Refs._fields) - 2
    r = Refs(*refs[:n], refs[n : n + 6], refs[n + 6 :])
    rows, width = r.x.shape
    seg_len = rows // SEG
    me_b, me = lax.axis_index("batch"), lax.axis_index("seq")
    nstate = 16
    hv = r.vpre.shape[1]
    ff = r.epre.shape[1]
    zd = r.qk.shape[1]
    group = r.probs.shape[1]
    groups = rows // group
    reset0 = width + zd
    cand0 = reset0 + hv
    gates = cand0 + width
    scale = 1.0 / math.sqrt(zd)

    sources = (r.w_value, r.w_gates, r.w_output, r.w_expand, r.w_shrink, r.w_output, r.w_value)
    places = (r.wa, r.wg, r.wb, r.wa, r.wb, r.wb, r.wa)
    weights = [
        pltpu.make_async_copy(a, b, r.wsem.at[i]) for i, (a, b) in enumerate(zip(sources, places))
    ]
    cot_copy = pltpu.make_async_copy(r.cot, r.cot_v, r.wsem.at[len(weights)])
    for copy in weights[:3] + [cot_copy]:
        copy.start()

    gate_cols = [i * TILE for i in range(width // TILE)]
    gate_cols += [reset0 + i * TILE for i in range((hv + width) // TILE)]

    def tall_job(ref, i):
        return [(b, 0, TILE, ref, b * BLOCK, i * TILE) for b in range(2)]

    def wide_job(ref, cols):
        return [(b, 0, TILE, ref, 0, cols[b]) for b in range(2)]

    pieces = [tall_job(r.dw_shrink, i) for i in range(width // TILE)]
    pieces += [wide_job(r.dw_expand, (i, i + TILE)) for i in range(0, ff, 2 * TILE)]
    pieces += [tall_job(r.dw_output, i) for i in range(width // TILE)]
    pieces += [wide_job(r.dw_value, (i, i + TILE)) for i in range(0, hv, 2 * TILE)]
    pieces += [wide_job(r.dw_gates, gate_cols[i : i + 2]) for i in range(0, len(gate_cols), 2)]
    pieces.append([(0, 0, zd, r.dw_gates, 0, width), (0, zd, TILE - zd, r.sums, 0, 0)])
    kinds = [KINDS[j % len(KINDS)] for j in range(len(pieces))]
    comm = Reducer(
        stage_orders(batch, seq), slot_count(seq), kinds, pieces, r.tile, r.red, r.sems
    )
    _core, chips, _line = bits_of(batch, seq)

    barrier = pltpu.get_barrier_semaphore()

    def greet(k, _):
        pl.semaphore_signal(
            barrier, inc=1, device_id=(me_b, lax.rem(me + k, seq)), device_id_type=MESH
        )
        return 0

    lax.fori_loop(1, seq, greet, 0)
    for bit in chips:
        pl.semaphore_signal(barrier, inc=1, device_id=partner(bit), device_id_type=MESH)

    alpha, damping = sigmoid(r.alpha[...]), sigmoid(r.delta[...])
    rate = alpha * damping
    series = jnp.full_like(rate, 1.0 / 7.0)
    for n in range(6, 0, -1):
        series = series * rate + 1.0 / n
    log_decay = -rate * series
    for i, value in enumerate(
        (
            1.0 - rate,
            alpha * r.beta[...] * r.eta[...],
            jnp.exp(seg_len * log_decay),
            jnp.exp(rows * log_decay),
        )
    ):
        r.tables[i] = value
    decay, coef, dec_seg, dec_all = (r.tables.at[i] for i in range(4))

    def unfold(source, target, row=0):
        for d in range(source.shape[0]):
            target[row : row + 1, d * LANES : (d + 1) * LANES] = source[d : d + 1, :]

    unfold(r.b_value_in, r.b_value)
    unfold(r.b_gates_in, r.b_gates)
    unfold(r.b_expand_in, r.b_expand)
    for i in range(2):
        r.gains[2 * i : 2 * i + 1, :] = r.norm_gain[i : i + 1, :]
        r.gains[2 * i + 1 : 2 * i + 2, :] = r.norm_shift[i : i + 1, :]
    for i, source in enumerate((r.omega_in, r.b_output_in, r.b_shrink_in)):
        unfold(source, r.gains, 4 + i)
    gain0, shift0, gain1, shift1, omega, b_output, b_shrink = (
        r.gains[i : i + 1, :] for i in range(7)
    )

    first_end = r.lengths[0, 0]
    second_end = first_end + r.lengths[0, 1]

    def keep(group_id):
        starts = (group_id == 0) | (group_id == first_end) | (group_id == second_end)
        return jnp.where(starts, 0.0, 1.0)

    def keep_block(k):
        value = keep(k * groups)
        for g in range(1, groups):
            value = value * keep(k * groups + g)
        return value

    keep_seg = [
        keep(me * groups + k * groups // SEG) if k % (SEG // groups) == 0 else 1.0
        for k in range(SEG)
    ]

    def tiles(count, body, us, parts=1):
        for p in range(parts):
            pl.loop(count * p // parts, count * (p + 1) // parts)(body)
            comm.tick(us / parts)

    def zero_small(i):
        r.s768[i : i + 1, :] = jnp.zeros((1, width), f32)

    for i in range(8):
        zero_small(i)

    def add768(i, value, cols=slice(None)):
        r.s768[i : i + 1, cols] += jnp.sum(value, axis=0, keepdims=True)

    RC = 32

    def norm_stats(value):
        centre = value - jnp.mean(value, axis=-1, keepdims=True)
        inv = lax.rsqrt(jnp.mean(centre * centre, axis=-1, keepdims=True) + 1e-05)
        return centre * inv, inv

    def norm_back(grad, n, inv):
        return inv * (
            grad
            - jnp.mean(grad, axis=-1, keepdims=True)
            - n * jnp.mean(grad * n, axis=-1, keepdims=True)
        )

    @pl.loop(0, rows // RC)
    def _(i):
        part = at(i, RC)
        n, _inv = norm_stats(r.x[part, :])
        value = n * gain0 + shift0
        row_set(r.normed, part, value)
        r.lh[part, :width], r.ll[part, :width] = split(value)

    def seg_rows(t):
        return pl.ds(t, SEG, stride=seg_len)

    def rows_of(ref, count, cols):
        return [jnp.broadcast_to(ref[n : n + 1, cols], (SEG, LANES)) for n in count]

    def end_states(source, reverse, target):
        @pl.loop(0, width // LANES)
        def _(d):
            cols = at(d, LANES)
            dec = rows_of(decay, range(nstate), cols)

            def turn(t, state):
                at_t = seg_len - 1 - t if reverse else t
                value = source[d, seg_rows(at_t), :]
                return tuple(a * s + value for a, s in zip(dec, state))

            zero = jnp.zeros((SEG, LANES), f32)
            state = lax.fori_loop(0, seg_len, turn, (zero,) * nstate, unroll=8)
            for n in range(nstate):
                target[d, n * SEG : (n + 1) * SEG, :] = state[n]

    def seg_of(k):
        return pl.ds(k, nstate, stride=SEG)

    def exchange(buffer, send_sem, recv_sem):
        def copy_to(k):
            peer = lax.rem(me + k, seq)
            return pltpu.make_async_remote_copy(
                src_ref=buffer.at[me],
                dst_ref=buffer.at[me],
                send_sem=send_sem.at[k],
                recv_sem=recv_sem.at[me],
                device_id=(me_b, peer),
                device_id_type=MESH,
            )

        def copy_from(k):
            peer = lax.rem(me + k, seq)
            return pltpu.make_async_remote_copy(
                src_ref=buffer.at[me],
                dst_ref=buffer.at[peer],
                send_sem=send_sem.at[k],
                recv_sem=recv_sem.at[peer],
                device_id=(me_b, peer),
                device_id_type=MESH,
            )

        def start():
            def one(k, _):
                copy_to(k).start()
                return 0

            lax.fori_loop(1, seq, one, 0)

        def wait():
            def one(k, _):
                copy_to(k).wait_send()
                copy_from(k).wait_recv()
                return 0

            lax.fori_loop(1, seq, one, 0)

        return start, wait

    end_states(r.normed, False, r.ends)
    total = jnp.zeros((nstate, width), f32)
    for k in range(SEG):
        total = keep_seg[k] * total * dec_seg[...] + row_get(r.ends, seg_of(k))
    r.e_recv[me] = total
    pl.semaphore_wait(barrier, seq - 1 + len(chips))
    start_e, wait_e = exchange(r.e_recv, r.send, r.recv)
    start_e()

    weights[0].wait()

    @pl.loop(0, hv // TILE)
    def _(i):
        c = at(i, TILE)
        w = r.wa[:, c]
        r.vpre[:, c] = (
            dot(r.lh[:, :width], w) + dot(r.ll[:, :width], w) + r.b_value[:, c]
        )

    weights[3].start()

    wait_e()

    def carry_step(k, carried):
        new = dec_all[...] * (keep_block(k) * carried) + r.e_recv[k]
        return jnp.where(k < me, new, carried)

    state = lax.fori_loop(0, seq, carry_step, jnp.zeros((nstate, width), f32))
    for k in range(SEG):
        state = keep_seg[k] * state
        row_set(r.starts, seg_of(k), state)
        if k < SEG - 1:
            state = dec_seg[...] * state + row_get(r.ends, seg_of(k))

    @pl.loop(0, width // LANES)
    def _(d):
        cols = at(d, LANES)
        dec = rows_of(decay, range(nstate), cols)
        mix = rows_of(coef, range(nstate), cols)

        def turn(t, state):
            value = r.normed[d, seg_rows(t), :]
            state = tuple(a * s + value for a, s in zip(dec, state))
            terms = [m * s for m, s in zip(mix, state)]
            while len(terms) > 1:
                terms = [a + b for a, b in zip(terms[::2], terms[1::2])]
            r.mpre[d, seg_rows(t), :] = terms[0]
            return state

        first = tuple(r.starts[d, n * SEG : (n + 1) * SEG, :] for n in range(nstate))
        lax.fori_loop(0, seg_len, turn, first, unroll=4)

    @pl.loop(0, rows // RC)
    def _(i):
        part = at(i, RC)
        value = row_get(r.mpre, part) + omega * row_get(r.normed, part)
        row_set(r.mpre, part, value)
        r.lh[part, :width], r.ll[part, :width] = split(silu(value))

    weights[1].wait()

    def gate_tile(c):
        w = r.wg[:, c]
        r.gate[:, c] = (
            dot(r.lh[:, :width], w) + dot(r.ll[:, :width], w) + r.b_gates[:, c]
        )

    @pl.loop(0, width // TILE)
    def _(i):
        gate_tile(at(i, TILE))

    gate_tile(pl.ds(width, zd))

    @pl.loop(0, (hv + width) // TILE)
    def _(i):
        gate_tile(off(reset0, i, TILE))

    lag = lax.broadcasted_iota(jnp.int32, (group, group), 0) - lax.broadcasted_iota(
        jnp.int32, (group, group), 1
    )
    row_id = lax.broadcasted_iota(jnp.int32, (group, group), 0)
    causal = lag >= 0
    table = jnp.broadcast_to(r.bias[...], (group, group))
    for b in range(group.bit_length() - 1):
        moved = pltpu.roll(table, 1 << b, 1)
        table = jnp.where((row_id & (1 << b)) != 0, moved, table)
    q_gain, k_gain, q_shift = (r.qk[i : i + 1, :] for i in range(3))
    r.square[...] = table.T

    @pl.loop(0, groups)
    def _(g):
        part = at(g, group)
        shared = silu(r.gate[part, width:reset0])
        q = split(shared * q_gain + q_shift)
        k = split(shared * k_gain)
        scores = dot3(q, k, NT) * scale + r.square[...]
        scores = jnp.where(causal, scores, -1e30)
        p = jnp.exp(scores - jnp.max(scores, axis=-1, keepdims=True))
        p = p / jnp.sum(p, axis=-1, keepdims=True)
        r.probs[part, :] = p
        p = split(p)

        @pl.loop(0, hv // TILE)
        def _(i):
            c = at(i, TILE)
            v = split(silu(r.vpre[part, c]))
            attended = dot3(p, v)
            r.att[part, c] = attended
            gated = attended * silu(r.gate[part, off(reset0, i, TILE)])
            r.lh[part, c], r.ll[part, c] = split(gated)

    weights[2].wait()

    @pl.loop(0, width // TILE)
    def _(i):
        c = at(i, TILE)
        w = r.wb[:, c]
        value = (
            dot(r.lh[...], w)
            + dot(r.ll[...], w)
            + (r.gate[:, off(cand0, i, TILE)] + r.gains[5:6, c])
        )
        r.hpre[:, c] = value
        x = r.x[:, c]
        r.mid[:, c] = x + sigmoid(r.gate[:, c]) * (silu(value) - x)

    weights[4].start()

    @pl.loop(0, rows // RC)
    def _(i):
        part = at(i, RC)
        n, _inv = norm_stats(r.mid[part, :])
        r.lh[part, :width], r.ll[part, :width] = split(n * gain1 + shift1)

    weights[3].wait()

    @pl.loop(0, ff // TILE)
    def _(i):
        c = at(i, TILE)
        w = r.wa[:, c]
        r.epre[:, c] = (
            dot(r.lh[:, :width], w) + dot(r.ll[:, :width], w) + r.b_expand[:, c]
        )

    comm.advance(50.0)
    cot_copy.wait()

    def transposed(source, count, first=0):
        @pl.loop(0, count // LANES)
        def _(i):
            here = off(first, i, LANES)
            r.th[here, :], r.tl[here, :] = split(source(i, at(i, LANES)).T)

    def products(j, pairs):
        slot = comm.acquire(j)
        for b, (first, grad) in enumerate(pairs):
            g = split(grad)
            cols = grad.shape[1]

            @pl.loop(0, BLOCK // TILE)
            def _(k):
                a = off(first, k, TILE)
                value = dot3((r.th[a, :], r.tl[a, :]), g)
                if cols == TILE:
                    r.tile[slot, b, at(k, TILE), :] = value
                else:
                    r.tile[slot, b, at(k, TILE), :cols] = value

        comm.advance(1.0 * len(pairs))
        return slot

    def tall(j, grad):
        products(j, [(0, grad), (BLOCK, grad)])
        comm.produced(j)
        comm.tick()

    def wide(j, first, left, right):
        products(j, [(first, left), (first, right)])
        comm.produced(j)
        comm.tick()

    def cols_of(ref, i, start=0):
        return ref[:, start + i * TILE : start + (i + 1) * TILE]

    transposed(lambda i, c: silu(r.epre[:, c]), ff)
    comm.advance(2.0)
    for i in range(width // TILE):
        tall(i, cols_of(r.cot_v, i))

    def inner_halves(i):
        c = at(i, TILE)
        r.lh[:, c], r.ll[:, c] = split(silu(r.epre[:, c]))

    tiles(ff // TILE, inner_halves, 1.2)
    weights[4].wait()

    def out_tile(i):
        c = at(i, TILE)
        w = r.wb[:, c]
        r.out[:, c] = r.mid[:, c] + (dot(r.lh[...], w) + dot(r.ll[...], w) + r.gains[6:7, c])

    tiles(width // TILE, out_tile, 3.0)
    out_copy = pltpu.make_async_copy(r.out, r.out_hbm, r.osem.at[0])
    out_copy.start()

    def cot_halves(i):
        part = at(i, RC)
        value = r.cot_v[part, :]
        add768(6, value)
        r.lh[part, :width], r.ll[part, :width] = split(value)

    tiles(rows // RC, cot_halves, 1.0)

    def inner_back(i):
        c = at(i, TILE)
        w = r.wb[c, :]
        value = (dot(r.lh[:, :width], w, NT) + dot(r.ll[:, :width], w, NT)) * dsilu(
            r.epre[:, c]
        )
        r.epre[:, c] = value
        r.s_expand[:, c] = jnp.sum(value, axis=0, keepdims=True)

    tiles(ff // TILE, inner_back, 3.2)
    weights[5].start()

    def expand_halves(i):
        c = at(i, TILE)
        r.lh[:, c], r.ll[:, c] = split(r.epre[:, c])

    tiles(ff // TILE, expand_halves, 0.8)

    @pl.loop(0, rows // RC)
    def _(i):
        part = at(i, RC)
        n, _inv = norm_stats(r.mid[part, :])
        row_set(r.dnorm, part, n * gain1 + shift1)

    transposed(lambda i, c: r.dnorm[i], width)
    comm.tick(2.0)
    for i in range(ff // (2 * TILE)):
        wide(3 + i, 0, cols_of(r.epre, 2 * i), cols_of(r.epre, 2 * i + 1))

    @pl.loop(0, width // TILE)
    def _(i):
        c = at(i, TILE)
        w = r.wa[c, :]
        r.dx[:, c] = dot(r.lh[...], w, NT) + dot(r.ll[...], w, NT)

    weights[6].start()
    comm.tick(3.0)

    def middle_back(i):
        part = at(i, RC)
        grad = r.dx[part, :]
        n, inv = norm_stats(r.mid[part, :])
        add768(2, grad * n)
        add768(3, grad)
        dmid = r.cot_v[part, :] + norm_back(grad * gain1, n, inv)
        update = sigmoid(r.gate[part, :width])
        pre = r.hpre[part, :]
        x = r.x[part, :]
        dhpre = dmid * update * dsilu(pre)
        r.dx[part, :] = dmid * (1.0 - update)
        dupdate = dmid * (silu(pre) - x) * (update * (1.0 - update))
        r.gate[part, :width] = dupdate
        r.gate[part, cand0:] = dhpre
        r.lh[part, :width], r.ll[part, :width] = split(dhpre)
        r.s_gates[:, :width] = (
            jnp.where(i == 0, 0.0, r.s_gates[:, :width])
            + jnp.sum(dupdate, axis=0, keepdims=True)
        )
        add768(5, dhpre)

    tiles(rows // RC, middle_back, 5.0, 2)

    transposed(lambda i, c: r.att[:, c] * silu(r.gate[:, off(reset0, i, LANES)]), hv)
    weights[5].wait()
    comm.tick(3.0)
    for i in range(width // TILE):
        tall(6 + i, cols_of(r.gate, i, cand0))

    def attended_back(i):
        c = at(i, TILE)
        w = r.wb[c, :]
        gated = dot(r.lh[:, :width], w, NT) + dot(r.ll[:, :width], w, NT)
        here = off(reset0, i, TILE)
        pre = r.gate[:, here]
        dreset = gated * r.att[:, c] * dsilu(pre)
        r.att[:, c] = gated * silu(pre)
        r.gate[:, here] = dreset
        r.s_gates[:, here] = jnp.sum(dreset, axis=0, keepdims=True)

    tiles(hv // TILE, attended_back, 3.5)

    r.s_small[...] = jnp.zeros_like(r.s_small)
    r.square[...] = jnp.zeros((group, group), f32)

    def attention_back(g):
        part = at(g, group)
        p = r.probs[part, :]
        p_t = split(p.T)

        def value_tile(i, dp):
            c = at(i, TILE)
            pre = r.vpre[part, c]
            d_att = split(r.att[part, c])
            r.vpre[part, c] = dot3(p_t, d_att) * dsilu(pre)
            return dp + dot3(d_att, split(silu(pre)), NT)

        dp = lax.fori_loop(0, hv // TILE, value_tile, jnp.zeros((group, group), f32))
        ds = p * (dp - jnp.sum(dp * p, axis=-1, keepdims=True))
        r.square[...] += ds
        ds = ds * scale
        pre = r.gate[part, width:reset0]
        shared = silu(pre)
        dq = dot3(split(ds), split(shared * k_gain))
        dk = dot3(split(ds.T), split(shared * q_gain + q_shift))
        for n, value in enumerate((dq * shared, dk * shared, dq)):
            r.s_small[n : n + 1, :] += jnp.sum(value, axis=0, keepdims=True)
        r.gate[part, width:reset0] = (dq * q_gain + dk * k_gain) * dsilu(pre)

    tiles(groups, attention_back, 8.4, 4)
    diagonals = r.square[...].T
    for b in range(group.bit_length() - 1):
        moved = pltpu.roll(diagonals, group - (1 << b), 1)
        diagonals = jnp.where((row_id & (1 << b)) != 0, moved, diagonals)
    r.s_small[3:4, :] = jnp.sum(diagonals, axis=0, keepdims=True)
    r.s_gates[:, width:reset0] = jnp.sum(r.gate[:, width:reset0], axis=0, keepdims=True)
    r.s_gates[:, cand0:] = r.s768[5:6, :]

    comm.tick(0.5)
    weights[6].wait()

    @pl.loop(0, hv // TILE)
    def _(i):
        c = at(i, TILE)
        value = r.vpre[:, c]
        r.s_value[:, c] = jnp.sum(value, axis=0, keepdims=True)
        r.lh[:, c], r.ll[:, c] = split(value)

    @pl.loop(0, width // TILE)
    def _(i):
        c = at(i, TILE)
        w = r.wa[c, :]
        col_set(r.dnorm, i, dot(r.lh[...], w, NT) + dot(r.ll[...], w, NT))

    comm.tick(4.2)
    transposed(lambda i, c: r.normed[i], width, width)
    transposed(lambda i, c: silu(r.mpre[i]), width)
    comm.tick(2.5)

    def gate_section(start, size, first, last):
        @pl.loop(0, size // LANES)
        def _(i):
            c = at(i, LANES)
            r.lh[:, c], r.ll[:, c] = split(r.gate[:, off(start, i, LANES)])

        @pl.loop(0, width // TILE)
        def _(i):
            c = at(i, TILE)
            w = r.wg[c, start : start + size]
            value = dot(r.lh[:, :size], w, NT) + dot(r.ll[:, :size], w, NT)
            if not first:
                value += r.att[:, c]
            if last:
                value = value * dsilu(col_get(r.mpre, i))
                col_set(r.mpre, i, value)
                add768(4, value * col_get(r.normed, i), c)
                col_set(r.dnorm, i, col_get(r.dnorm, i) + r.gains[4:5, c] * value)
            else:
                r.att[:, c] = value

        comm.tick(size * 8.0 / gates)

    gate_section(0, reset0, True, False)
    gate_section(reset0, hv, False, False)
    gate_section(cand0, width, False, True)

    end_states(r.mpre, True, r.ends)
    adj = jnp.zeros((nstate, width), f32)
    for k in reversed(range(SEG)):
        if k < SEG - 1:
            adj = dec_seg[...] * (keep_seg[k + 1] * adj)
        adj = adj + row_get(r.ends, seg_of(k))
    r.f_recv[me] = adj
    start_f, wait_f = exchange(r.f_recv, r.send2, r.recv2)
    start_f()

    comm.tick(4.0)
    wait_f()
    comm.tick(7.0)

    def adj_step(j, carried):
        k = seq - 1 - j
        new = keep(k * groups) * r.f_recv[k] + dec_all[...] * (keep_block(k) * carried)
        return jnp.where(k > me, new, carried)

    adj = lax.fori_loop(0, seq, adj_step, jnp.zeros((nstate, width), f32))
    for k in reversed(range(SEG)):
        fresh = row_get(r.ends, seg_of(k))
        row_set(r.ends, seg_of(k), adj)
        if k > 0:
            adj = keep_seg[k] * (dec_seg[...] * adj + fresh)

    half = nstate // 2
    for h in range(2):
        states = range(h * half, (h + 1) * half)

        def average_back(d):
            cols = at(d, LANES)
            dec = rows_of(decay, states, cols)
            mix = rows_of(coef, states, cols)

            def ahead(t, state):
                value = r.normed[d, seg_rows(t), :]
                for n in range(half):
                    r.epre[at(t, SEG), n * LANES : (n + 1) * LANES] = state[n]
                return tuple(a * s + value for a, s in zip(dec, state))

            first = tuple(r.starts[d, n * SEG : (n + 1) * SEG, :] for n in states)
            lax.fori_loop(0, seg_len, ahead, first, unroll=4)

            def back(j, carried):
                t = seg_len - 1 - j
                adj, p_sum, q_sum = carried
                grad = r.mpre[d, seg_rows(t), :]
                value = r.normed[d, seg_rows(t), :]
                adj = tuple(a * s + grad for a, s in zip(dec, adj))
                p_sum = tuple(p + a * value for p, a in zip(p_sum, adj))
                q_sum = tuple(
                    q + a * r.epre[at(t, SEG), n * LANES : (n + 1) * LANES]
                    for n, (q, a) in enumerate(zip(q_sum, adj))
                )
                terms = [m * a for m, a in zip(mix, adj)]
                while len(terms) > 1:
                    terms = [a + b for a, b in zip(terms[::2], terms[1::2])]
                r.dnorm[d, seg_rows(t), :] += terms[0]
                return adj, p_sum, q_sum

            zero = (jnp.zeros((SEG, LANES), f32),) * half
            last = tuple(r.ends[d, n * SEG : (n + 1) * SEG, :] for n in states)
            _adj, p_sum, q_sum = lax.fori_loop(0, seg_len, back, (last, zero, zero), unroll=4)
            for n in range(half):
                row = 8 + h * half + n
                r.s768[row : row + 1, cols] = jnp.sum(p_sum[n], axis=0, keepdims=True)
                row = row + nstate
                r.s768[row : row + 1, cols] = jnp.sum(q_sum[n], axis=0, keepdims=True)

        tiles(width // LANES, average_back, 12.0, 6)

    def first_back(i):
        part = at(i, RC)
        grad = row_get(r.dnorm, part)
        n, inv = norm_stats(r.x[part, :])
        add768(0, grad * n)
        add768(1, grad)
        r.dx[part, :] += norm_back(grad * gain0, n, inv)

    tiles(rows // RC, first_back, 3.0)
    dx_copy = pltpu.make_async_copy(r.dx, r.dx_hbm, r.osem.at[1])
    dx_copy.start()

    for i in range(hv // (2 * TILE)):
        wide(9 + i, width, cols_of(r.vpre, 2 * i), cols_of(r.vpre, 2 * i + 1))
    for i in range(len(gate_cols) // 2):
        left, right = gate_cols[2 * i : 2 * i + 2]
        wide(12 + i, 0, cols_of(r.gate, 0, left), cols_of(r.gate, 0, right))

    slot = products(comm.jobs - 1, [(0, r.gate[:, width:reset0])])
    r.tile[slot, 0, :, zd:] = jnp.zeros((BLOCK, TILE - zd), f32)
    place = 0

    def put(value):
        nonlocal place
        count = value.shape[0]
        r.tile[slot, 0, place : place + count, zd:] = value
        place += count

    for d in range(width // LANES):
        put(r.s768[:, d * LANES : (d + 1) * LANES])
    put(r.s_small[...])
    for ref in (r.s_value, r.s_expand, r.s_gates):
        for d in range(ref.shape[1] // LANES):
            put(ref[:, d * LANES : (d + 1) * LANES])
    comm.produced(comm.jobs - 1)
    comm.drain()
    out_copy.wait()
    dx_copy.wait()


def finish(sums, alpha, delta, beta, eta, *outs):
    gain, shift, d_alpha, d_delta, d_beta, d_eta, omega, b_output, b_shrink = outs[:9]
    qk, bias, b_value, b_expand, b_gates = outs[9:]
    nstate, width = alpha.shape
    tall_rows = 8 + 2 * nstate
    for d in range(width // LANES):
        cols = slice(d * LANES, (d + 1) * LANES)
        row = d * tall_rows
        for n in range(2):
            gain[n : n + 1, cols] = sums[row + 2 * n : row + 2 * n + 1, :]
            shift[n : n + 1, cols] = sums[row + 2 * n + 1 : row + 2 * n + 2, :]
        for n, target in enumerate((omega, b_output, b_shrink)):
            target[d : d + 1, :] = sums[row + 4 + n : row + 5 + n, :]
        p_sum = sums[row + 8 : row + 8 + nstate, :]
        q_sum = sums[row + 8 + nstate : row + 8 + 2 * nstate, :]
        rate, damping = sigmoid(alpha[:, cols]), sigmoid(delta[:, cols])
        d_inflow = eta[:, cols] * p_sum
        d_eta[:, cols] = rate * beta[:, cols] * p_sum
        d_decay = eta[:, cols] * (rate * beta[:, cols]) * q_sum
        d_rate = d_inflow * beta[:, cols] - d_decay * damping
        d_alpha[:, cols] = d_rate * rate * (1.0 - rate)
        d_delta[:, cols] = -d_decay * rate * damping * (1.0 - damping)
        d_beta[:, cols] = d_inflow * rate
    place = width // LANES * tall_rows
    qk[...] = sums[place : place + 3, :]
    bias[...] = sums[place + 3 : place + 4, :]
    place += 8
    for target in (b_value, b_expand, b_gates):
        target[...] = sums[place : place + target.shape[0], :]
        place += target.shape[0]


def layer(operands, batch, seq):
    rows, width = operands[0].shape
    w_value, w_gates, w_output, w_expand, w_shrink = operands[-5:]
    hv, gates, ff = w_value.shape[1], w_gates.shape[1], w_expand.shape[1]
    zd, group, nstate = operands[15].shape[1], operands[16].shape[1], operands[5].shape[0]
    vmem = pl.BlockSpec(memory_space=pltpu.VMEM)
    smem = pl.BlockSpec(memory_space=pltpu.SMEM)
    hbm = pl.BlockSpec(memory_space=pl.ANY)
    stages, slots = len(stage_orders(batch, seq)[0]), slot_count(seq)

    def shape(*dims, kind=f32):
        return jax.ShapeDtypeStruct(dims, kind)

    return pl.pallas_call(
        functools.partial(kernel, batch, seq),
        out_shape=(
            shape(rows, width),
            shape(rows, width),
            shape(width, hv),
            shape(width, gates),
            shape(hv, width),
            shape(width, ff),
            shape(ff, width),
            shape(BLOCK, TILE - zd),
        ),
        in_specs=[vmem, hbm, smem] + [vmem] * 14 + [hbm] * 5,
        out_specs=(hbm,) * 8,
        scratch_shapes=[
            pltpu.VMEM(w_value.shape, bf16),
            pltpu.VMEM(w_output.shape, bf16),
            pltpu.VMEM(w_gates.shape, bf16),
            pltpu.VMEM((rows, width), f32),
            pltpu.VMEM((rows, width), f32),
            pltpu.VMEM((rows, width), f32),
            pltpu.VMEM((4, nstate, width), f32),
            pltpu.VMEM((8, width), f32),
            pltpu.VMEM((1, hv), f32),
            pltpu.VMEM((1, gates), f32),
            pltpu.VMEM((1, ff), f32),
            pltpu.VMEM((width // LANES, rows, LANES), f32),
            pltpu.VMEM((rows, hv), f32),
            pltpu.VMEM((rows, gates), f32),
            pltpu.VMEM((rows, hv), f32),
            pltpu.VMEM((rows, width), f32),
            pltpu.VMEM((rows, width), f32),
            pltpu.VMEM((rows, ff), f32),
            pltpu.VMEM((width // LANES, rows, LANES), f32),
            pltpu.VMEM((width // LANES, rows, LANES), f32),
            pltpu.VMEM((rows, group), f32),
            pltpu.VMEM((group, group), f32),
            pltpu.VMEM((rows, max(hv, ff)), bf16),
            pltpu.VMEM((rows, max(hv, ff)), bf16),
            pltpu.VMEM((max(hv, ff), rows), bf16),
            pltpu.VMEM((max(hv, ff), rows), bf16),
            pltpu.VMEM((8 + 2 * nstate, width), f32),
            pltpu.VMEM((1, hv), f32),
            pltpu.VMEM((1, ff), f32),
            pltpu.VMEM((1, gates), f32),
            pltpu.VMEM((8, zd), f32),
            pltpu.VMEM((width // LANES, nstate * SEG, LANES), f32),
            pltpu.VMEM((width // LANES, nstate * SEG, LANES), f32),
            pltpu.VMEM((seq, nstate, width), f32),
            pltpu.VMEM((seq, nstate, width), f32),
            pltpu.SemaphoreType.DMA((8,)),
            pltpu.SemaphoreType.DMA((2,)),
            pltpu.SemaphoreType.DMA((seq,)),
            pltpu.SemaphoreType.DMA((seq,)),
            pltpu.SemaphoreType.DMA((seq,)),
            pltpu.SemaphoreType.DMA((seq,)),
            pltpu.VMEM((TILES, 2, BLOCK, TILE), f32),
            pltpu.SemaphoreType.DMA((stages, slots)),
            pltpu.SemaphoreType.DMA((stages, slots)),
            pltpu.SemaphoreType.REGULAR((stages, slots)),
            pltpu.SemaphoreType.DMA((JOBS, 2)),
            pltpu.SemaphoreType.DMA((JOBS, HALVINGS, 2)),
            pltpu.SemaphoreType.DMA((JOBS, HALVINGS, 2)),
        ]
        + [pltpu.VMEM((slots, 2, count, TILE), f32) for count in stage_rows(stages)],
        compiler_params=pltpu.CompilerParams(
            collective_id=0, has_side_effects=True, vmem_limit_bytes=63 << 20
        ),
        cost_estimate=pl.CostEstimate(
            flops=52_000_000_000, bytes_accessed=60_000_000, transcendentals=20_000_000
        ),
    )(*operands)


def shards(
    batch,
    seq,
    tokens,
    lengths,
    cotangent,
    norm_gain,
    norm_shift,
    alpha_logit,
    delta_logit,
    ema_beta,
    ema_eta,
    ema_omega,
    w_value,
    b_value,
    w_gates,
    b_gates,
    query_key,
    position_bias,
    w_output,
    b_output,
    w_expand,
    b_expand,
    w_shrink,
    b_shrink,
):
    def lines(vector):
        return vector.reshape(-1, LANES)

    averages = (alpha_logit.T, delta_logit.T, ema_beta.T, ema_eta.T)
    operands = (tokens[0], cotangent[0], lengths, norm_gain.T, norm_shift.T) + averages
    operands += (lines(ema_omega), lines(b_output), lines(b_shrink))
    operands += (lines(b_value), lines(b_gates), lines(b_expand))
    operands += (query_key.T, position_bias[None])
    operands += (w_value, w_gates, w_output, w_expand, w_shrink)
    output, grad_tokens, dw_value, dw_gates, dw_output, dw_expand, dw_shrink, sums = layer(
        operands, batch, seq
    )
    like = (norm_gain.T, norm_shift.T) + averages
    like += (lines(ema_omega), lines(b_output), lines(b_shrink), query_key.T)
    like += (position_bias[None], lines(b_value), lines(b_expand), lines(b_gates))
    small = pl.pallas_call(
        finish, out_shape=tuple(jax.ShapeDtypeStruct(a.shape, f32) for a in like)
    )(sums, *averages)
    gain, shift, d_alpha, d_delta, d_beta, d_eta, d_omega, d_output, d_shrink = small[:9]
    d_qk, d_bias, d_value, d_expand, d_gates = small[9:]
    return (
        output[None],
        grad_tokens[None],
        gain.T,
        shift.T,
        d_alpha.T,
        d_delta.T,
        d_beta.T,
        d_eta.T,
        d_omega.reshape(-1),
        dw_value,
        d_value.reshape(-1),
        dw_gates,
        d_gates.reshape(-1),
        d_qk.T,
        d_bias[0],
        dw_output,
        d_output.reshape(-1),
        dw_expand,
        d_expand.reshape(-1),
        dw_shrink,
        d_shrink.reshape(-1),
    )


def solution(mesh):
    token_spec = P("batch", "seq", None)
    return jax.shard_map(
        functools.partial(shards, mesh.shape["batch"], mesh.shape["seq"]),
        mesh=mesh,
        in_specs=(token_spec, P("batch", None), token_spec) + (P(),) * 19,
        out_specs=(token_spec, token_spec) + (P(),) * 19,
        check_vma=False,
    )
```

```python
import functools
import math
import typing

import jax
import jax.numpy as jnp
from jax import lax
from jax.experimental import pallas as pl
from jax.experimental.pallas import tpu as pltpu
from jax.sharding import PartitionSpec as P

f32 = jnp.float32
bf16 = jnp.bfloat16
MESH = pl.DeviceIdType.MESH

SEG = 8
LANES = 128
TILE = 256

NN = (((1,), (0,)), ((), ()))
NT = (((1,), (1,)), ((), ()))


def split(value):
    high = value.astype(bf16)
    return high, (value - high.astype(f32)).astype(bf16)


def dot(a, b, dims=NN):
    return lax.dot_general(a, b, dims, preferred_element_type=f32)


def dot3(a, b, dims=NN):
    a_high, a_low = a
    b_high, b_low = b
    return dot(a_high, b_high, dims) + (dot(a_high, b_low, dims) + dot(a_low, b_high, dims))


def sigmoid(value):
    return 1.0 / (1.0 + jnp.exp(-value))


def silu(value):
    return value * sigmoid(value)


def dsilu(value):
    s = sigmoid(value)
    return s * (1.0 + value * (1.0 - s))


def row_get(ref, part):
    return jnp.concatenate([ref[d, part, :] for d in range(ref.shape[0])], axis=-1)


def row_set(ref, part, value):
    for d in range(ref.shape[0]):
        ref[d, part, :] = value[:, d * LANES : (d + 1) * LANES]


def col_get(ref, i, size=TILE):
    n = size // LANES
    return jnp.concatenate([ref[i * n + k] for k in range(n)], axis=-1)


def col_set(ref, i, value):
    n = value.shape[1] // LANES
    for k in range(n):
        ref[i * n + k] = value[:, k * LANES : (k + 1) * LANES]


def at(i, size):
    return pl.ds(pl.multiple_of(i * size, size), size)


def off(start, i, size):
    return pl.ds(pl.multiple_of(start + i * size, LANES), size)


def bit_of(bit):
    name, step = bit
    return lax.rem(lax.div(lax.axis_index(name), step), 2)


def partner(bit):
    name, step = bit
    where = {"batch": lax.axis_index("batch"), "seq": lax.axis_index("seq")}
    where[name] = where[name] + step * (1 - 2 * bit_of(bit))
    return (where["batch"], where["seq"])


HALVINGS = 5
BLOCK = 768
TILES = 2
SERVICE = 0.5
JOBS = 19
KINDS = (0, 1, 0, 1, 2, 0, 1, 0, 1, 3)


def slot_count(seq):
    return 8 if seq <= 16 else 4


def bits_of(batch, seq):
    chips = [("batch", 1 << k) for k in range(batch.bit_length() - 1)]
    line = [("seq", 1 << k) for k in range(1, seq.bit_length() - 1)]
    return ("seq", 1), chips, line


def stage_orders(batch, seq):
    core, chips, line = bits_of(batch, seq)
    flipped = chips[::-1]
    return (
        [core] + chips + line,
        [core] + flipped + line,
        [core] + line + chips,
        [core] + line + flipped,
    )


def stage_rows(count):
    return [BLOCK >> (min(s, HALVINGS - 1) + 1) for s in range(count)]


class Links:
    LATENCY = 8.0
    CORE, LINE = 0.6, 0.041

    def __init__(self):
        self.now = 0.0
        self.active = {}
        self.arrived = {}

    def uses(self, bit):
        name, step = bit
        if bit == ("seq", 1):
            return (("core", 1),)
        if name == "batch":
            return ((name + str(step), 1),)
        return (("ends", 1),) if step == 2 else (("ends", 1), ("middle", 2))

    def start(self, key, size, bit):
        self.active[key] = [size, self.uses(bit)]

    def rates(self):
        load = {}
        for _size, uses in self.active.values():
            for link, weight in uses:
                load[link] = load.get(link, 0) + weight
        return {
            key: min((self.CORE if link == "core" else self.LINE) / load[link] for link, _w in uses)
            for key, (_size, uses) in self.active.items()
        }

    def forward(self, until=None):
        while self.active:
            rates = self.rates()
            key = min(self.active, key=lambda k: self.active[k][0] / rates[k])
            step = self.active[key][0] / rates[key]
            if until is not None and self.now + step > until:
                step = until - self.now
                key = None
            for k in self.active:
                self.active[k][0] -= step * rates[k]
            self.now += step
            if key is None:
                return
            del self.active[key]
            self.arrived[key] = self.now + self.LATENCY
            if until is None:
                return
        if until is not None:
            self.now = max(self.now, until)


class Reducer:
    def __init__(self, orders, slots, kinds, pieces, tile, red, sems):
        self.slots = slots
        self.orders, self.kinds, self.pieces = orders, kinds, pieces
        self.subs = [max(p[0] for p in job) + 1 for job in pieces]
        self.tile, self.red = tile, red
        self.send, self.recv, self.credit, self.local, self.gsend, self.grecv = sems
        self.stages = len(orders[0])
        self.halvings = min(HALVINGS, self.stages)
        self.rows = stage_rows(self.stages)
        self.jobs = len(pieces)
        self.links = Links()
        self.due = {}
        self.done = [-1] * self.jobs

    def order(self, j):
        return self.orders[self.kinds[j]]

    def part(self, ref, slot, j, start, size):
        if not isinstance(start, int):
            start = pl.multiple_of(start, 8)
        return ref.at[slot, pl.ds(0, self.subs[j]), pl.ds(start, size), :]

    def held(self, j, s):
        if s < 0:
            return self.tile, j % TILES, BLOCK
        return self.red[s], j % self.slots, self.rows[s]

    def keep_start(self, j, s):
        return bit_of(self.order(j)[s]) * self.rows[s] if s < self.halvings else 0

    def give_start(self, j, s):
        return (1 - bit_of(self.order(j)[s])) * self.rows[s] if s < self.halvings else 0

    def scatter_copy(self, j, s):
        ref, slot, _rows = self.held(j, s - 1)
        into, into_slot, rows = self.held(j, s)
        return pltpu.make_async_remote_copy(
            src_ref=self.part(ref, slot, j, self.give_start(j, s), rows),
            dst_ref=self.part(into, into_slot, j, 0, rows),
            send_sem=self.send.at[s, into_slot],
            recv_sem=self.recv.at[s, into_slot],
            device_id=partner(self.order(j)[s]),
            device_id_type=MESH,
        )

    def owned(self, j, s, flip=False):
        start = 0
        for t in range(s + 1):
            bit = bit_of(self.order(j)[t])
            if flip and t == s:
                bit = 1 - bit
            start = start + bit * self.rows[t]
        return [
            target.at[
                pl.ds(pl.multiple_of(row + start, 8), self.rows[s]), pl.ds(col, count)
            ]
            for _block, _from, count, target, row, col in self.pieces[j]
        ]

    def final(self, j):
        ref, slot, rows = self.held(j, self.stages - 1)
        return [
            ref.at[slot, block, pl.ds(0, rows), pl.ds(from_col, count)]
            for block, from_col, count, _target, _row, _col in self.pieces[j]
        ]

    def gather_copies(self, j, s, arriving=False):
        last = s == self.halvings - 1
        sources = self.final(j) if last else self.owned(j, s)
        return [
            pltpu.make_async_remote_copy(
                src_ref=source,
                dst_ref=target,
                send_sem=self.gsend.at[j, s, p],
                recv_sem=self.grecv.at[j, s, p],
                device_id=partner(self.order(j)[s]),
                device_id_type=MESH,
            )
            for p, (source, target) in enumerate(zip(sources, self.owned(j, s, flip=arriving)))
        ]

    def local_copies(self, j):
        pairs = zip(self.final(j), self.owned(j, self.halvings - 1))
        return [
            pltpu.make_async_copy(source, target, self.local.at[j, p])
            for p, (source, target) in enumerate(pairs)
        ]

    def sent(self, j, event, s):
        size = self.rows[s] * self.subs[j] * TILE * 4e-6
        self.links.start((j, event), size, self.order(j)[s])
        self.due[j] = event

    def advance(self, us):
        self.links.forward(self.links.now + us)

    def run(self, j):
        event = self.due.pop(j)
        while (j, event) not in self.links.arrived:
            self.links.forward()
        self.links.forward(max(self.links.now, self.links.arrived.pop((j, event))))
        n = self.stages
        if event < n:
            s = event
            copy = self.scatter_copy(j, s)
            copy.wait_send()
            copy.wait_recv()
            self.add(j, s)
            if s > 0:
                self.give_credit(j, s - 1)
            if s < n - 1:
                self.start_scatter(j, s + 1)
            else:
                for copy in self.local_copies(j) + self.gather_copies(j, self.halvings - 1):
                    copy.start()
                self.sent(j, event + 1, self.halvings - 1)
        else:
            s = self.halvings - 1 - (event - n)
            for copy in self.gather_copies(j, s, True):
                copy.wait_recv()
            if s == self.halvings - 1:
                for copy in self.gather_copies(j, s):
                    copy.wait_send()
                for copy in self.local_copies(j):
                    copy.wait()
                self.give_credit(j, n - 1)
            if s > 0:
                for copy in self.gather_copies(j, s - 1):
                    copy.start()
                self.sent(j, event + 1, s - 1)
        self.done[j] = event
        self.advance(SERVICE)

    def add(self, j, s):
        ref, slot, _rows = self.held(j, s - 1)
        into, into_slot, rows = self.held(j, s)
        start = self.keep_start(j, s)
        step = min(48, rows)

        @pl.loop(0, rows // step)
        def _(i):
            for b in range(self.subs[j]):
                here = pl.ds(pl.multiple_of(start + i * step, 8), step)
                there = pl.ds(pl.multiple_of(i * step, 8), step)
                into[into_slot, b, there, :] += ref[slot, b, here, :]

    def give_credit(self, j, s):
        if j + self.slots < self.jobs:
            pl.semaphore_signal(
                self.credit.at[s, j % self.slots],
                inc=1,
                device_id=partner(self.order(j + self.slots)[s]),
                device_id_type=MESH,
            )

    def start_scatter(self, j, s):
        if j >= self.slots:
            self.reach(j - self.slots, s + 1)
            pl.semaphore_wait(self.credit.at[s, j % self.slots], 1)
        self.scatter_copy(j, s).start()
        self.sent(j, s, s)

    def reach(self, j, event):
        while self.done[j] < event:
            self.run(j)

    def acquire(self, j):
        if j >= TILES:
            self.reach(j - TILES, 0)
        return j % TILES

    def produced(self, j):
        self.start_scatter(j, 0)

    def tick(self, us=0.0):
        self.advance(us)
        while True:
            ready = {k: t for k, t in self.links.arrived.items() if t <= self.links.now}
            if not ready:
                break
            self.run(min(ready, key=ready.get)[0])

    def drain(self):
        while self.due:
            if not self.links.arrived:
                self.links.forward()
            self.run(min(self.links.arrived, key=self.links.arrived.get)[0])
        for j in range(self.jobs):
            for s in range(self.halvings - 1):
                for copy in self.gather_copies(j, s):
                    copy.wait_send()


class Refs(typing.NamedTuple):
    x: typing.Any
    cot: typing.Any
    lengths: typing.Any
    norm_gain: typing.Any
    norm_shift: typing.Any
    alpha: typing.Any
    delta: typing.Any
    beta: typing.Any
    eta: typing.Any
    omega_in: typing.Any
    b_output_in: typing.Any
    b_shrink_in: typing.Any
    b_value_in: typing.Any
    b_gates_in: typing.Any
    b_expand_in: typing.Any
    qk: typing.Any
    bias: typing.Any
    w_value: typing.Any
    w_gates: typing.Any
    w_output: typing.Any
    w_expand: typing.Any
    w_shrink: typing.Any
    out_hbm: typing.Any
    dx_hbm: typing.Any
    dw_value: typing.Any
    dw_gates: typing.Any
    dw_output: typing.Any
    dw_expand: typing.Any
    dw_shrink: typing.Any
    sums: typing.Any
    wa: typing.Any
    wb: typing.Any
    wg: typing.Any
    cot_v: typing.Any
    dx: typing.Any
    tables: typing.Any
    gains: typing.Any
    b_value: typing.Any
    b_gates: typing.Any
    b_expand: typing.Any
    normed: typing.Any
    vpre: typing.Any
    gate: typing.Any
    att: typing.Any
    hpre: typing.Any
    mid: typing.Any
    epre: typing.Any
    mpre: typing.Any
    dnorm: typing.Any
    probs: typing.Any
    square: typing.Any
    lh: typing.Any
    ll: typing.Any
    th: typing.Any
    tl: typing.Any
    s768: typing.Any
    s_value: typing.Any
    s_expand: typing.Any
    s_gates: typing.Any
    s_small: typing.Any
    ends: typing.Any
    starts: typing.Any
    e_recv: typing.Any
    f_recv: typing.Any
    wsem: typing.Any
    osem: typing.Any
    send: typing.Any
    recv: typing.Any
    send2: typing.Any
    recv2: typing.Any
    tile: typing.Any
    sems: typing.Any
    red: typing.Any


def kernel(batch, seq, *refs):
    n = len(Refs._fields) - 2
    r = Refs(*refs[:n], refs[n : n + 6], refs[n + 6 :])
    rows, width = r.x.shape
    seg_len = rows // SEG
    me_b, me = lax.axis_index("batch"), lax.axis_index("seq")
    nstate = 16
    hv = r.vpre.shape[1]
    ff = r.epre.shape[1]
    zd = r.qk.shape[1]
    group = r.probs.shape[1]
    groups = rows // group
    reset0 = width + zd
    cand0 = reset0 + hv
    gates = cand0 + width
    scale = 1.0 / math.sqrt(zd)

    sources = (r.w_value, r.w_gates, r.w_output, r.w_expand, r.w_shrink, r.w_output, r.w_value)
    places = (r.wa, r.wg, r.wb, r.wa, r.wb, r.wb, r.wa)
    weights = [
        pltpu.make_async_copy(a, b, r.wsem.at[i]) for i, (a, b) in enumerate(zip(sources, places))
    ]
    cot_copy = pltpu.make_async_copy(r.cot, r.cot_v, r.wsem.at[len(weights)])
    for copy in weights[:3] + [cot_copy]:
        copy.start()

    gate_cols = [i * TILE for i in range(width // TILE)]
    gate_cols += [reset0 + i * TILE for i in range((hv + width) // TILE)]

    def tall_job(ref, i):
        return [(b, 0, TILE, ref, b * BLOCK, i * TILE) for b in range(2)]

    def wide_job(ref, cols):
        return [(b, 0, TILE, ref, 0, cols[b]) for b in range(2)]

    pieces = [tall_job(r.dw_shrink, i) for i in range(width // TILE)]
    pieces += [wide_job(r.dw_expand, (i, i + TILE)) for i in range(0, ff, 2 * TILE)]
    pieces += [tall_job(r.dw_output, i) for i in range(width // TILE)]
    pieces += [wide_job(r.dw_value, (i, i + TILE)) for i in range(0, hv, 2 * TILE)]
    pieces += [wide_job(r.dw_gates, gate_cols[i : i + 2]) for i in range(0, len(gate_cols), 2)]
    pieces.append([(0, 0, zd, r.dw_gates, 0, width), (0, zd, TILE - zd, r.sums, 0, 0)])
    kinds = [KINDS[j % len(KINDS)] for j in range(len(pieces))]
    comm = Reducer(
        stage_orders(batch, seq), slot_count(seq), kinds, pieces, r.tile, r.red, r.sems
    )
    _core, chips, _line = bits_of(batch, seq)

    barrier = pltpu.get_barrier_semaphore()

    def greet(k, _):
        pl.semaphore_signal(
            barrier, inc=1, device_id=(me_b, lax.rem(me + k, seq)), device_id_type=MESH
        )
        return 0

    lax.fori_loop(1, seq, greet, 0)
    for bit in chips:
        pl.semaphore_signal(barrier, inc=1, device_id=partner(bit), device_id_type=MESH)

    alpha, damping = sigmoid(r.alpha[...]), sigmoid(r.delta[...])
    rate = alpha * damping
    series = jnp.full_like(rate, 1.0 / 7.0)
    for n in range(6, 0, -1):
        series = series * rate + 1.0 / n
    log_decay = -rate * series
    for i, value in enumerate(
        (
            1.0 - rate,
            alpha * r.beta[...] * r.eta[...],
            jnp.exp(seg_len * log_decay),
            jnp.exp(rows * log_decay),
        )
    ):
        r.tables[i] = value
    decay, coef, dec_seg, dec_all = (r.tables.at[i] for i in range(4))

    def unfold(source, target, row=0):
        for d in range(source.shape[0]):
            target[row : row + 1, d * LANES : (d + 1) * LANES] = source[d : d + 1, :]

    unfold(r.b_value_in, r.b_value)
    unfold(r.b_gates_in, r.b_gates)
    unfold(r.b_expand_in, r.b_expand)
    for i in range(2):
        r.gains[2 * i : 2 * i + 1, :] = r.norm_gain[i : i + 1, :]
        r.gains[2 * i + 1 : 2 * i + 2, :] = r.norm_shift[i : i + 1, :]
    for i, source in enumerate((r.omega_in, r.b_output_in, r.b_shrink_in)):
        unfold(source, r.gains, 4 + i)
    gain0, shift0, gain1, shift1, omega, b_output, b_shrink = (
        r.gains[i : i + 1, :] for i in range(7)
    )

    first_end = r.lengths[0, 0]
    second_end = first_end + r.lengths[0, 1]

    def keep(group_id):
        starts = (group_id == 0) | (group_id == first_end) | (group_id == second_end)
        return jnp.where(starts, 0.0, 1.0)

    def keep_block(k):
        value = keep(k * groups)
        for g in range(1, groups):
            value = value * keep(k * groups + g)
        return value

    keep_seg = [
        keep(me * groups + k * groups // SEG) if k % (SEG // groups) == 0 else 1.0
        for k in range(SEG)
    ]

    def tiles(count, body, us, parts=1):
        for p in range(parts):
            pl.loop(count * p // parts, count * (p + 1) // parts)(body)
            comm.tick(us / parts)

    def zero_small(i):
        r.s768[i : i + 1, :] = jnp.zeros((1, width), f32)

    for i in range(8):
        zero_small(i)

    def add768(i, value, cols=slice(None)):
        r.s768[i : i + 1, cols] += jnp.sum(value, axis=0, keepdims=True)

    RC = 32

    def norm_stats(value):
        centre = value - jnp.mean(value, axis=-1, keepdims=True)
        inv = lax.rsqrt(jnp.mean(centre * centre, axis=-1, keepdims=True) + 1e-05)
        return centre * inv, inv

    def norm_back(grad, n, inv):
        return inv * (
            grad
            - jnp.mean(grad, axis=-1, keepdims=True)
            - n * jnp.mean(grad * n, axis=-1, keepdims=True)
        )

    @pl.loop(0, rows // RC)
    def _(i):
        part = at(i, RC)
        n, _inv = norm_stats(r.x[part, :])
        value = n * gain0 + shift0
        row_set(r.normed, part, value)
        r.lh[part, :width], r.ll[part, :width] = split(value)

    def seg_rows(t):
        return pl.ds(t, SEG, stride=seg_len)

    def rows_of(ref, count, cols):
        return [jnp.broadcast_to(ref[n : n + 1, cols], (SEG, LANES)) for n in count]

    def end_states(source, reverse, target):
        @pl.loop(0, width // LANES)
        def _(d):
            cols = at(d, LANES)
            dec = rows_of(decay, range(nstate), cols)

            def turn(t, state):
                at_t = seg_len - 1 - t if reverse else t
                value = source[d, seg_rows(at_t), :]
                return tuple(a * s + value for a, s in zip(dec, state))

            zero = jnp.zeros((SEG, LANES), f32)
            state = lax.fori_loop(0, seg_len, turn, (zero,) * nstate, unroll=8)
            for n in range(nstate):
                target[d, n * SEG : (n + 1) * SEG, :] = state[n]

    def seg_of(k):
        return pl.ds(k, nstate, stride=SEG)

    def exchange(buffer, send_sem, recv_sem):
        def copy_to(k):
            peer = lax.rem(me + k, seq)
            return pltpu.make_async_remote_copy(
                src_ref=buffer.at[me],
                dst_ref=buffer.at[me],
                send_sem=send_sem.at[k],
                recv_sem=recv_sem.at[me],
                device_id=(me_b, peer),
                device_id_type=MESH,
            )

        def copy_from(k):
            peer = lax.rem(me + k, seq)
            return pltpu.make_async_remote_copy(
                src_ref=buffer.at[me],
                dst_ref=buffer.at[peer],
                send_sem=send_sem.at[k],
                recv_sem=recv_sem.at[peer],
                device_id=(me_b, peer),
                device_id_type=MESH,
            )

        def start():
            def one(k, _):
                copy_to(k).start()
                return 0

            lax.fori_loop(1, seq, one, 0)

        def wait():
            def one(k, _):
                copy_to(k).wait_send()
                copy_from(k).wait_recv()
                return 0

            lax.fori_loop(1, seq, one, 0)

        return start, wait

    end_states(r.normed, False, r.ends)
    total = jnp.zeros((nstate, width), f32)
    for k in range(SEG):
        total = keep_seg[k] * total * dec_seg[...] + row_get(r.ends, seg_of(k))
    r.e_recv[me] = total
    pl.semaphore_wait(barrier, seq - 1 + len(chips))
    start_e, wait_e = exchange(r.e_recv, r.send, r.recv)
    start_e()

    weights[0].wait()

    @pl.loop(0, hv // TILE)
    def _(i):
        c = at(i, TILE)
        w = r.wa[:, c]
        r.vpre[:, c] = (
            dot(r.lh[:, :width], w) + dot(r.ll[:, :width], w) + r.b_value[:, c]
        )

    weights[3].start()

    wait_e()

    def carry_step(k, carried):
        new = dec_all[...] * (keep_block(k) * carried) + r.e_recv[k]
        return jnp.where(k < me, new, carried)

    state = lax.fori_loop(0, seq, carry_step, jnp.zeros((nstate, width), f32))
    for k in range(SEG):
        state = keep_seg[k] * state
        row_set(r.starts, seg_of(k), state)
        if k < SEG - 1:
            state = dec_seg[...] * state + row_get(r.ends, seg_of(k))

    @pl.loop(0, width // LANES)
    def _(d):
        cols = at(d, LANES)
        dec = rows_of(decay, range(nstate), cols)
        mix = rows_of(coef, range(nstate), cols)

        def turn(t, state):
            value = r.normed[d, seg_rows(t), :]
            state = tuple(a * s + value for a, s in zip(dec, state))
            terms = [m * s for m, s in zip(mix, state)]
            while len(terms) > 1:
                terms = [a + b for a, b in zip(terms[::2], terms[1::2])]
            r.mpre[d, seg_rows(t), :] = terms[0]
            return state

        first = tuple(r.starts[d, n * SEG : (n + 1) * SEG, :] for n in range(nstate))
        lax.fori_loop(0, seg_len, turn, first, unroll=4)

    @pl.loop(0, rows // RC)
    def _(i):
        part = at(i, RC)
        value = row_get(r.mpre, part) + omega * row_get(r.normed, part)
        row_set(r.mpre, part, value)
        r.lh[part, :width], r.ll[part, :width] = split(silu(value))

    weights[1].wait()

    def gate_tile(c):
        w = r.wg[:, c]
        r.gate[:, c] = (
            dot(r.lh[:, :width], w) + dot(r.ll[:, :width], w) + r.b_gates[:, c]
        )

    @pl.loop(0, width // TILE)
    def _(i):
        gate_tile(at(i, TILE))

    gate_tile(pl.ds(width, zd))

    @pl.loop(0, (hv + width) // TILE)
    def _(i):
        gate_tile(off(reset0, i, TILE))

    lag = lax.broadcasted_iota(jnp.int32, (group, group), 0) - lax.broadcasted_iota(
        jnp.int32, (group, group), 1
    )
    row_id = lax.broadcasted_iota(jnp.int32, (group, group), 0)
    causal = lag >= 0
    table = jnp.broadcast_to(r.bias[...], (group, group))
    for b in range(group.bit_length() - 1):
        moved = pltpu.roll(table, 1 << b, 1)
        table = jnp.where((row_id & (1 << b)) != 0, moved, table)
    q_gain, k_gain, q_shift = (r.qk[i : i + 1, :] for i in range(3))
    r.square[...] = table.T

    @pl.loop(0, groups)
    def _(g):
        part = at(g, group)
        shared = silu(r.gate[part, width:reset0])
        q = split(shared * q_gain + q_shift)
        k = split(shared * k_gain)
        scores = dot3(q, k, NT) * scale + r.square[...]
        scores = jnp.where(causal, scores, -1e30)
        p = jnp.exp(scores - jnp.max(scores, axis=-1, keepdims=True))
        p = p / jnp.sum(p, axis=-1, keepdims=True)
        r.probs[part, :] = p
        p = split(p)

        @pl.loop(0, hv // TILE)
        def _(i):
            c = at(i, TILE)
            v = split(silu(r.vpre[part, c]))
            attended = dot3(p, v)
            r.att[part, c] = attended
            gated = attended * silu(r.gate[part, off(reset0, i, TILE)])
            r.lh[part, c], r.ll[part, c] = split(gated)

    weights[2].wait()

    @pl.loop(0, width // TILE)
    def _(i):
        c = at(i, TILE)
        w = r.wb[:, c]
        value = (
            dot(r.lh[...], w)
            + dot(r.ll[...], w)
            + (r.gate[:, off(cand0, i, TILE)] + r.gains[5:6, c])
        )
        r.hpre[:, c] = value
        x = r.x[:, c]
        r.mid[:, c] = x + sigmoid(r.gate[:, c]) * (silu(value) - x)

    weights[4].start()

    @pl.loop(0, rows // RC)
    def _(i):
        part = at(i, RC)
        n, _inv = norm_stats(r.mid[part, :])
        r.lh[part, :width], r.ll[part, :width] = split(n * gain1 + shift1)

    weights[3].wait()

    @pl.loop(0, ff // TILE)
    def _(i):
        c = at(i, TILE)
        w = r.wa[:, c]
        r.epre[:, c] = (
            dot(r.lh[:, :width], w) + dot(r.ll[:, :width], w) + r.b_expand[:, c]
        )

    comm.advance(50.0)
    cot_copy.wait()

    def transposed(source, count, first=0):
        @pl.loop(0, count // LANES)
        def _(i):
            here = off(first, i, LANES)
            r.th[here, :], r.tl[here, :] = split(source(i, at(i, LANES)).T)

    def products(j, pairs):
        slot = comm.acquire(j)
        for b, (first, grad) in enumerate(pairs):
            g = split(grad)
            cols = grad.shape[1]

            @pl.loop(0, BLOCK // TILE)
            def _(k):
                a = off(first, k, TILE)
                value = dot3((r.th[a, :], r.tl[a, :]), g)
                if cols == TILE:
                    r.tile[slot, b, at(k, TILE), :] = value
                else:
                    r.tile[slot, b, at(k, TILE), :cols] = value

        comm.advance(1.0 * len(pairs))
        return slot

    def tall(j, grad):
        products(j, [(0, grad), (BLOCK, grad)])
        comm.produced(j)
        comm.tick()

    def wide(j, first, left, right):
        products(j, [(first, left), (first, right)])
        comm.produced(j)
        comm.tick()

    def cols_of(ref, i, start=0):
        return ref[:, start + i * TILE : start + (i + 1) * TILE]

    transposed(lambda i, c: silu(r.epre[:, c]), ff)
    comm.advance(2.0)
    for i in range(width // TILE):
        tall(i, cols_of(r.cot_v, i))

    def inner_halves(i):
        c = at(i, TILE)
        r.lh[:, c], r.ll[:, c] = split(silu(r.epre[:, c]))

    tiles(ff // TILE, inner_halves, 1.2)
    weights[4].wait()

    def out_tile(i):
        c = at(i, TILE)
        w = r.wb[:, c]
        r.dx[:, c] = r.mid[:, c] + (dot(r.lh[...], w) + dot(r.ll[...], w) + r.gains[6:7, c])

    tiles(width // TILE, out_tile, 3.0)
    out_copy = pltpu.make_async_copy(r.dx, r.out_hbm, r.osem.at[0])
    out_copy.start()

    def cot_halves(i):
        part = at(i, RC)
        value = r.cot_v[part, :]
        add768(6, value)
        r.lh[part, :width], r.ll[part, :width] = split(value)

    tiles(rows // RC, cot_halves, 1.0)

    def inner_back(i):
        c = at(i, TILE)
        w = r.wb[c, :]
        value = (dot(r.lh[:, :width], w, NT) + dot(r.ll[:, :width], w, NT)) * dsilu(
            r.epre[:, c]
        )
        r.epre[:, c] = value
        r.s_expand[:, c] = jnp.sum(value, axis=0, keepdims=True)

    tiles(ff // TILE, inner_back, 3.2)
    weights[5].start()

    def expand_halves(i):
        c = at(i, TILE)
        r.lh[:, c], r.ll[:, c] = split(r.epre[:, c])

    tiles(ff // TILE, expand_halves, 0.8)

    @pl.loop(0, rows // RC)
    def _(i):
        part = at(i, RC)
        n, _inv = norm_stats(r.mid[part, :])
        row_set(r.dnorm, part, n * gain1 + shift1)

    transposed(lambda i, c: r.dnorm[i], width)
    comm.tick(2.0)
    for i in range(ff // (2 * TILE)):
        wide(3 + i, 0, cols_of(r.epre, 2 * i), cols_of(r.epre, 2 * i + 1))

    out_copy.wait()

    @pl.loop(0, width // TILE)
    def _(i):
        c = at(i, TILE)
        w = r.wa[c, :]
        r.dx[:, c] = dot(r.lh[...], w, NT) + dot(r.ll[...], w, NT)

    weights[6].start()
    comm.tick(3.0)

    def middle_back(i):
        part = at(i, RC)
        grad = r.dx[part, :]
        n, inv = norm_stats(r.mid[part, :])
        add768(2, grad * n)
        add768(3, grad)
        dmid = r.cot_v[part, :] + norm_back(grad * gain1, n, inv)
        update = sigmoid(r.gate[part, :width])
        pre = r.hpre[part, :]
        x = r.x[part, :]
        dhpre = dmid * update * dsilu(pre)
        r.dx[part, :] = dmid * (1.0 - update)
        dupdate = dmid * (silu(pre) - x) * (update * (1.0 - update))
        r.gate[part, :width] = dupdate
        r.gate[part, cand0:] = dhpre
        r.lh[part, :width], r.ll[part, :width] = split(dhpre)
        r.s_gates[:, :width] = (
            jnp.where(i == 0, 0.0, r.s_gates[:, :width])
            + jnp.sum(dupdate, axis=0, keepdims=True)
        )
        add768(5, dhpre)

    tiles(rows // RC, middle_back, 5.0, 2)

    transposed(lambda i, c: r.att[:, c] * silu(r.gate[:, off(reset0, i, LANES)]), hv)
    weights[5].wait()
    comm.tick(3.0)
    for i in range(width // TILE):
        tall(6 + i, cols_of(r.gate, i, cand0))

    def attended_back(i):
        c = at(i, TILE)
        w = r.wb[c, :]
        gated = dot(r.lh[:, :width], w, NT) + dot(r.ll[:, :width], w, NT)
        here = off(reset0, i, TILE)
        pre = r.gate[:, here]
        dreset = gated * r.att[:, c] * dsilu(pre)
        r.att[:, c] = gated * silu(pre)
        r.gate[:, here] = dreset
        r.s_gates[:, here] = jnp.sum(dreset, axis=0, keepdims=True)

    tiles(hv // TILE, attended_back, 3.5)

    r.s_small[...] = jnp.zeros_like(r.s_small)
    r.square[...] = jnp.zeros((group, group), f32)

    def attention_back(g):
        part = at(g, group)
        p = r.probs[part, :]
        p_t = split(p.T)

        def value_tile(i, dp):
            c = at(i, TILE)
            pre = r.vpre[part, c]
            d_att = split(r.att[part, c])
            r.vpre[part, c] = dot3(p_t, d_att) * dsilu(pre)
            return dp + dot3(d_att, split(silu(pre)), NT)

        dp = lax.fori_loop(0, hv // TILE, value_tile, jnp.zeros((group, group), f32))
        ds = p * (dp - jnp.sum(dp * p, axis=-1, keepdims=True))
        r.square[...] += ds
        ds = ds * scale
        pre = r.gate[part, width:reset0]
        shared = silu(pre)
        dq = dot3(split(ds), split(shared * k_gain))
        dk = dot3(split(ds.T), split(shared * q_gain + q_shift))
        for n, value in enumerate((dq * shared, dk * shared, dq)):
            r.s_small[n : n + 1, :] += jnp.sum(value, axis=0, keepdims=True)
        r.gate[part, width:reset0] = (dq * q_gain + dk * k_gain) * dsilu(pre)

    tiles(groups, attention_back, 8.4, 4)
    diagonals = r.square[...].T
    for b in range(group.bit_length() - 1):
        moved = pltpu.roll(diagonals, group - (1 << b), 1)
        diagonals = jnp.where((row_id & (1 << b)) != 0, moved, diagonals)
    r.s_small[3:4, :] = jnp.sum(diagonals, axis=0, keepdims=True)
    r.s_gates[:, width:reset0] = jnp.sum(r.gate[:, width:reset0], axis=0, keepdims=True)
    r.s_gates[:, cand0:] = r.s768[5:6, :]

    comm.tick(0.5)
    weights[6].wait()

    @pl.loop(0, hv // TILE)
    def _(i):
        c = at(i, TILE)
        value = r.vpre[:, c]
        r.s_value[:, c] = jnp.sum(value, axis=0, keepdims=True)
        r.lh[:, c], r.ll[:, c] = split(value)

    @pl.loop(0, width // TILE)
    def _(i):
        c = at(i, TILE)
        w = r.wa[c, :]
        col_set(r.dnorm, i, dot(r.lh[...], w, NT) + dot(r.ll[...], w, NT))

    comm.tick(4.2)
    transposed(lambda i, c: r.normed[i], width, width)
    transposed(lambda i, c: silu(r.mpre[i]), width)
    comm.tick(2.5)

    for i in range(hv // (2 * TILE)):
        wide(9 + i, width, cols_of(r.vpre, 2 * i), cols_of(r.vpre, 2 * i + 1))
    for i in range(len(gate_cols) // 2):
        left, right = gate_cols[2 * i : 2 * i + 2]
        wide(12 + i, 0, cols_of(r.gate, 0, left), cols_of(r.gate, 0, right))

    def gate_section(start, size, first, last):
        @pl.loop(0, size // LANES)
        def _(i):
            c = at(i, LANES)
            r.lh[:, c], r.ll[:, c] = split(r.gate[:, off(start, i, LANES)])

        @pl.loop(0, width // TILE)
        def _(i):
            c = at(i, TILE)
            w = r.wg[c, start : start + size]
            value = dot(r.lh[:, :size], w, NT) + dot(r.ll[:, :size], w, NT)
            if not first:
                value += r.att[:, c]
            if last:
                value = value * dsilu(col_get(r.mpre, i))
                col_set(r.mpre, i, value)
                add768(4, value * col_get(r.normed, i), c)
                col_set(r.dnorm, i, col_get(r.dnorm, i) + r.gains[4:5, c] * value)
            else:
                r.att[:, c] = value

        comm.tick(size * 8.0 / gates)

    gate_section(0, reset0, True, False)
    gate_section(reset0, hv, False, False)
    gate_section(cand0, width, False, True)

    end_states(r.mpre, True, r.ends)
    adj = jnp.zeros((nstate, width), f32)
    for k in reversed(range(SEG)):
        if k < SEG - 1:
            adj = dec_seg[...] * (keep_seg[k + 1] * adj)
        adj = adj + row_get(r.ends, seg_of(k))
    r.f_recv[me] = adj
    start_f, wait_f = exchange(r.f_recv, r.send2, r.recv2)
    start_f()

    comm.tick(4.0)
    wait_f()
    comm.tick(7.0)

    def adj_step(j, carried):
        k = seq - 1 - j
        new = keep(k * groups) * r.f_recv[k] + dec_all[...] * (keep_block(k) * carried)
        return jnp.where(k > me, new, carried)

    adj = lax.fori_loop(0, seq, adj_step, jnp.zeros((nstate, width), f32))
    for k in reversed(range(SEG)):
        fresh = row_get(r.ends, seg_of(k))
        row_set(r.ends, seg_of(k), adj)
        if k > 0:
            adj = keep_seg[k] * (dec_seg[...] * adj + fresh)

    half = nstate // 2
    for h in range(2):
        states = range(h * half, (h + 1) * half)

        def average_back(d):
            cols = at(d, LANES)
            dec = rows_of(decay, states, cols)
            mix = rows_of(coef, states, cols)

            def ahead(t, state):
                value = r.normed[d, seg_rows(t), :]
                for n in range(half):
                    r.epre[at(t, SEG), n * LANES : (n + 1) * LANES] = state[n]
                return tuple(a * s + value for a, s in zip(dec, state))

            first = tuple(r.starts[d, n * SEG : (n + 1) * SEG, :] for n in states)
            lax.fori_loop(0, seg_len, ahead, first, unroll=4)

            def back(j, carried):
                t = seg_len - 1 - j
                adj, p_sum, q_sum = carried
                grad = r.mpre[d, seg_rows(t), :]
                value = r.normed[d, seg_rows(t), :]
                adj = tuple(a * s + grad for a, s in zip(dec, adj))
                p_sum = tuple(p + a * value for p, a in zip(p_sum, adj))
                q_sum = tuple(
                    q + a * r.epre[at(t, SEG), n * LANES : (n + 1) * LANES]
                    for n, (q, a) in enumerate(zip(q_sum, adj))
                )
                terms = [m * a for m, a in zip(mix, adj)]
                while len(terms) > 1:
                    terms = [a + b for a, b in zip(terms[::2], terms[1::2])]
                r.dnorm[d, seg_rows(t), :] += terms[0]
                return adj, p_sum, q_sum

            zero = (jnp.zeros((SEG, LANES), f32),) * half
            last = tuple(r.ends[d, n * SEG : (n + 1) * SEG, :] for n in states)
            _adj, p_sum, q_sum = lax.fori_loop(0, seg_len, back, (last, zero, zero), unroll=4)
            for n in range(half):
                row = 8 + h * half + n
                r.s768[row : row + 1, cols] = jnp.sum(p_sum[n], axis=0, keepdims=True)
                row = row + nstate
                r.s768[row : row + 1, cols] = jnp.sum(q_sum[n], axis=0, keepdims=True)

        tiles(width // LANES, average_back, 12.0, 6)

    def first_back(i):
        part = at(i, RC)
        grad = row_get(r.dnorm, part)
        n, inv = norm_stats(r.x[part, :])
        add768(0, grad * n)
        add768(1, grad)
        r.dx[part, :] += norm_back(grad * gain0, n, inv)

    tiles(rows // RC, first_back, 3.0)
    dx_copy = pltpu.make_async_copy(r.dx, r.dx_hbm, r.osem.at[1])
    dx_copy.start()

    slot = products(comm.jobs - 1, [(0, r.gate[:, width:reset0])])
    r.tile[slot, 0, :, zd:] = jnp.zeros((BLOCK, TILE - zd), f32)
    place = 0

    def put(value):
        nonlocal place
        count = value.shape[0]
        r.tile[slot, 0, place : place + count, zd:] = value
        place += count

    for d in range(width // LANES):
        put(r.s768[:, d * LANES : (d + 1) * LANES])
    put(r.s_small[...])
    for ref in (r.s_value, r.s_expand, r.s_gates):
        for d in range(ref.shape[1] // LANES):
            put(ref[:, d * LANES : (d + 1) * LANES])
    comm.produced(comm.jobs - 1)
    comm.drain()
    dx_copy.wait()


def finish(sums, alpha, delta, beta, eta, *outs):
    gain, shift, d_alpha, d_delta, d_beta, d_eta, omega, b_output, b_shrink = outs[:9]
    qk, bias, b_value, b_expand, b_gates = outs[9:]
    nstate, width = alpha.shape
    tall_rows = 8 + 2 * nstate
    for d in range(width // LANES):
        cols = slice(d * LANES, (d + 1) * LANES)
        row = d * tall_rows
        for n in range(2):
            gain[n : n + 1, cols] = sums[row + 2 * n : row + 2 * n + 1, :]
            shift[n : n + 1, cols] = sums[row + 2 * n + 1 : row + 2 * n + 2, :]
        for n, target in enumerate((omega, b_output, b_shrink)):
            target[d : d + 1, :] = sums[row + 4 + n : row + 5 + n, :]
        p_sum = sums[row + 8 : row + 8 + nstate, :]
        q_sum = sums[row + 8 + nstate : row + 8 + 2 * nstate, :]
        rate, damping = sigmoid(alpha[:, cols]), sigmoid(delta[:, cols])
        d_inflow = eta[:, cols] * p_sum
        d_eta[:, cols] = rate * beta[:, cols] * p_sum
        d_decay = eta[:, cols] * (rate * beta[:, cols]) * q_sum
        d_rate = d_inflow * beta[:, cols] - d_decay * damping
        d_alpha[:, cols] = d_rate * rate * (1.0 - rate)
        d_delta[:, cols] = -d_decay * rate * damping * (1.0 - damping)
        d_beta[:, cols] = d_inflow * rate
    place = width // LANES * tall_rows
    qk[...] = sums[place : place + 3, :]
    bias[...] = sums[place + 3 : place + 4, :]
    place += 8
    for target in (b_value, b_expand, b_gates):
        target[...] = sums[place : place + target.shape[0], :]
        place += target.shape[0]


def layer(operands, batch, seq):
    rows, width = operands[0].shape
    w_value, w_gates, w_output, w_expand, w_shrink = operands[-5:]
    hv, gates, ff = w_value.shape[1], w_gates.shape[1], w_expand.shape[1]
    zd, group, nstate = operands[15].shape[1], operands[16].shape[1], operands[5].shape[0]
    vmem = pl.BlockSpec(memory_space=pltpu.VMEM)
    smem = pl.BlockSpec(memory_space=pltpu.SMEM)
    hbm = pl.BlockSpec(memory_space=pl.ANY)
    stages, slots = len(stage_orders(batch, seq)[0]), slot_count(seq)

    def shape(*dims, kind=f32):
        return jax.ShapeDtypeStruct(dims, kind)

    return pl.pallas_call(
        functools.partial(kernel, batch, seq),
        out_shape=(
            shape(rows, width),
            shape(rows, width),
            shape(width, hv),
            shape(width, gates),
            shape(hv, width),
            shape(width, ff),
            shape(ff, width),
            shape(BLOCK, TILE - zd),
        ),
        in_specs=[vmem, hbm, smem] + [vmem] * 14 + [hbm] * 5,
        out_specs=(hbm,) * 8,
        scratch_shapes=[
            pltpu.VMEM(w_value.shape, bf16),
            pltpu.VMEM(w_output.shape, bf16),
            pltpu.VMEM(w_gates.shape, bf16),
            pltpu.VMEM((rows, width), f32),
            pltpu.VMEM((rows, width), f32),
            pltpu.VMEM((4, nstate, width), f32),
            pltpu.VMEM((8, width), f32),
            pltpu.VMEM((1, hv), f32),
            pltpu.VMEM((1, gates), f32),
            pltpu.VMEM((1, ff), f32),
            pltpu.VMEM((width // LANES, rows, LANES), f32),
            pltpu.VMEM((rows, hv), f32),
            pltpu.VMEM((rows, gates), f32),
            pltpu.VMEM((rows, hv), f32),
            pltpu.VMEM((rows, width), f32),
            pltpu.VMEM((rows, width), f32),
            pltpu.VMEM((rows, ff), f32),
            pltpu.VMEM((width // LANES, rows, LANES), f32),
            pltpu.VMEM((width // LANES, rows, LANES), f32),
            pltpu.VMEM((rows, group), f32),
            pltpu.VMEM((group, group), f32),
            pltpu.VMEM((rows, max(hv, ff)), bf16),
            pltpu.VMEM((rows, max(hv, ff)), bf16),
            pltpu.VMEM((max(hv, ff), rows), bf16),
            pltpu.VMEM((max(hv, ff), rows), bf16),
            pltpu.VMEM((8 + 2 * nstate, width), f32),
            pltpu.VMEM((1, hv), f32),
            pltpu.VMEM((1, ff), f32),
            pltpu.VMEM((1, gates), f32),
            pltpu.VMEM((8, zd), f32),
            pltpu.VMEM((width // LANES, nstate * SEG, LANES), f32),
            pltpu.VMEM((width // LANES, nstate * SEG, LANES), f32),
            pltpu.VMEM((seq, nstate, width), f32),
            pltpu.VMEM((seq, nstate, width), f32),
            pltpu.SemaphoreType.DMA((8,)),
            pltpu.SemaphoreType.DMA((2,)),
            pltpu.SemaphoreType.DMA((seq,)),
            pltpu.SemaphoreType.DMA((seq,)),
            pltpu.SemaphoreType.DMA((seq,)),
            pltpu.SemaphoreType.DMA((seq,)),
            pltpu.VMEM((TILES, 2, BLOCK, TILE), f32),
            pltpu.SemaphoreType.DMA((stages, slots)),
            pltpu.SemaphoreType.DMA((stages, slots)),
            pltpu.SemaphoreType.REGULAR((stages, slots)),
            pltpu.SemaphoreType.DMA((JOBS, 2)),
            pltpu.SemaphoreType.DMA((JOBS, HALVINGS, 2)),
            pltpu.SemaphoreType.DMA((JOBS, HALVINGS, 2)),
        ]
        + [pltpu.VMEM((slots, 2, count, TILE), f32) for count in stage_rows(stages)],
        compiler_params=pltpu.CompilerParams(
            collective_id=0, has_side_effects=True, vmem_limit_bytes=63 << 20
        ),
        cost_estimate=pl.CostEstimate(
            flops=52_000_000_000, bytes_accessed=60_000_000, transcendentals=20_000_000
        ),
    )(*operands)


def shards(
    batch,
    seq,
    tokens,
    lengths,
    cotangent,
    norm_gain,
    norm_shift,
    alpha_logit,
    delta_logit,
    ema_beta,
    ema_eta,
    ema_omega,
    w_value,
    b_value,
    w_gates,
    b_gates,
    query_key,
    position_bias,
    w_output,
    b_output,
    w_expand,
    b_expand,
    w_shrink,
    b_shrink,
):
    def lines(vector):
        return vector.reshape(-1, LANES)

    averages = (alpha_logit.T, delta_logit.T, ema_beta.T, ema_eta.T)
    operands = (tokens[0], cotangent[0], lengths, norm_gain.T, norm_shift.T) + averages
    operands += (lines(ema_omega), lines(b_output), lines(b_shrink))
    operands += (lines(b_value), lines(b_gates), lines(b_expand))
    operands += (query_key.T, position_bias[None])
    operands += (w_value, w_gates, w_output, w_expand, w_shrink)
    output, grad_tokens, dw_value, dw_gates, dw_output, dw_expand, dw_shrink, sums = layer(
        operands, batch, seq
    )
    like = (norm_gain.T, norm_shift.T) + averages
    like += (lines(ema_omega), lines(b_output), lines(b_shrink), query_key.T)
    like += (position_bias[None], lines(b_value), lines(b_expand), lines(b_gates))
    small = pl.pallas_call(
        finish, out_shape=tuple(jax.ShapeDtypeStruct(a.shape, f32) for a in like)
    )(sums, *averages)
    gain, shift, d_alpha, d_delta, d_beta, d_eta, d_omega, d_output, d_shrink = small[:9]
    d_qk, d_bias, d_value, d_expand, d_gates = small[9:]
    return (
        output[None],
        grad_tokens[None],
        gain.T,
        shift.T,
        d_alpha.T,
        d_delta.T,
        d_beta.T,
        d_eta.T,
        d_omega.reshape(-1),
        dw_value,
        d_value.reshape(-1),
        dw_gates,
        d_gates.reshape(-1),
        d_qk.T,
        d_bias[0],
        dw_output,
        d_output.reshape(-1),
        dw_expand,
        d_expand.reshape(-1),
        dw_shrink,
        d_shrink.reshape(-1),
    )


def solution(mesh):
    token_spec = P("batch", "seq", None)
    return jax.shard_map(
        functools.partial(shards, mesh.shape["batch"], mesh.shape["seq"]),
        mesh=mesh,
        in_specs=(token_spec, P("batch", None), token_spec) + (P(),) * 19,
        out_specs=(token_spec, token_spec) + (P(),) * 19,
        check_vma=False,
    )
```

```python
import functools
import math
import typing

import jax
import jax.numpy as jnp
from jax import lax
from jax.experimental import pallas as pl
from jax.experimental.pallas import tpu as pltpu
from jax.sharding import PartitionSpec as P

f32 = jnp.float32
bf16 = jnp.bfloat16
MESH = pl.DeviceIdType.MESH

SEG = 8
LANES = 128
TILE = 256

NN = (((1,), (0,)), ((), ()))
NT = (((1,), (1,)), ((), ()))


def split(value):
    high = value.astype(bf16)
    return high, (value - high.astype(f32)).astype(bf16)


def dot(a, b, dims=NN):
    return lax.dot_general(a, b, dims, preferred_element_type=f32)


def dot3(a, b, dims=NN):
    a_high, a_low = a
    b_high, b_low = b
    return dot(a_high, b_high, dims) + (dot(a_high, b_low, dims) + dot(a_low, b_high, dims))


def sigmoid(value):
    return 1.0 / (1.0 + jnp.exp(-value))


def silu(value):
    return value * sigmoid(value)


def dsilu(value):
    s = sigmoid(value)
    return s * (1.0 + value * (1.0 - s))


def row_get(ref, part):
    return jnp.concatenate([ref[d, part, :] for d in range(ref.shape[0])], axis=-1)


def row_set(ref, part, value):
    for d in range(ref.shape[0]):
        ref[d, part, :] = value[:, d * LANES : (d + 1) * LANES]


def col_get(ref, i, size=TILE):
    n = size // LANES
    return jnp.concatenate([ref[i * n + k] for k in range(n)], axis=-1)


def col_set(ref, i, value):
    n = value.shape[1] // LANES
    for k in range(n):
        ref[i * n + k] = value[:, k * LANES : (k + 1) * LANES]


def at(i, size):
    return pl.ds(pl.multiple_of(i * size, size), size)


def off(start, i, size):
    return pl.ds(pl.multiple_of(start + i * size, LANES), size)


def bit_of(bit):
    name, step = bit
    return lax.rem(lax.div(lax.axis_index(name), step), 2)


def partner(bit):
    name, step = bit
    where = {"batch": lax.axis_index("batch"), "seq": lax.axis_index("seq")}
    where[name] = where[name] + step * (1 - 2 * bit_of(bit))
    return (where["batch"], where["seq"])


HALVINGS = 5
BLOCK = 768
TILES = 2
SERVICE = 0.5
JOBS = 19
KINDS = ((0, 3), (0, 1), (1, 0), (1, 2), (0, 3), (1, 2), (0, 1), (0, 0), (1, 2), (0, 1), (1, 0), (0, 1), (1, 3), (0, 1), (0, 3), (1, 0), (0, 1), (1, 2), (1, 2))


def slot_count(seq):
    return 8 if seq <= 16 else 4


def bits_of(batch, seq):
    chips = [("batch", 1 << k) for k in range(batch.bit_length() - 1)]
    line = [("seq", 1 << k) for k in range(1, seq.bit_length() - 1)]
    return ("seq", 1), chips, line


def stage_orders(batch, seq):
    core, chips, line = bits_of(batch, seq)
    flipped = chips[::-1]
    return (
        [core] + chips + line,
        [core] + flipped + line,
        [core] + line + chips,
        [core] + line + flipped,
    )


def stage_rows(count):
    return [BLOCK >> (min(s, HALVINGS - 1) + 1) for s in range(count)]


class Links:
    LATENCY = 8.0
    CORE, LINE = 0.6, 0.041

    def __init__(self):
        self.now = 0.0
        self.active = {}
        self.arrived = {}

    def uses(self, bit):
        name, step = bit
        if bit == ("seq", 1):
            return (("core", 1),)
        if name == "batch":
            return ((name + str(step), 1),)
        return (("ends", 1),) if step == 2 else (("ends", 1), ("middle", 2))

    def start(self, key, size, bit):
        self.active[key] = [size, self.uses(bit)]

    def rates(self):
        load = {}
        for _size, uses in self.active.values():
            for link, weight in uses:
                load[link] = load.get(link, 0) + weight
        return {
            key: min((self.CORE if link == "core" else self.LINE) / load[link] for link, _w in uses)
            for key, (_size, uses) in self.active.items()
        }

    def forward(self, until=None):
        while self.active:
            rates = self.rates()
            key = min(self.active, key=lambda k: self.active[k][0] / rates[k])
            step = self.active[key][0] / rates[key]
            if until is not None and self.now + step > until:
                step = until - self.now
                key = None
            for k in self.active:
                self.active[k][0] -= step * rates[k]
            self.now += step
            if key is None:
                return
            del self.active[key]
            self.arrived[key] = self.now + self.LATENCY
            if until is None:
                return
        if until is not None:
            self.now = max(self.now, until)


class Reducer:
    def __init__(self, orders, slots, kinds, pieces, tile, red, sems):
        self.slots = slots
        self.orders, self.kinds, self.pieces = orders, kinds, pieces
        self.subs = [max(p[0] for p in job) + 1 for job in pieces]
        self.tile, self.red = tile, red
        self.send, self.recv, self.credit, self.local, self.gsend, self.grecv = sems
        self.stages = len(orders[0])
        self.halvings = min(HALVINGS, self.stages)
        self.rows = stage_rows(self.stages)
        self.jobs = len(pieces)
        self.links = Links()
        self.due = {}
        self.done = [-1] * self.jobs

    def order(self, j, b):
        return self.orders[self.kinds[j][b]]

    def held(self, j, s):
        if s < 0:
            return self.tile, j % TILES, BLOCK
        return self.red[s], j % self.slots, self.rows[s]

    def keep_start(self, j, b, s):
        return bit_of(self.order(j, b)[s]) * self.rows[s] if s < self.halvings else 0

    def give_start(self, j, b, s):
        return (1 - bit_of(self.order(j, b)[s])) * self.rows[s] if s < self.halvings else 0

    def scatter_copies(self, j, s):
        ref, slot, _rows = self.held(j, s - 1)
        into, into_slot, rows = self.held(j, s)
        copies = []
        for b in range(self.subs[j]):
            start = self.give_start(j, b, s)
            if not isinstance(start, int):
                start = pl.multiple_of(start, 8)
            copies.append(
                pltpu.make_async_remote_copy(
                    src_ref=ref.at[slot, b, pl.ds(start, rows), :],
                    dst_ref=into.at[into_slot, b],
                    send_sem=self.send.at[s, into_slot, b],
                    recv_sem=self.recv.at[s, into_slot, b],
                    device_id=partner(self.order(j, b)[s]),
                    device_id_type=MESH,
                )
            )
        return copies

    def owned(self, j, s, flip=False):
        views = []
        for block, _from, count, target, row, col in self.pieces[j]:
            start = row
            for t in range(s + 1):
                bit = bit_of(self.order(j, block)[t])
                if flip and t == s:
                    bit = 1 - bit
                start = start + bit * self.rows[t]
            views.append(
                target.at[pl.ds(pl.multiple_of(start, 8), self.rows[s]), pl.ds(col, count)]
            )
        return views

    def final(self, j):
        ref, slot, rows = self.held(j, self.stages - 1)
        return [
            ref.at[slot, block, pl.ds(0, rows), pl.ds(from_col, count)]
            for block, from_col, count, _target, _row, _col in self.pieces[j]
        ]

    def gather_copies(self, j, s, arriving=False):
        last = s == self.halvings - 1
        sources = self.final(j) if last else self.owned(j, s)
        blocks = [piece[0] for piece in self.pieces[j]]
        return [
            pltpu.make_async_remote_copy(
                src_ref=source,
                dst_ref=target,
                send_sem=self.gsend.at[j, s, p],
                recv_sem=self.grecv.at[j, s, p],
                device_id=partner(self.order(j, blocks[p])[s]),
                device_id_type=MESH,
            )
            for p, (source, target) in enumerate(zip(sources, self.owned(j, s, flip=arriving)))
        ]

    def local_copies(self, j):
        pairs = zip(self.final(j), self.owned(j, self.halvings - 1))
        return [
            pltpu.make_async_copy(source, target, self.local.at[j, p])
            for p, (source, target) in enumerate(pairs)
        ]

    def sent(self, j, event, s):
        size = self.rows[s] * TILE * 4e-6
        for b in range(self.subs[j]):
            self.links.start((j, event, b), size, self.order(j, b)[s])
        self.due[j] = event

    def arrival(self, j):
        times = [self.links.arrived.get((j, self.due[j], b)) for b in range(self.subs[j])]
        return None if None in times else max(times)

    def first_due(self):
        times = {j: self.arrival(j) for j in self.due}
        times = {j: time for j, time in times.items() if time is not None}
        if not times:
            return None, None
        j = min(times, key=times.get)
        return j, times[j]

    def advance(self, us):
        self.links.forward(self.links.now + us)

    def run(self, j):
        while self.arrival(j) is None:
            self.links.forward()
        self.links.forward(max(self.links.now, self.arrival(j)))
        event = self.due.pop(j)
        for b in range(self.subs[j]):
            self.links.arrived.pop((j, event, b))
        n = self.stages
        if event < n:
            s = event
            for copy in self.scatter_copies(j, s):
                copy.wait_send()
                copy.wait_recv()
            self.add(j, s)
            if s > 0:
                self.give_credit(j, s - 1)
            if s < n - 1:
                self.start_scatter(j, s + 1)
            else:
                for copy in self.local_copies(j) + self.gather_copies(j, self.halvings - 1):
                    copy.start()
                self.sent(j, event + 1, self.halvings - 1)
        else:
            s = self.halvings - 1 - (event - n)
            for copy in self.gather_copies(j, s, True):
                copy.wait_recv()
            if s == self.halvings - 1:
                for copy in self.gather_copies(j, s):
                    copy.wait_send()
                for copy in self.local_copies(j):
                    copy.wait()
                self.give_credit(j, n - 1)
            if s > 0:
                for copy in self.gather_copies(j, s - 1):
                    copy.start()
                self.sent(j, event + 1, s - 1)
        self.done[j] = event
        self.advance(SERVICE)

    def add(self, j, s):
        ref, slot, _rows = self.held(j, s - 1)
        into, into_slot, rows = self.held(j, s)
        starts = [self.keep_start(j, b, s) for b in range(self.subs[j])]
        step = min(48, rows)

        @pl.loop(0, rows // step)
        def _(i):
            for b in range(self.subs[j]):
                here = pl.ds(pl.multiple_of(starts[b] + i * step, 8), step)
                there = pl.ds(pl.multiple_of(i * step, 8), step)
                into[into_slot, b, there, :] += ref[slot, b, here, :]

    def give_credit(self, j, s):
        after = j + self.slots
        if after < self.jobs:
            for b in range(self.subs[after]):
                pl.semaphore_signal(
                    self.credit.at[s, j % self.slots, b],
                    inc=1,
                    device_id=partner(self.order(after, b)[s]),
                    device_id_type=MESH,
                )

    def start_scatter(self, j, s):
        if j >= self.slots:
            self.reach(j - self.slots, s + 1)
            for b in range(self.subs[j]):
                pl.semaphore_wait(self.credit.at[s, j % self.slots, b], 1)
        for copy in self.scatter_copies(j, s):
            copy.start()
        self.sent(j, s, s)

    def reach(self, j, event):
        while self.done[j] < event:
            self.run(j)

    def acquire(self, j):
        if j >= TILES:
            self.reach(j - TILES, 0)
        return j % TILES

    def produced(self, j):
        self.start_scatter(j, 0)

    def tick(self, us=0.0):
        self.advance(us)
        while True:
            j, time = self.first_due()
            if j is None or time > self.links.now:
                break
            self.run(j)

    def drain(self):
        while self.due:
            j, _time = self.first_due()
            if j is None:
                self.links.forward()
            else:
                self.run(j)
        for j in range(self.jobs):
            for s in range(self.halvings - 1):
                for copy in self.gather_copies(j, s):
                    copy.wait_send()


class Refs(typing.NamedTuple):
    x: typing.Any
    cot: typing.Any
    lengths: typing.Any
    norm_gain: typing.Any
    norm_shift: typing.Any
    alpha: typing.Any
    delta: typing.Any
    beta: typing.Any
    eta: typing.Any
    omega_in: typing.Any
    b_output_in: typing.Any
    b_shrink_in: typing.Any
    b_value_in: typing.Any
    b_gates_in: typing.Any
    b_expand_in: typing.Any
    qk: typing.Any
    bias: typing.Any
    w_value: typing.Any
    w_gates: typing.Any
    w_output: typing.Any
    w_expand: typing.Any
    w_shrink: typing.Any
    out_hbm: typing.Any
    dx_hbm: typing.Any
    dw_value: typing.Any
    dw_gates: typing.Any
    dw_output: typing.Any
    dw_expand: typing.Any
    dw_shrink: typing.Any
    sums: typing.Any
    wa: typing.Any
    wb: typing.Any
    wg: typing.Any
    cot_v: typing.Any
    dx: typing.Any
    tables: typing.Any
    gains: typing.Any
    b_value: typing.Any
    b_gates: typing.Any
    b_expand: typing.Any
    normed: typing.Any
    vpre: typing.Any
    gate: typing.Any
    att: typing.Any
    hpre: typing.Any
    mid: typing.Any
    epre: typing.Any
    mpre: typing.Any
    dnorm: typing.Any
    probs: typing.Any
    square: typing.Any
    lh: typing.Any
    ll: typing.Any
    th: typing.Any
    tl: typing.Any
    s768: typing.Any
    s_value: typing.Any
    s_expand: typing.Any
    s_gates: typing.Any
    s_small: typing.Any
    ends: typing.Any
    starts: typing.Any
    e_recv: typing.Any
    f_recv: typing.Any
    wsem: typing.Any
    osem: typing.Any
    send: typing.Any
    recv: typing.Any
    send2: typing.Any
    recv2: typing.Any
    tile: typing.Any
    sems: typing.Any
    red: typing.Any


def kernel(batch, seq, *refs):
    n = len(Refs._fields) - 2
    r = Refs(*refs[:n], refs[n : n + 6], refs[n + 6 :])
    rows, width = r.x.shape
    seg_len = rows // SEG
    me_b, me = lax.axis_index("batch"), lax.axis_index("seq")
    nstate = 16
    hv = r.vpre.shape[1]
    ff = r.epre.shape[1]
    zd = r.qk.shape[1]
    group = r.probs.shape[1]
    groups = rows // group
    reset0 = width + zd
    cand0 = reset0 + hv
    gates = cand0 + width
    scale = 1.0 / math.sqrt(zd)

    sources = (r.w_value, r.w_gates, r.w_output, r.w_expand, r.w_shrink, r.w_output, r.w_value)
    places = (r.wa, r.wg, r.wb, r.wa, r.wb, r.wb, r.wa)
    weights = [
        pltpu.make_async_copy(a, b, r.wsem.at[i]) for i, (a, b) in enumerate(zip(sources, places))
    ]
    cot_copy = pltpu.make_async_copy(r.cot, r.cot_v, r.wsem.at[len(weights)])
    for copy in weights[:3] + [cot_copy]:
        copy.start()

    gate_cols = [i * TILE for i in range(width // TILE)]
    gate_cols += [reset0 + i * TILE for i in range((hv + width) // TILE)]

    def tall_job(ref, i):
        return [(b, 0, TILE, ref, b * BLOCK, i * TILE) for b in range(2)]

    def wide_job(ref, cols):
        return [(b, 0, TILE, ref, 0, cols[b]) for b in range(2)]

    pieces = [tall_job(r.dw_shrink, i) for i in range(width // TILE)]
    pieces += [wide_job(r.dw_expand, (i, i + TILE)) for i in range(0, ff, 2 * TILE)]
    pieces += [tall_job(r.dw_output, i) for i in range(width // TILE)]
    pieces += [wide_job(r.dw_value, (i, i + TILE)) for i in range(0, hv, 2 * TILE)]
    pieces += [wide_job(r.dw_gates, gate_cols[i : i + 2]) for i in range(0, len(gate_cols), 2)]
    pieces.append([(0, 0, zd, r.dw_gates, 0, width), (0, zd, TILE - zd, r.sums, 0, 0)])
    kinds = [KINDS[j % len(KINDS)] for j in range(len(pieces))]
    comm = Reducer(
        stage_orders(batch, seq), slot_count(seq), kinds, pieces, r.tile, r.red, r.sems
    )
    _core, chips, _line = bits_of(batch, seq)

    barrier = pltpu.get_barrier_semaphore()

    def greet(k, _):
        pl.semaphore_signal(
            barrier, inc=1, device_id=(me_b, lax.rem(me + k, seq)), device_id_type=MESH
        )
        return 0

    lax.fori_loop(1, seq, greet, 0)
    for bit in chips:
        pl.semaphore_signal(barrier, inc=1, device_id=partner(bit), device_id_type=MESH)

    alpha, damping = sigmoid(r.alpha[...]), sigmoid(r.delta[...])
    rate = alpha * damping
    series = jnp.full_like(rate, 1.0 / 7.0)
    for n in range(6, 0, -1):
        series = series * rate + 1.0 / n
    log_decay = -rate * series
    for i, value in enumerate(
        (
            1.0 - rate,
            alpha * r.beta[...] * r.eta[...],
            jnp.exp(seg_len * log_decay),
            jnp.exp(rows * log_decay),
        )
    ):
        r.tables[i] = value
    decay, coef, dec_seg, dec_all = (r.tables.at[i] for i in range(4))

    def unfold(source, target, row=0):
        for d in range(source.shape[0]):
            target[row : row + 1, d * LANES : (d + 1) * LANES] = source[d : d + 1, :]

    unfold(r.b_value_in, r.b_value)
    unfold(r.b_gates_in, r.b_gates)
    unfold(r.b_expand_in, r.b_expand)
    for i in range(2):
        r.gains[2 * i : 2 * i + 1, :] = r.norm_gain[i : i + 1, :]
        r.gains[2 * i + 1 : 2 * i + 2, :] = r.norm_shift[i : i + 1, :]
    for i, source in enumerate((r.omega_in, r.b_output_in, r.b_shrink_in)):
        unfold(source, r.gains, 4 + i)
    gain0, shift0, gain1, shift1, omega, b_output, b_shrink = (
        r.gains[i : i + 1, :] for i in range(7)
    )

    first_end = r.lengths[0, 0]
    second_end = first_end + r.lengths[0, 1]

    def keep(group_id):
        starts = (group_id == 0) | (group_id == first_end) | (group_id == second_end)
        return jnp.where(starts, 0.0, 1.0)

    def keep_block(k):
        value = keep(k * groups)
        for g in range(1, groups):
            value = value * keep(k * groups + g)
        return value

    keep_seg = [
        keep(me * groups + k * groups // SEG) if k % (SEG // groups) == 0 else 1.0
        for k in range(SEG)
    ]

    def tiles(count, body, us, parts=1):
        for p in range(parts):
            pl.loop(count * p // parts, count * (p + 1) // parts)(body)
            comm.tick(us / parts)

    def zero_small(i):
        r.s768[i : i + 1, :] = jnp.zeros((1, width), f32)

    for i in range(8):
        zero_small(i)

    def add768(i, value, cols=slice(None)):
        r.s768[i : i + 1, cols] += jnp.sum(value, axis=0, keepdims=True)

    RC = 32

    def norm_stats(value):
        centre = value - jnp.mean(value, axis=-1, keepdims=True)
        inv = lax.rsqrt(jnp.mean(centre * centre, axis=-1, keepdims=True) + 1e-05)
        return centre * inv, inv

    def norm_back(grad, n, inv):
        return inv * (
            grad
            - jnp.mean(grad, axis=-1, keepdims=True)
            - n * jnp.mean(grad * n, axis=-1, keepdims=True)
        )

    @pl.loop(0, rows // RC)
    def _(i):
        part = at(i, RC)
        n, _inv = norm_stats(r.x[part, :])
        value = n * gain0 + shift0
        row_set(r.normed, part, value)
        r.lh[part, :width], r.ll[part, :width] = split(value)

    def seg_rows(t):
        return pl.ds(t, SEG, stride=seg_len)

    def rows_of(ref, count, cols):
        return [jnp.broadcast_to(ref[n : n + 1, cols], (SEG, LANES)) for n in count]

    def end_states(source, reverse, target):
        @pl.loop(0, width // LANES)
        def _(d):
            cols = at(d, LANES)
            dec = rows_of(decay, range(nstate), cols)

            def turn(t, state):
                at_t = seg_len - 1 - t if reverse else t
                value = source[d, seg_rows(at_t), :]
                return tuple(a * s + value for a, s in zip(dec, state))

            zero = jnp.zeros((SEG, LANES), f32)
            state = lax.fori_loop(0, seg_len, turn, (zero,) * nstate, unroll=8)
            for n in range(nstate):
                target[d, n * SEG : (n + 1) * SEG, :] = state[n]

    def seg_of(k):
        return pl.ds(k, nstate, stride=SEG)

    def exchange(buffer, send_sem, recv_sem):
        def copy_to(k):
            peer = lax.rem(me + k, seq)
            return pltpu.make_async_remote_copy(
                src_ref=buffer.at[me],
                dst_ref=buffer.at[me],
                send_sem=send_sem.at[k],
                recv_sem=recv_sem.at[me],
                device_id=(me_b, peer),
                device_id_type=MESH,
            )

        def copy_from(k):
            peer = lax.rem(me + k, seq)
            return pltpu.make_async_remote_copy(
                src_ref=buffer.at[me],
                dst_ref=buffer.at[peer],
                send_sem=send_sem.at[k],
                recv_sem=recv_sem.at[peer],
                device_id=(me_b, peer),
                device_id_type=MESH,
            )

        def start():
            def one(k, _):
                copy_to(k).start()
                return 0

            lax.fori_loop(1, seq, one, 0)

        def wait():
            def one(k, _):
                copy_to(k).wait_send()
                copy_from(k).wait_recv()
                return 0

            lax.fori_loop(1, seq, one, 0)

        return start, wait

    end_states(r.normed, False, r.ends)
    total = jnp.zeros((nstate, width), f32)
    for k in range(SEG):
        total = keep_seg[k] * total * dec_seg[...] + row_get(r.ends, seg_of(k))
    r.e_recv[me] = total
    pl.semaphore_wait(barrier, seq - 1 + len(chips))
    start_e, wait_e = exchange(r.e_recv, r.send, r.recv)
    start_e()

    weights[0].wait()

    @pl.loop(0, hv // TILE)
    def _(i):
        c = at(i, TILE)
        w = r.wa[:, c]
        r.vpre[:, c] = (
            dot(r.lh[:, :width], w) + dot(r.ll[:, :width], w) + r.b_value[:, c]
        )

    weights[3].start()

    wait_e()

    def carry_step(k, carried):
        new = dec_all[...] * (keep_block(k) * carried) + r.e_recv[k]
        return jnp.where(k < me, new, carried)

    state = lax.fori_loop(0, seq, carry_step, jnp.zeros((nstate, width), f32))
    for k in range(SEG):
        state = keep_seg[k] * state
        row_set(r.starts, seg_of(k), state)
        if k < SEG - 1:
            state = dec_seg[...] * state + row_get(r.ends, seg_of(k))

    @pl.loop(0, width // LANES)
    def _(d):
        cols = at(d, LANES)
        dec = rows_of(decay, range(nstate), cols)
        mix = rows_of(coef, range(nstate), cols)

        def turn(t, state):
            value = r.normed[d, seg_rows(t), :]
            state = tuple(a * s + value for a, s in zip(dec, state))
            terms = [m * s for m, s in zip(mix, state)]
            while len(terms) > 1:
                terms = [a + b for a, b in zip(terms[::2], terms[1::2])]
            r.mpre[d, seg_rows(t), :] = terms[0]
            return state

        first = tuple(r.starts[d, n * SEG : (n + 1) * SEG, :] for n in range(nstate))
        lax.fori_loop(0, seg_len, turn, first, unroll=4)

    @pl.loop(0, rows // RC)
    def _(i):
        part = at(i, RC)
        value = row_get(r.mpre, part) + omega * row_get(r.normed, part)
        row_set(r.mpre, part, value)
        r.lh[part, :width], r.ll[part, :width] = split(silu(value))

    weights[1].wait()

    def gate_tile(c):
        w = r.wg[:, c]
        r.gate[:, c] = (
            dot(r.lh[:, :width], w) + dot(r.ll[:, :width], w) + r.b_gates[:, c]
        )

    @pl.loop(0, width // TILE)
    def _(i):
        gate_tile(at(i, TILE))

    gate_tile(pl.ds(width, zd))

    @pl.loop(0, (hv + width) // TILE)
    def _(i):
        gate_tile(off(reset0, i, TILE))

    lag = lax.broadcasted_iota(jnp.int32, (group, group), 0) - lax.broadcasted_iota(
        jnp.int32, (group, group), 1
    )
    row_id = lax.broadcasted_iota(jnp.int32, (group, group), 0)
    causal = lag >= 0
    table = jnp.broadcast_to(r.bias[...], (group, group))
    for b in range(group.bit_length() - 1):
        moved = pltpu.roll(table, 1 << b, 1)
        table = jnp.where((row_id & (1 << b)) != 0, moved, table)
    q_gain, k_gain, q_shift = (r.qk[i : i + 1, :] for i in range(3))
    r.square[...] = table.T

    @pl.loop(0, groups)
    def _(g):
        part = at(g, group)
        shared = silu(r.gate[part, width:reset0])
        q = split(shared * q_gain + q_shift)
        k = split(shared * k_gain)
        scores = dot3(q, k, NT) * scale + r.square[...]
        scores = jnp.where(causal, scores, -1e30)
        p = jnp.exp(scores - jnp.max(scores, axis=-1, keepdims=True))
        p = p / jnp.sum(p, axis=-1, keepdims=True)
        r.probs[part, :] = p
        p = split(p)

        @pl.loop(0, hv // TILE)
        def _(i):
            c = at(i, TILE)
            v = split(silu(r.vpre[part, c]))
            attended = dot3(p, v)
            r.att[part, c] = attended
            gated = attended * silu(r.gate[part, off(reset0, i, TILE)])
            r.lh[part, c], r.ll[part, c] = split(gated)

    weights[2].wait()

    @pl.loop(0, width // TILE)
    def _(i):
        c = at(i, TILE)
        w = r.wb[:, c]
        value = (
            dot(r.lh[...], w)
            + dot(r.ll[...], w)
            + (r.gate[:, off(cand0, i, TILE)] + r.gains[5:6, c])
        )
        r.hpre[:, c] = value
        x = r.x[:, c]
        r.mid[:, c] = x + sigmoid(r.gate[:, c]) * (silu(value) - x)

    weights[4].start()

    @pl.loop(0, rows // RC)
    def _(i):
        part = at(i, RC)
        n, _inv = norm_stats(r.mid[part, :])
        r.lh[part, :width], r.ll[part, :width] = split(n * gain1 + shift1)

    weights[3].wait()

    @pl.loop(0, ff // TILE)
    def _(i):
        c = at(i, TILE)
        w = r.wa[:, c]
        r.epre[:, c] = (
            dot(r.lh[:, :width], w) + dot(r.ll[:, :width], w) + r.b_expand[:, c]
        )

    comm.advance(50.0)
    cot_copy.wait()

    def transposed(source, count, first=0):
        @pl.loop(0, count // LANES)
        def _(i):
            here = off(first, i, LANES)
            r.th[here, :], r.tl[here, :] = split(source(i, at(i, LANES)).T)

    def products(j, pairs):
        slot = comm.acquire(j)
        for b, (first, grad) in enumerate(pairs):
            g = split(grad)
            cols = grad.shape[1]

            @pl.loop(0, BLOCK // TILE)
            def _(k):
                a = off(first, k, TILE)
                value = dot3((r.th[a, :], r.tl[a, :]), g)
                if cols == TILE:
                    r.tile[slot, b, at(k, TILE), :] = value
                else:
                    r.tile[slot, b, at(k, TILE), :cols] = value

        comm.advance(1.0 * len(pairs))
        return slot

    def tall(j, grad):
        products(j, [(0, grad), (BLOCK, grad)])
        comm.produced(j)
        comm.tick()

    def wide(j, first, left, right):
        products(j, [(first, left), (first, right)])
        comm.produced(j)
        comm.tick()

    def cols_of(ref, i, start=0):
        return ref[:, start + i * TILE : start + (i + 1) * TILE]

    transposed(lambda i, c: silu(r.epre[:, c]), ff)
    comm.advance(2.0)
    for i in range(width // TILE):
        tall(i, cols_of(r.cot_v, i))

    def inner_halves(i):
        c = at(i, TILE)
        r.lh[:, c], r.ll[:, c] = split(silu(r.epre[:, c]))

    tiles(ff // TILE, inner_halves, 1.2)
    weights[4].wait()

    def out_tile(i):
        c = at(i, TILE)
        w = r.wb[:, c]
        r.dx[:, c] = r.mid[:, c] + (dot(r.lh[...], w) + dot(r.ll[...], w) + r.gains[6:7, c])

    tiles(width // TILE, out_tile, 3.0)
    out_copy = pltpu.make_async_copy(r.dx, r.out_hbm, r.osem.at[0])
    out_copy.start()

    def cot_halves(i):
        part = at(i, RC)
        value = r.cot_v[part, :]
        add768(6, value)
        r.lh[part, :width], r.ll[part, :width] = split(value)

    tiles(rows // RC, cot_halves, 1.0)

    def inner_back(i):
        c = at(i, TILE)
        w = r.wb[c, :]
        value = (dot(r.lh[:, :width], w, NT) + dot(r.ll[:, :width], w, NT)) * dsilu(
            r.epre[:, c]
        )
        r.epre[:, c] = value
        r.s_expand[:, c] = jnp.sum(value, axis=0, keepdims=True)

    tiles(ff // TILE, inner_back, 3.2)
    weights[5].start()

    def expand_halves(i):
        c = at(i, TILE)
        r.lh[:, c], r.ll[:, c] = split(r.epre[:, c])

    tiles(ff // TILE, expand_halves, 0.8)

    @pl.loop(0, rows // RC)
    def _(i):
        part = at(i, RC)
        n, _inv = norm_stats(r.mid[part, :])
        row_set(r.dnorm, part, n * gain1 + shift1)

    transposed(lambda i, c: r.dnorm[i], width)
    comm.tick(2.0)
    for i in range(ff // (2 * TILE)):
        wide(3 + i, 0, cols_of(r.epre, 2 * i), cols_of(r.epre, 2 * i + 1))

    out_copy.wait()

    @pl.loop(0, width // TILE)
    def _(i):
        c = at(i, TILE)
        w = r.wa[c, :]
        r.dx[:, c] = dot(r.lh[...], w, NT) + dot(r.ll[...], w, NT)

    weights[6].start()
    comm.tick(3.0)

    def middle_back(i):
        part = at(i, RC)
        grad = r.dx[part, :]
        n, inv = norm_stats(r.mid[part, :])
        add768(2, grad * n)
        add768(3, grad)
        dmid = r.cot_v[part, :] + norm_back(grad * gain1, n, inv)
        update = sigmoid(r.gate[part, :width])
        pre = r.hpre[part, :]
        x = r.x[part, :]
        dhpre = dmid * update * dsilu(pre)
        r.dx[part, :] = dmid * (1.0 - update)
        dupdate = dmid * (silu(pre) - x) * (update * (1.0 - update))
        r.gate[part, :width] = dupdate
        r.gate[part, cand0:] = dhpre
        r.lh[part, :width], r.ll[part, :width] = split(dhpre)
        r.s_gates[:, :width] = (
            jnp.where(i == 0, 0.0, r.s_gates[:, :width])
            + jnp.sum(dupdate, axis=0, keepdims=True)
        )
        add768(5, dhpre)

    tiles(rows // RC, middle_back, 5.0, 2)

    transposed(lambda i, c: r.att[:, c] * silu(r.gate[:, off(reset0, i, LANES)]), hv)
    weights[5].wait()
    comm.tick(3.0)
    for i in range(width // TILE):
        tall(6 + i, cols_of(r.gate, i, cand0))

    def attended_back(i):
        c = at(i, TILE)
        w = r.wb[c, :]
        gated = dot(r.lh[:, :width], w, NT) + dot(r.ll[:, :width], w, NT)
        here = off(reset0, i, TILE)
        pre = r.gate[:, here]
        dreset = gated * r.att[:, c] * dsilu(pre)
        r.att[:, c] = gated * silu(pre)
        r.gate[:, here] = dreset
        r.s_gates[:, here] = jnp.sum(dreset, axis=0, keepdims=True)

    tiles(hv // TILE, attended_back, 3.5)

    r.s_small[...] = jnp.zeros_like(r.s_small)
    r.square[...] = jnp.zeros((group, group), f32)

    def attention_back(g):
        part = at(g, group)
        p = r.probs[part, :]
        p_t = split(p.T)

        def value_tile(i, dp):
            c = at(i, TILE)
            pre = r.vpre[part, c]
            d_att = split(r.att[part, c])
            r.vpre[part, c] = dot3(p_t, d_att) * dsilu(pre)
            return dp + dot3(d_att, split(silu(pre)), NT)

        dp = lax.fori_loop(0, hv // TILE, value_tile, jnp.zeros((group, group), f32))
        ds = p * (dp - jnp.sum(dp * p, axis=-1, keepdims=True))
        r.square[...] += ds
        ds = ds * scale
        pre = r.gate[part, width:reset0]
        shared = silu(pre)
        dq = dot3(split(ds), split(shared * k_gain))
        dk = dot3(split(ds.T), split(shared * q_gain + q_shift))
        for n, value in enumerate((dq * shared, dk * shared, dq)):
            r.s_small[n : n + 1, :] += jnp.sum(value, axis=0, keepdims=True)
        r.gate[part, width:reset0] = (dq * q_gain + dk * k_gain) * dsilu(pre)

    tiles(groups, attention_back, 8.4, 4)
    diagonals = r.square[...].T
    for b in range(group.bit_length() - 1):
        moved = pltpu.roll(diagonals, group - (1 << b), 1)
        diagonals = jnp.where((row_id & (1 << b)) != 0, moved, diagonals)
    r.s_small[3:4, :] = jnp.sum(diagonals, axis=0, keepdims=True)
    r.s_gates[:, width:reset0] = jnp.sum(r.gate[:, width:reset0], axis=0, keepdims=True)
    r.s_gates[:, cand0:] = r.s768[5:6, :]

    comm.tick(0.5)
    weights[6].wait()

    @pl.loop(0, hv // TILE)
    def _(i):
        c = at(i, TILE)
        value = r.vpre[:, c]
        r.s_value[:, c] = jnp.sum(value, axis=0, keepdims=True)
        r.lh[:, c], r.ll[:, c] = split(value)

    @pl.loop(0, width // TILE)
    def _(i):
        c = at(i, TILE)
        w = r.wa[c, :]
        col_set(r.dnorm, i, dot(r.lh[...], w, NT) + dot(r.ll[...], w, NT))

    comm.tick(4.2)
    transposed(lambda i, c: r.normed[i], width, width)
    transposed(lambda i, c: silu(r.mpre[i]), width)
    comm.tick(2.5)

    def gate_section(start, size, first, last):
        @pl.loop(0, size // LANES)
        def _(i):
            c = at(i, LANES)
            r.lh[:, c], r.ll[:, c] = split(r.gate[:, off(start, i, LANES)])

        @pl.loop(0, width // TILE)
        def _(i):
            c = at(i, TILE)
            w = r.wg[c, start : start + size]
            value = dot(r.lh[:, :size], w, NT) + dot(r.ll[:, :size], w, NT)
            if not first:
                value += r.att[:, c]
            if last:
                value = value * dsilu(col_get(r.mpre, i))
                col_set(r.mpre, i, value)
                add768(4, value * col_get(r.normed, i), c)
                col_set(r.dnorm, i, col_get(r.dnorm, i) + r.gains[4:5, c] * value)
            else:
                r.att[:, c] = value

        comm.tick(size * 8.0 / gates)

    gate_section(0, reset0, True, False)
    gate_section(reset0, hv, False, False)
    gate_section(cand0, width, False, True)

    for i in range(hv // (2 * TILE)):
        wide(9 + i, width, cols_of(r.vpre, 2 * i), cols_of(r.vpre, 2 * i + 1))
    for i in range(len(gate_cols) // 2):
        left, right = gate_cols[2 * i : 2 * i + 2]
        wide(12 + i, 0, cols_of(r.gate, 0, left), cols_of(r.gate, 0, right))

    end_states(r.mpre, True, r.ends)
    adj = jnp.zeros((nstate, width), f32)
    for k in reversed(range(SEG)):
        if k < SEG - 1:
            adj = dec_seg[...] * (keep_seg[k + 1] * adj)
        adj = adj + row_get(r.ends, seg_of(k))
    r.f_recv[me] = adj
    start_f, wait_f = exchange(r.f_recv, r.send2, r.recv2)
    start_f()

    comm.tick(4.0)
    wait_f()
    comm.tick(7.0)

    def adj_step(j, carried):
        k = seq - 1 - j
        new = keep(k * groups) * r.f_recv[k] + dec_all[...] * (keep_block(k) * carried)
        return jnp.where(k > me, new, carried)

    adj = lax.fori_loop(0, seq, adj_step, jnp.zeros((nstate, width), f32))
    for k in reversed(range(SEG)):
        fresh = row_get(r.ends, seg_of(k))
        row_set(r.ends, seg_of(k), adj)
        if k > 0:
            adj = keep_seg[k] * (dec_seg[...] * adj + fresh)

    half = nstate // 2
    for h in range(2):
        states = range(h * half, (h + 1) * half)

        def average_back(d):
            cols = at(d, LANES)
            dec = rows_of(decay, states, cols)
            mix = rows_of(coef, states, cols)

            def ahead(t, state):
                value = r.normed[d, seg_rows(t), :]
                for n in range(half):
                    r.epre[at(t, SEG), n * LANES : (n + 1) * LANES] = state[n]
                return tuple(a * s + value for a, s in zip(dec, state))

            first = tuple(r.starts[d, n * SEG : (n + 1) * SEG, :] for n in states)
            lax.fori_loop(0, seg_len, ahead, first, unroll=4)

            def back(j, carried):
                t = seg_len - 1 - j
                adj, p_sum, q_sum = carried
                grad = r.mpre[d, seg_rows(t), :]
                value = r.normed[d, seg_rows(t), :]
                adj = tuple(a * s + grad for a, s in zip(dec, adj))
                p_sum = tuple(p + a * value for p, a in zip(p_sum, adj))
                q_sum = tuple(
                    q + a * r.epre[at(t, SEG), n * LANES : (n + 1) * LANES]
                    for n, (q, a) in enumerate(zip(q_sum, adj))
                )
                terms = [m * a for m, a in zip(mix, adj)]
                while len(terms) > 1:
                    terms = [a + b for a, b in zip(terms[::2], terms[1::2])]
                r.dnorm[d, seg_rows(t), :] += terms[0]
                return adj, p_sum, q_sum

            zero = (jnp.zeros((SEG, LANES), f32),) * half
            last = tuple(r.ends[d, n * SEG : (n + 1) * SEG, :] for n in states)
            _adj, p_sum, q_sum = lax.fori_loop(0, seg_len, back, (last, zero, zero), unroll=4)
            for n in range(half):
                row = 8 + h * half + n
                r.s768[row : row + 1, cols] = jnp.sum(p_sum[n], axis=0, keepdims=True)
                row = row + nstate
                r.s768[row : row + 1, cols] = jnp.sum(q_sum[n], axis=0, keepdims=True)

        tiles(width // LANES, average_back, 12.0, 6)

    def first_back(i):
        part = at(i, RC)
        grad = row_get(r.dnorm, part)
        n, inv = norm_stats(r.x[part, :])
        add768(0, grad * n)
        add768(1, grad)
        r.dx[part, :] += norm_back(grad * gain0, n, inv)

    tiles(rows // RC, first_back, 3.0)
    dx_copy = pltpu.make_async_copy(r.dx, r.dx_hbm, r.osem.at[1])
    dx_copy.start()

    slot = products(comm.jobs - 1, [(0, r.gate[:, width:reset0])])
    r.tile[slot, 0, :, zd:] = jnp.zeros((BLOCK, TILE - zd), f32)
    place = 0

    def put(value):
        nonlocal place
        count = value.shape[0]
        r.tile[slot, 0, place : place + count, zd:] = value
        place += count

    for d in range(width // LANES):
        put(r.s768[:, d * LANES : (d + 1) * LANES])
    put(r.s_small[...])
    for ref in (r.s_value, r.s_expand, r.s_gates):
        for d in range(ref.shape[1] // LANES):
            put(ref[:, d * LANES : (d + 1) * LANES])
    comm.produced(comm.jobs - 1)
    comm.drain()
    dx_copy.wait()


def finish(sums, alpha, delta, beta, eta, *outs):
    gain, shift, d_alpha, d_delta, d_beta, d_eta, omega, b_output, b_shrink = outs[:9]
    qk, bias, b_value, b_expand, b_gates = outs[9:]
    nstate, width = alpha.shape
    tall_rows = 8 + 2 * nstate
    for d in range(width // LANES):
        cols = slice(d * LANES, (d + 1) * LANES)
        row = d * tall_rows
        for n in range(2):
            gain[n : n + 1, cols] = sums[row + 2 * n : row + 2 * n + 1, :]
            shift[n : n + 1, cols] = sums[row + 2 * n + 1 : row + 2 * n + 2, :]
        for n, target in enumerate((omega, b_output, b_shrink)):
            target[d : d + 1, :] = sums[row + 4 + n : row + 5 + n, :]
        p_sum = sums[row + 8 : row + 8 + nstate, :]
        q_sum = sums[row + 8 + nstate : row + 8 + 2 * nstate, :]
        rate, damping = sigmoid(alpha[:, cols]), sigmoid(delta[:, cols])
        d_inflow = eta[:, cols] * p_sum
        d_eta[:, cols] = rate * beta[:, cols] * p_sum
        d_decay = eta[:, cols] * (rate * beta[:, cols]) * q_sum
        d_rate = d_inflow * beta[:, cols] - d_decay * damping
        d_alpha[:, cols] = d_rate * rate * (1.0 - rate)
        d_delta[:, cols] = -d_decay * rate * damping * (1.0 - damping)
        d_beta[:, cols] = d_inflow * rate
    place = width // LANES * tall_rows
    qk[...] = sums[place : place + 3, :]
    bias[...] = sums[place + 3 : place + 4, :]
    place += 8
    for target in (b_value, b_expand, b_gates):
        target[...] = sums[place : place + target.shape[0], :]
        place += target.shape[0]


def layer(operands, batch, seq):
    rows, width = operands[0].shape
    w_value, w_gates, w_output, w_expand, w_shrink = operands[-5:]
    hv, gates, ff = w_value.shape[1], w_gates.shape[1], w_expand.shape[1]
    zd, group, nstate = operands[15].shape[1], operands[16].shape[1], operands[5].shape[0]
    vmem = pl.BlockSpec(memory_space=pltpu.VMEM)
    smem = pl.BlockSpec(memory_space=pltpu.SMEM)
    hbm = pl.BlockSpec(memory_space=pl.ANY)
    stages, slots = len(stage_orders(batch, seq)[0]), slot_count(seq)

    def shape(*dims, kind=f32):
        return jax.ShapeDtypeStruct(dims, kind)

    return pl.pallas_call(
        functools.partial(kernel, batch, seq),
        out_shape=(
            shape(rows, width),
            shape(rows, width),
            shape(width, hv),
            shape(width, gates),
            shape(hv, width),
            shape(width, ff),
            shape(ff, width),
            shape(BLOCK, TILE - zd),
        ),
        in_specs=[vmem, hbm, smem] + [vmem] * 14 + [hbm] * 5,
        out_specs=(hbm,) * 8,
        scratch_shapes=[
            pltpu.VMEM(w_value.shape, bf16),
            pltpu.VMEM(w_output.shape, bf16),
            pltpu.VMEM(w_gates.shape, bf16),
            pltpu.VMEM((rows, width), f32),
            pltpu.VMEM((rows, width), f32),
            pltpu.VMEM((4, nstate, width), f32),
            pltpu.VMEM((8, width), f32),
            pltpu.VMEM((1, hv), f32),
            pltpu.VMEM((1, gates), f32),
            pltpu.VMEM((1, ff), f32),
            pltpu.VMEM((width // LANES, rows, LANES), f32),
            pltpu.VMEM((rows, hv), f32),
            pltpu.VMEM((rows, gates), f32),
            pltpu.VMEM((rows, hv), f32),
            pltpu.VMEM((rows, width), f32),
            pltpu.VMEM((rows, width), f32),
            pltpu.VMEM((rows, ff), f32),
            pltpu.VMEM((width // LANES, rows, LANES), f32),
            pltpu.VMEM((width // LANES, rows, LANES), f32),
            pltpu.VMEM((rows, group), f32),
            pltpu.VMEM((group, group), f32),
            pltpu.VMEM((rows, max(hv, ff)), bf16),
            pltpu.VMEM((rows, max(hv, ff)), bf16),
            pltpu.VMEM((max(hv, ff), rows), bf16),
            pltpu.VMEM((max(hv, ff), rows), bf16),
            pltpu.VMEM((8 + 2 * nstate, width), f32),
            pltpu.VMEM((1, hv), f32),
            pltpu.VMEM((1, ff), f32),
            pltpu.VMEM((1, gates), f32),
            pltpu.VMEM((8, zd), f32),
            pltpu.VMEM((width // LANES, nstate * SEG, LANES), f32),
            pltpu.VMEM((width // LANES, nstate * SEG, LANES), f32),
            pltpu.VMEM((seq, nstate, width), f32),
            pltpu.VMEM((seq, nstate, width), f32),
            pltpu.SemaphoreType.DMA((8,)),
            pltpu.SemaphoreType.DMA((2,)),
            pltpu.SemaphoreType.DMA((seq,)),
            pltpu.SemaphoreType.DMA((seq,)),
            pltpu.SemaphoreType.DMA((seq,)),
            pltpu.SemaphoreType.DMA((seq,)),
            pltpu.VMEM((TILES, 2, BLOCK, TILE), f32),
            pltpu.SemaphoreType.DMA((stages, slots, 2)),
            pltpu.SemaphoreType.DMA((stages, slots, 2)),
            pltpu.SemaphoreType.REGULAR((stages, slots, 2)),
            pltpu.SemaphoreType.DMA((JOBS, 2)),
            pltpu.SemaphoreType.DMA((JOBS, HALVINGS, 2)),
            pltpu.SemaphoreType.DMA((JOBS, HALVINGS, 2)),
        ]
        + [pltpu.VMEM((slots, 2, count, TILE), f32) for count in stage_rows(stages)],
        compiler_params=pltpu.CompilerParams(
            collective_id=0, has_side_effects=True, vmem_limit_bytes=63 << 20
        ),
        cost_estimate=pl.CostEstimate(
            flops=52_000_000_000, bytes_accessed=60_000_000, transcendentals=20_000_000
        ),
    )(*operands)


def shards(
    batch,
    seq,
    tokens,
    lengths,
    cotangent,
    norm_gain,
    norm_shift,
    alpha_logit,
    delta_logit,
    ema_beta,
    ema_eta,
    ema_omega,
    w_value,
    b_value,
    w_gates,
    b_gates,
    query_key,
    position_bias,
    w_output,
    b_output,
    w_expand,
    b_expand,
    w_shrink,
    b_shrink,
):
    def lines(vector):
        return vector.reshape(-1, LANES)

    averages = (alpha_logit.T, delta_logit.T, ema_beta.T, ema_eta.T)
    operands = (tokens[0], cotangent[0], lengths, norm_gain.T, norm_shift.T) + averages
    operands += (lines(ema_omega), lines(b_output), lines(b_shrink))
    operands += (lines(b_value), lines(b_gates), lines(b_expand))
    operands += (query_key.T, position_bias[None])
    operands += (w_value, w_gates, w_output, w_expand, w_shrink)
    output, grad_tokens, dw_value, dw_gates, dw_output, dw_expand, dw_shrink, sums = layer(
        operands, batch, seq
    )
    like = (norm_gain.T, norm_shift.T) + averages
    like += (lines(ema_omega), lines(b_output), lines(b_shrink), query_key.T)
    like += (position_bias[None], lines(b_value), lines(b_expand), lines(b_gates))
    small = pl.pallas_call(
        finish, out_shape=tuple(jax.ShapeDtypeStruct(a.shape, f32) for a in like)
    )(sums, *averages)
    gain, shift, d_alpha, d_delta, d_beta, d_eta, d_omega, d_output, d_shrink = small[:9]
    d_qk, d_bias, d_value, d_expand, d_gates = small[9:]
    return (
        output[None],
        grad_tokens[None],
        gain.T,
        shift.T,
        d_alpha.T,
        d_delta.T,
        d_beta.T,
        d_eta.T,
        d_omega.reshape(-1),
        dw_value,
        d_value.reshape(-1),
        dw_gates,
        d_gates.reshape(-1),
        d_qk.T,
        d_bias[0],
        dw_output,
        d_output.reshape(-1),
        dw_expand,
        d_expand.reshape(-1),
        dw_shrink,
        d_shrink.reshape(-1),
    )


def solution(mesh):
    token_spec = P("batch", "seq", None)
    return jax.shard_map(
        functools.partial(shards, mesh.shape["batch"], mesh.shape["seq"]),
        mesh=mesh,
        in_specs=(token_spec, P("batch", None), token_spec) + (P(),) * 19,
        out_specs=(token_spec, token_spec) + (P(),) * 19,
        check_vma=False,
    )
```

```python
import functools
import math
import typing

import jax
import jax.numpy as jnp
from jax import lax
from jax.experimental import pallas as pl
from jax.experimental.pallas import tpu as pltpu
from jax.sharding import PartitionSpec as P

f32 = jnp.float32
bf16 = jnp.bfloat16
MESH = pl.DeviceIdType.MESH

SEG = 8
LANES = 128
TILE = 256

NN = (((1,), (0,)), ((), ()))
NT = (((1,), (1,)), ((), ()))


def split(value):
    high = value.astype(bf16)
    return high, (value - high.astype(f32)).astype(bf16)


def dot(a, b, dims=NN):
    return lax.dot_general(a, b, dims, preferred_element_type=f32)


def dot3(a, b, dims=NN):
    a_high, a_low = a
    b_high, b_low = b
    return dot(a_high, b_high, dims) + (dot(a_high, b_low, dims) + dot(a_low, b_high, dims))


def sigmoid(value):
    return 1.0 / (1.0 + jnp.exp(-value))


def silu(value):
    return value * sigmoid(value)


def dsilu(value):
    s = sigmoid(value)
    return s * (1.0 + value * (1.0 - s))


def row_get(ref, part):
    return jnp.concatenate([ref[d, part, :] for d in range(ref.shape[0])], axis=-1)


def row_set(ref, part, value):
    for d in range(ref.shape[0]):
        ref[d, part, :] = value[:, d * LANES : (d + 1) * LANES]


def col_get(ref, i, size=TILE):
    n = size // LANES
    return jnp.concatenate([ref[i * n + k] for k in range(n)], axis=-1)


def col_set(ref, i, value):
    n = value.shape[1] // LANES
    for k in range(n):
        ref[i * n + k] = value[:, k * LANES : (k + 1) * LANES]


def at(i, size):
    return pl.ds(pl.multiple_of(i * size, size), size)


def off(start, i, size):
    return pl.ds(pl.multiple_of(start + i * size, LANES), size)


def bit_of(bit):
    name, step = bit
    return lax.rem(lax.div(lax.axis_index(name), step), 2)


def partner(bit):
    name, step = bit
    where = {"batch": lax.axis_index("batch"), "seq": lax.axis_index("seq")}
    where[name] = where[name] + step * (1 - 2 * bit_of(bit))
    return (where["batch"], where["seq"])


HALVINGS = 5
BLOCK = 768
TILES = 2
SERVICE = 0.5
JOBS = 19
KINDS = ((0, 3), (1, 0), (0, 3), (0, 1), (0, 3), (1, 2), (0, 1), (0, 0), (0, 1), (1, 0), (0, 1), (1, 0), (1, 3), (0, 1), (0, 3), (1, 0), (0, 2), (1, 3), (1, 1))


def slot_count(seq):
    return 8 if seq <= 16 else 4


def bits_of(batch, seq):
    chips = [("batch", 1 << k) for k in range(batch.bit_length() - 1)]
    line = [("seq", 1 << k) for k in range(1, seq.bit_length() - 1)]
    return ("seq", 1), chips, line


def stage_orders(batch, seq):
    core, chips, line = bits_of(batch, seq)
    flipped = chips[::-1]
    return (
        [core] + chips + line,
        [core] + flipped + line,
        [core] + line + chips,
        [core] + line + flipped,
    )


def stage_rows(count):
    return [BLOCK >> (min(s, HALVINGS - 1) + 1) for s in range(count)]


class Links:
    LATENCY = 5.06
    CORE, LINE = 0.6, 0.041

    def __init__(self):
        self.now = 0.0
        self.active = {}
        self.arrived = {}

    def uses(self, bit):
        name, step = bit
        if bit == ("seq", 1):
            return (("core", 1),)
        if name == "batch":
            return ((name + str(step), 1),)
        return (("ends", 1),) if step == 2 else (("ends", 1), ("middle", 2))

    def start(self, key, size, bit):
        self.active[key] = [size, self.uses(bit)]

    def rates(self):
        load = {}
        for _size, uses in self.active.values():
            for link, weight in uses:
                load[link] = load.get(link, 0) + weight
        return {
            key: min((self.CORE if link == "core" else self.LINE) / load[link] for link, _w in uses)
            for key, (_size, uses) in self.active.items()
        }

    def forward(self, until=None):
        while self.active:
            rates = self.rates()
            key = min(self.active, key=lambda k: self.active[k][0] / rates[k])
            step = self.active[key][0] / rates[key]
            if until is not None and self.now + step > until:
                step = until - self.now
                key = None
            for k in self.active:
                self.active[k][0] -= step * rates[k]
            self.now += step
            if key is None:
                return
            del self.active[key]
            self.arrived[key] = self.now + self.LATENCY
            if until is None:
                return
        if until is not None:
            self.now = max(self.now, until)


class Reducer:
    def __init__(self, orders, slots, kinds, pieces, tile, red, sems):
        self.slots = slots
        self.orders, self.kinds, self.pieces = orders, kinds, pieces
        self.subs = [max(p[0] for p in job) + 1 for job in pieces]
        self.tile, self.red = tile, red
        self.send, self.recv, self.credit, self.local, self.gsend, self.grecv = sems
        self.stages = len(orders[0])
        self.halvings = min(HALVINGS, self.stages)
        self.rows = stage_rows(self.stages)
        self.jobs = len(pieces)
        self.links = Links()
        self.due = {}
        self.done = [-1] * self.jobs

    def order(self, j, b):
        return self.orders[self.kinds[j][b]]

    def held(self, j, s):
        if s < 0:
            return self.tile, j % TILES, BLOCK
        return self.red[s], j % self.slots, self.rows[s]

    def keep_start(self, j, b, s):
        return bit_of(self.order(j, b)[s]) * self.rows[s] if s < self.halvings else 0

    def give_start(self, j, b, s):
        return (1 - bit_of(self.order(j, b)[s])) * self.rows[s] if s < self.halvings else 0

    def scatter_copies(self, j, s):
        ref, slot, _rows = self.held(j, s - 1)
        into, into_slot, rows = self.held(j, s)
        copies = []
        for b in range(self.subs[j]):
            start = self.give_start(j, b, s)
            if not isinstance(start, int):
                start = pl.multiple_of(start, 8)
            copies.append(
                pltpu.make_async_remote_copy(
                    src_ref=ref.at[slot, b, pl.ds(start, rows), :],
                    dst_ref=into.at[into_slot, b],
                    send_sem=self.send.at[s, into_slot, b],
                    recv_sem=self.recv.at[s, into_slot, b],
                    device_id=partner(self.order(j, b)[s]),
                    device_id_type=MESH,
                )
            )
        return copies

    def owned(self, j, s, flip=False):
        views = []
        for block, _from, count, target, row, col in self.pieces[j]:
            start = row
            for t in range(s + 1):
                bit = bit_of(self.order(j, block)[t])
                if flip and t == s:
                    bit = 1 - bit
                start = start + bit * self.rows[t]
            views.append(
                target.at[pl.ds(pl.multiple_of(start, 8), self.rows[s]), pl.ds(col, count)]
            )
        return views

    def final(self, j):
        ref, slot, rows = self.held(j, self.stages - 1)
        return [
            ref.at[slot, block, pl.ds(0, rows), pl.ds(from_col, count)]
            for block, from_col, count, _target, _row, _col in self.pieces[j]
        ]

    def gather_copies(self, j, s, arriving=False):
        last = s == self.halvings - 1
        sources = self.final(j) if last else self.owned(j, s)
        blocks = [piece[0] for piece in self.pieces[j]]
        return [
            pltpu.make_async_remote_copy(
                src_ref=source,
                dst_ref=target,
                send_sem=self.gsend.at[j, s, p],
                recv_sem=self.grecv.at[j, s, p],
                device_id=partner(self.order(j, blocks[p])[s]),
                device_id_type=MESH,
            )
            for p, (source, target) in enumerate(zip(sources, self.owned(j, s, flip=arriving)))
        ]

    def local_copies(self, j):
        pairs = zip(self.final(j), self.owned(j, self.halvings - 1))
        return [
            pltpu.make_async_copy(source, target, self.local.at[j, p])
            for p, (source, target) in enumerate(pairs)
        ]

    def sent(self, j, event, s):
        size = self.rows[s] * TILE * 4e-6
        for b in range(self.subs[j]):
            self.links.start((j, event, b), size, self.order(j, b)[s])
        self.due[j] = event

    def arrival(self, j):
        times = [self.links.arrived.get((j, self.due[j], b)) for b in range(self.subs[j])]
        return None if None in times else max(times)

    def first_due(self):
        times = {j: self.arrival(j) for j in self.due}
        times = {j: time for j, time in times.items() if time is not None}
        if not times:
            return None, None
        j = min(times, key=times.get)
        return j, times[j]

    def advance(self, us):
        self.links.forward(self.links.now + us)

    def run(self, j):
        while self.arrival(j) is None:
            self.links.forward()
        self.links.forward(max(self.links.now, self.arrival(j)))
        event = self.due.pop(j)
        for b in range(self.subs[j]):
            self.links.arrived.pop((j, event, b))
        n = self.stages
        if event < n:
            s = event
            for copy in self.scatter_copies(j, s):
                copy.wait_send()
                copy.wait_recv()
            self.add(j, s)
            if s > 0:
                self.give_credit(j, s - 1)
            if s < n - 1:
                self.start_scatter(j, s + 1)
            else:
                for copy in self.local_copies(j) + self.gather_copies(j, self.halvings - 1):
                    copy.start()
                self.sent(j, event + 1, self.halvings - 1)
        else:
            s = self.halvings - 1 - (event - n)
            for copy in self.gather_copies(j, s, True):
                copy.wait_recv()
            if s == self.halvings - 1:
                for copy in self.gather_copies(j, s):
                    copy.wait_send()
                for copy in self.local_copies(j):
                    copy.wait()
                self.give_credit(j, n - 1)
            if s > 0:
                for copy in self.gather_copies(j, s - 1):
                    copy.start()
                self.sent(j, event + 1, s - 1)
        self.done[j] = event
        self.advance(SERVICE)

    def add(self, j, s):
        ref, slot, _rows = self.held(j, s - 1)
        into, into_slot, rows = self.held(j, s)
        starts = [self.keep_start(j, b, s) for b in range(self.subs[j])]
        step = min(48, rows)

        @pl.loop(0, rows // step)
        def _(i):
            for b in range(self.subs[j]):
                here = pl.ds(pl.multiple_of(starts[b] + i * step, 8), step)
                there = pl.ds(pl.multiple_of(i * step, 8), step)
                into[into_slot, b, there, :] += ref[slot, b, here, :]

    def give_credit(self, j, s):
        after = j + self.slots
        if after < self.jobs:
            for b in range(self.subs[after]):
                pl.semaphore_signal(
                    self.credit.at[s, j % self.slots, b],
                    inc=1,
                    device_id=partner(self.order(after, b)[s]),
                    device_id_type=MESH,
                )

    def start_scatter(self, j, s):
        if j >= self.slots:
            self.reach(j - self.slots, s + 1)
            for b in range(self.subs[j]):
                pl.semaphore_wait(self.credit.at[s, j % self.slots, b], 1)
        for copy in self.scatter_copies(j, s):
            copy.start()
        self.sent(j, s, s)

    def reach(self, j, event):
        while self.done[j] < event:
            self.run(j)

    def acquire(self, j):
        if j >= TILES:
            self.reach(j - TILES, 0)
        return j % TILES

    def produced(self, j):
        self.start_scatter(j, 0)

    def tick(self, us=0.0):
        self.advance(us)
        while True:
            j, time = self.first_due()
            if j is None or time > self.links.now:
                break
            self.run(j)

    def drain(self):
        while self.due:
            j, _time = self.first_due()
            if j is None:
                self.links.forward()
            else:
                self.run(j)
        for j in range(self.jobs):
            for s in range(self.halvings - 1):
                for copy in self.gather_copies(j, s):
                    copy.wait_send()


class Refs(typing.NamedTuple):
    x: typing.Any
    cot: typing.Any
    lengths: typing.Any
    norm_gain: typing.Any
    norm_shift: typing.Any
    alpha: typing.Any
    delta: typing.Any
    beta: typing.Any
    eta: typing.Any
    omega_in: typing.Any
    b_output_in: typing.Any
    b_shrink_in: typing.Any
    b_value_in: typing.Any
    b_gates_in: typing.Any
    b_expand_in: typing.Any
    qk: typing.Any
    bias: typing.Any
    w_value: typing.Any
    w_gates: typing.Any
    w_output: typing.Any
    w_expand: typing.Any
    w_shrink: typing.Any
    out_hbm: typing.Any
    dx_hbm: typing.Any
    dw_value: typing.Any
    dw_gates: typing.Any
    dw_output: typing.Any
    dw_expand: typing.Any
    dw_shrink: typing.Any
    sums: typing.Any
    wa: typing.Any
    wb: typing.Any
    wg: typing.Any
    cot_v: typing.Any
    dx: typing.Any
    tables: typing.Any
    gains: typing.Any
    b_value: typing.Any
    b_gates: typing.Any
    b_expand: typing.Any
    normed: typing.Any
    vpre: typing.Any
    gate: typing.Any
    att: typing.Any
    hpre: typing.Any
    mid: typing.Any
    epre: typing.Any
    mpre: typing.Any
    dnorm: typing.Any
    probs: typing.Any
    square: typing.Any
    lh: typing.Any
    ll: typing.Any
    th: typing.Any
    tl: typing.Any
    s768: typing.Any
    s_value: typing.Any
    s_expand: typing.Any
    s_gates: typing.Any
    s_small: typing.Any
    ends: typing.Any
    starts: typing.Any
    e_recv: typing.Any
    f_recv: typing.Any
    wsem: typing.Any
    osem: typing.Any
    send: typing.Any
    recv: typing.Any
    send2: typing.Any
    recv2: typing.Any
    tile: typing.Any
    sems: typing.Any
    red: typing.Any


def kernel(batch, seq, *refs):
    n = len(Refs._fields) - 2
    r = Refs(*refs[:n], refs[n : n + 6], refs[n + 6 :])
    rows, width = r.x.shape
    seg_len = rows // SEG
    me_b, me = lax.axis_index("batch"), lax.axis_index("seq")
    nstate = 16
    hv = r.vpre.shape[1]
    ff = r.epre.shape[1]
    zd = r.qk.shape[1]
    group = r.probs.shape[1]
    groups = rows // group
    reset0 = width + zd
    cand0 = reset0 + hv
    gates = cand0 + width
    scale = 1.0 / math.sqrt(zd)

    sources = (r.w_value, r.w_gates, r.w_output, r.w_expand, r.w_shrink, r.w_output, r.w_value)
    places = (r.wa, r.wg, r.wb, r.wa, r.wb, r.wb, r.wa)
    weights = [
        pltpu.make_async_copy(a, b, r.wsem.at[i]) for i, (a, b) in enumerate(zip(sources, places))
    ]
    cot_copy = pltpu.make_async_copy(r.cot, r.cot_v, r.wsem.at[len(weights)])
    for copy in weights[:3] + [cot_copy]:
        copy.start()

    gate_cols = [i * TILE for i in range(width // TILE)]
    gate_cols += [reset0 + i * TILE for i in range((hv + width) // TILE)]

    def tall_job(ref, i):
        return [(b, 0, TILE, ref, b * BLOCK, i * TILE) for b in range(2)]

    def wide_job(ref, cols):
        return [(b, 0, TILE, ref, 0, cols[b]) for b in range(2)]

    pieces = [tall_job(r.dw_shrink, i) for i in range(width // TILE)]
    pieces += [wide_job(r.dw_expand, (i, i + TILE)) for i in range(0, ff, 2 * TILE)]
    pieces += [tall_job(r.dw_output, i) for i in range(width // TILE)]
    pieces += [wide_job(r.dw_value, (i, i + TILE)) for i in range(0, hv, 2 * TILE)]
    pieces += [wide_job(r.dw_gates, gate_cols[i : i + 2]) for i in range(0, len(gate_cols), 2)]
    pieces.append([(0, 0, zd, r.dw_gates, 0, width), (0, zd, TILE - zd, r.sums, 0, 0)])
    kinds = [KINDS[j % len(KINDS)] for j in range(len(pieces))]
    comm = Reducer(
        stage_orders(batch, seq), slot_count(seq), kinds, pieces, r.tile, r.red, r.sems
    )
    _core, chips, _line = bits_of(batch, seq)

    barrier = pltpu.get_barrier_semaphore()

    def greet(k, _):
        pl.semaphore_signal(
            barrier, inc=1, device_id=(me_b, lax.rem(me + k, seq)), device_id_type=MESH
        )
        return 0

    lax.fori_loop(1, seq, greet, 0)
    for bit in chips:
        pl.semaphore_signal(barrier, inc=1, device_id=partner(bit), device_id_type=MESH)

    alpha, damping = sigmoid(r.alpha[...]), sigmoid(r.delta[...])
    rate = alpha * damping
    series = jnp.full_like(rate, 1.0 / 7.0)
    for n in range(6, 0, -1):
        series = series * rate + 1.0 / n
    log_decay = -rate * series
    for i, value in enumerate(
        (
            1.0 - rate,
            alpha * r.beta[...] * r.eta[...],
            jnp.exp(seg_len * log_decay),
            jnp.exp(rows * log_decay),
        )
    ):
        r.tables[i] = value
    decay, coef, dec_seg, dec_all = (r.tables.at[i] for i in range(4))

    def unfold(source, target, row=0):
        for d in range(source.shape[0]):
            target[row : row + 1, d * LANES : (d + 1) * LANES] = source[d : d + 1, :]

    unfold(r.b_value_in, r.b_value)
    unfold(r.b_gates_in, r.b_gates)
    unfold(r.b_expand_in, r.b_expand)
    for i in range(2):
        r.gains[2 * i : 2 * i + 1, :] = r.norm_gain[i : i + 1, :]
        r.gains[2 * i + 1 : 2 * i + 2, :] = r.norm_shift[i : i + 1, :]
    for i, source in enumerate((r.omega_in, r.b_output_in, r.b_shrink_in)):
        unfold(source, r.gains, 4 + i)
    gain0, shift0, gain1, shift1, omega, b_output, b_shrink = (
        r.gains[i : i + 1, :] for i in range(7)
    )

    first_end = r.lengths[0, 0]
    second_end = first_end + r.lengths[0, 1]

    def keep(group_id):
        starts = (group_id == 0) | (group_id == first_end) | (group_id == second_end)
        return jnp.where(starts, 0.0, 1.0)

    def keep_block(k):
        value = keep(k * groups)
        for g in range(1, groups):
            value = value * keep(k * groups + g)
        return value

    keep_seg = [
        keep(me * groups + k * groups // SEG) if k % (SEG // groups) == 0 else 1.0
        for k in range(SEG)
    ]

    def tiles(count, body, us, parts=1):
        for p in range(parts):
            pl.loop(count * p // parts, count * (p + 1) // parts)(body)
            comm.tick(us / parts)

    def zero_small(i):
        r.s768[i : i + 1, :] = jnp.zeros((1, width), f32)

    for i in range(8):
        zero_small(i)

    def add768(i, value, cols=slice(None)):
        r.s768[i : i + 1, cols] += jnp.sum(value, axis=0, keepdims=True)

    RC = 32

    def norm_stats(value):
        centre = value - jnp.mean(value, axis=-1, keepdims=True)
        inv = lax.rsqrt(jnp.mean(centre * centre, axis=-1, keepdims=True) + 1e-05)
        return centre * inv, inv

    def norm_back(grad, n, inv):
        return inv * (
            grad
            - jnp.mean(grad, axis=-1, keepdims=True)
            - n * jnp.mean(grad * n, axis=-1, keepdims=True)
        )

    @pl.loop(0, rows // RC)
    def _(i):
        part = at(i, RC)
        n, _inv = norm_stats(r.x[part, :])
        value = n * gain0 + shift0
        row_set(r.normed, part, value)
        r.lh[part, :width], r.ll[part, :width] = split(value)

    def seg_rows(t):
        return pl.ds(t, SEG, stride=seg_len)

    def rows_of(ref, count, cols):
        return [jnp.broadcast_to(ref[n : n + 1, cols], (SEG, LANES)) for n in count]

    def end_states(source, reverse, target):
        @pl.loop(0, width // LANES)
        def _(d):
            cols = at(d, LANES)
            dec = rows_of(decay, range(nstate), cols)

            def turn(t, state):
                at_t = seg_len - 1 - t if reverse else t
                value = source[d, seg_rows(at_t), :]
                return tuple(a * s + value for a, s in zip(dec, state))

            zero = jnp.zeros((SEG, LANES), f32)
            state = lax.fori_loop(0, seg_len, turn, (zero,) * nstate, unroll=8)
            for n in range(nstate):
                target[d, n * SEG : (n + 1) * SEG, :] = state[n]

    def seg_of(k):
        return pl.ds(k, nstate, stride=SEG)

    def exchange(buffer, send_sem, recv_sem):
        def copy_to(k):
            peer = lax.rem(me + k, seq)
            return pltpu.make_async_remote_copy(
                src_ref=buffer.at[me],
                dst_ref=buffer.at[me],
                send_sem=send_sem.at[k],
                recv_sem=recv_sem.at[me],
                device_id=(me_b, peer),
                device_id_type=MESH,
            )

        def copy_from(k):
            peer = lax.rem(me + k, seq)
            return pltpu.make_async_remote_copy(
                src_ref=buffer.at[me],
                dst_ref=buffer.at[peer],
                send_sem=send_sem.at[k],
                recv_sem=recv_sem.at[peer],
                device_id=(me_b, peer),
                device_id_type=MESH,
            )

        def start():
            def one(k, _):
                copy_to(k).start()
                return 0

            lax.fori_loop(1, seq, one, 0)

        def wait():
            def one(k, _):
                copy_to(k).wait_send()
                copy_from(k).wait_recv()
                return 0

            lax.fori_loop(1, seq, one, 0)

        return start, wait

    end_states(r.normed, False, r.ends)
    total = jnp.zeros((nstate, width), f32)
    for k in range(SEG):
        total = keep_seg[k] * total * dec_seg[...] + row_get(r.ends, seg_of(k))
    r.e_recv[me] = total
    pl.semaphore_wait(barrier, seq - 1 + len(chips))
    start_e, wait_e = exchange(r.e_recv, r.send, r.recv)
    start_e()

    weights[0].wait()

    @pl.loop(0, hv // TILE)
    def _(i):
        c = at(i, TILE)
        w = r.wa[:, c]
        r.vpre[:, c] = (
            dot(r.lh[:, :width], w) + dot(r.ll[:, :width], w) + r.b_value[:, c]
        )

    weights[3].start()

    wait_e()

    def carry_step(k, carried):
        new = dec_all[...] * (keep_block(k) * carried) + r.e_recv[k]
        return jnp.where(k < me, new, carried)

    state = lax.fori_loop(0, seq, carry_step, jnp.zeros((nstate, width), f32))
    for k in range(SEG):
        state = keep_seg[k] * state
        row_set(r.starts, seg_of(k), state)
        if k < SEG - 1:
            state = dec_seg[...] * state + row_get(r.ends, seg_of(k))

    @pl.loop(0, width // LANES)
    def _(d):
        cols = at(d, LANES)
        dec = rows_of(decay, range(nstate), cols)
        mix = rows_of(coef, range(nstate), cols)

        def turn(t, state):
            value = r.normed[d, seg_rows(t), :]
            state = tuple(a * s + value for a, s in zip(dec, state))
            terms = [m * s for m, s in zip(mix, state)]
            while len(terms) > 1:
                terms = [a + b for a, b in zip(terms[::2], terms[1::2])]
            r.mpre[d, seg_rows(t), :] = terms[0]
            return state

        first = tuple(r.starts[d, n * SEG : (n + 1) * SEG, :] for n in range(nstate))
        lax.fori_loop(0, seg_len, turn, first, unroll=4)

    @pl.loop(0, rows // RC)
    def _(i):
        part = at(i, RC)
        value = row_get(r.mpre, part) + omega * row_get(r.normed, part)
        row_set(r.mpre, part, value)
        r.lh[part, :width], r.ll[part, :width] = split(silu(value))

    weights[1].wait()

    def gate_tile(c):
        w = r.wg[:, c]
        r.gate[:, c] = (
            dot(r.lh[:, :width], w) + dot(r.ll[:, :width], w) + r.b_gates[:, c]
        )

    @pl.loop(0, width // TILE)
    def _(i):
        gate_tile(at(i, TILE))

    gate_tile(pl.ds(width, zd))

    @pl.loop(0, (hv + width) // TILE)
    def _(i):
        gate_tile(off(reset0, i, TILE))

    lag = lax.broadcasted_iota(jnp.int32, (group, group), 0) - lax.broadcasted_iota(
        jnp.int32, (group, group), 1
    )
    row_id = lax.broadcasted_iota(jnp.int32, (group, group), 0)
    causal = lag >= 0
    table = jnp.broadcast_to(r.bias[...], (group, group))
    for b in range(group.bit_length() - 1):
        moved = pltpu.roll(table, 1 << b, 1)
        table = jnp.where((row_id & (1 << b)) != 0, moved, table)
    q_gain, k_gain, q_shift = (r.qk[i : i + 1, :] for i in range(3))
    r.square[...] = table.T

    @pl.loop(0, groups)
    def _(g):
        part = at(g, group)
        shared = silu(r.gate[part, width:reset0])
        q = split(shared * q_gain + q_shift)
        k = split(shared * k_gain)
        scores = dot3(q, k, NT) * scale + r.square[...]
        scores = jnp.where(causal, scores, -1e30)
        p = jnp.exp(scores - jnp.max(scores, axis=-1, keepdims=True))
        p = p / jnp.sum(p, axis=-1, keepdims=True)
        r.probs[part, :] = p
        p = split(p)

        @pl.loop(0, hv // TILE)
        def _(i):
            c = at(i, TILE)
            v = split(silu(r.vpre[part, c]))
            attended = dot3(p, v)
            r.att[part, c] = attended
            gated = attended * silu(r.gate[part, off(reset0, i, TILE)])
            r.lh[part, c], r.ll[part, c] = split(gated)

    weights[2].wait()

    @pl.loop(0, width // TILE)
    def _(i):
        c = at(i, TILE)
        w = r.wb[:, c]
        value = (
            dot(r.lh[...], w)
            + dot(r.ll[...], w)
            + (r.gate[:, off(cand0, i, TILE)] + r.gains[5:6, c])
        )
        r.hpre[:, c] = value
        x = r.x[:, c]
        r.mid[:, c] = x + sigmoid(r.gate[:, c]) * (silu(value) - x)

    weights[4].start()

    @pl.loop(0, rows // RC)
    def _(i):
        part = at(i, RC)
        n, _inv = norm_stats(r.mid[part, :])
        r.lh[part, :width], r.ll[part, :width] = split(n * gain1 + shift1)

    weights[3].wait()

    @pl.loop(0, ff // TILE)
    def _(i):
        c = at(i, TILE)
        w = r.wa[:, c]
        r.epre[:, c] = (
            dot(r.lh[:, :width], w) + dot(r.ll[:, :width], w) + r.b_expand[:, c]
        )

    comm.advance(50.0)
    cot_copy.wait()

    def transposed(source, count, first=0):
        @pl.loop(0, count // LANES)
        def _(i):
            here = off(first, i, LANES)
            r.th[here, :], r.tl[here, :] = split(source(i, at(i, LANES)).T)

    def products(j, pairs):
        slot = comm.acquire(j)
        for b, (first, grad) in enumerate(pairs):
            g = split(grad)
            cols = grad.shape[1]

            @pl.loop(0, BLOCK // TILE)
            def _(k):
                a = off(first, k, TILE)
                value = dot3((r.th[a, :], r.tl[a, :]), g)
                if cols == TILE:
                    r.tile[slot, b, at(k, TILE), :] = value
                else:
                    r.tile[slot, b, at(k, TILE), :cols] = value

        comm.advance(1.0 * len(pairs))
        return slot

    def tall(j, grad):
        products(j, [(0, grad), (BLOCK, grad)])
        comm.produced(j)
        comm.tick()

    def wide(j, first, left, right):
        products(j, [(first, left), (first, right)])
        comm.produced(j)
        comm.tick()

    def cols_of(ref, i, start=0):
        return ref[:, start + i * TILE : start + (i + 1) * TILE]

    transposed(lambda i, c: silu(r.epre[:, c]), ff)
    comm.advance(2.0)
    for i in range(width // TILE):
        tall(i, cols_of(r.cot_v, i))

    def inner_halves(i):
        c = at(i, TILE)
        r.lh[:, c], r.ll[:, c] = split(silu(r.epre[:, c]))

    tiles(ff // TILE, inner_halves, 1.2)
    weights[4].wait()

    def out_tile(i):
        c = at(i, TILE)
        w = r.wb[:, c]
        r.dx[:, c] = r.mid[:, c] + (dot(r.lh[...], w) + dot(r.ll[...], w) + r.gains[6:7, c])

    tiles(width // TILE, out_tile, 3.0)
    out_copy = pltpu.make_async_copy(r.dx, r.out_hbm, r.osem.at[0])
    out_copy.start()

    def cot_halves(i):
        part = at(i, RC)
        value = r.cot_v[part, :]
        add768(6, value)
        r.lh[part, :width], r.ll[part, :width] = split(value)

    tiles(rows // RC, cot_halves, 1.0)

    def inner_back(i):
        c = at(i, TILE)
        w = r.wb[c, :]
        value = (dot(r.lh[:, :width], w, NT) + dot(r.ll[:, :width], w, NT)) * dsilu(
            r.epre[:, c]
        )
        r.epre[:, c] = value
        r.s_expand[:, c] = jnp.sum(value, axis=0, keepdims=True)

    tiles(ff // TILE, inner_back, 3.2)
    weights[5].start()

    def expand_halves(i):
        c = at(i, TILE)
        r.lh[:, c], r.ll[:, c] = split(r.epre[:, c])

    tiles(ff // TILE, expand_halves, 0.8)

    @pl.loop(0, rows // RC)
    def _(i):
        part = at(i, RC)
        n, _inv = norm_stats(r.mid[part, :])
        row_set(r.dnorm, part, n * gain1 + shift1)

    transposed(lambda i, c: r.dnorm[i], width)
    comm.tick(2.0)
    for i in range(ff // (2 * TILE)):
        wide(3 + i, 0, cols_of(r.epre, 2 * i), cols_of(r.epre, 2 * i + 1))

    out_copy.wait()

    @pl.loop(0, width // TILE)
    def _(i):
        c = at(i, TILE)
        w = r.wa[c, :]
        r.dx[:, c] = dot(r.lh[...], w, NT) + dot(r.ll[...], w, NT)

    weights[6].start()
    comm.tick(3.0)

    def middle_back(i):
        part = at(i, RC)
        grad = r.dx[part, :]
        n, inv = norm_stats(r.mid[part, :])
        add768(2, grad * n)
        add768(3, grad)
        dmid = r.cot_v[part, :] + norm_back(grad * gain1, n, inv)
        update = sigmoid(r.gate[part, :width])
        pre = r.hpre[part, :]
        x = r.x[part, :]
        dhpre = dmid * update * dsilu(pre)
        r.dx[part, :] = dmid * (1.0 - update)
        dupdate = dmid * (silu(pre) - x) * (update * (1.0 - update))
        r.gate[part, :width] = dupdate
        r.gate[part, cand0:] = dhpre
        r.lh[part, :width], r.ll[part, :width] = split(dhpre)
        r.s_gates[:, :width] = (
            jnp.where(i == 0, 0.0, r.s_gates[:, :width])
            + jnp.sum(dupdate, axis=0, keepdims=True)
        )
        add768(5, dhpre)

    tiles(rows // RC, middle_back, 5.0, 2)

    transposed(lambda i, c: r.att[:, c] * silu(r.gate[:, off(reset0, i, LANES)]), hv)
    weights[5].wait()
    comm.tick(3.0)
    for i in range(width // TILE):
        tall(6 + i, cols_of(r.gate, i, cand0))

    def attended_back(i):
        c = at(i, TILE)
        w = r.wb[c, :]
        gated = dot(r.lh[:, :width], w, NT) + dot(r.ll[:, :width], w, NT)
        here = off(reset0, i, TILE)
        pre = r.gate[:, here]
        dreset = gated * r.att[:, c] * dsilu(pre)
        r.att[:, c] = gated * silu(pre)
        r.gate[:, here] = dreset
        r.s_gates[:, here] = jnp.sum(dreset, axis=0, keepdims=True)

    tiles(hv // TILE, attended_back, 3.5)

    r.s_small[...] = jnp.zeros_like(r.s_small)
    r.square[...] = jnp.zeros((group, group), f32)

    def attention_back(g):
        part = at(g, group)
        p = r.probs[part, :]
        p_t = split(p.T)

        def value_tile(i, dp):
            c = at(i, TILE)
            pre = r.vpre[part, c]
            d_att = split(r.att[part, c])
            r.vpre[part, c] = dot3(p_t, d_att) * dsilu(pre)
            return dp + dot3(d_att, split(silu(pre)), NT)

        dp = lax.fori_loop(0, hv // TILE, value_tile, jnp.zeros((group, group), f32))
        ds = p * (dp - jnp.sum(dp * p, axis=-1, keepdims=True))
        r.square[...] += ds
        ds = ds * scale
        pre = r.gate[part, width:reset0]
        shared = silu(pre)
        dq = dot3(split(ds), split(shared * k_gain))
        dk = dot3(split(ds.T), split(shared * q_gain + q_shift))
        for n, value in enumerate((dq * shared, dk * shared, dq)):
            r.s_small[n : n + 1, :] += jnp.sum(value, axis=0, keepdims=True)
        r.gate[part, width:reset0] = (dq * q_gain + dk * k_gain) * dsilu(pre)

    tiles(groups, attention_back, 8.4, 4)
    diagonals = r.square[...].T
    for b in range(group.bit_length() - 1):
        moved = pltpu.roll(diagonals, group - (1 << b), 1)
        diagonals = jnp.where((row_id & (1 << b)) != 0, moved, diagonals)
    r.s_small[3:4, :] = jnp.sum(diagonals, axis=0, keepdims=True)
    r.s_gates[:, width:reset0] = jnp.sum(r.gate[:, width:reset0], axis=0, keepdims=True)
    r.s_gates[:, cand0:] = r.s768[5:6, :]

    comm.tick(0.5)
    weights[6].wait()

    @pl.loop(0, hv // TILE)
    def _(i):
        c = at(i, TILE)
        value = r.vpre[:, c]
        r.s_value[:, c] = jnp.sum(value, axis=0, keepdims=True)
        r.lh[:, c], r.ll[:, c] = split(value)

    @pl.loop(0, width // TILE)
    def _(i):
        c = at(i, TILE)
        w = r.wa[c, :]
        col_set(r.dnorm, i, dot(r.lh[...], w, NT) + dot(r.ll[...], w, NT))

    comm.tick(4.2)
    transposed(lambda i, c: r.normed[i], width, width)
    transposed(lambda i, c: silu(r.mpre[i]), width)
    comm.tick(2.5)

    def gate_section(start, size, first, last):
        @pl.loop(0, size // LANES)
        def _(i):
            c = at(i, LANES)
            r.lh[:, c], r.ll[:, c] = split(r.gate[:, off(start, i, LANES)])

        @pl.loop(0, width // TILE)
        def _(i):
            c = at(i, TILE)
            w = r.wg[c, start : start + size]
            value = dot(r.lh[:, :size], w, NT) + dot(r.ll[:, :size], w, NT)
            if not first:
                value += r.att[:, c]
            if last:
                value = value * dsilu(col_get(r.mpre, i))
                col_set(r.mpre, i, value)
                add768(4, value * col_get(r.normed, i), c)
                col_set(r.dnorm, i, col_get(r.dnorm, i) + r.gains[4:5, c] * value)
            else:
                r.att[:, c] = value

        comm.tick(size * 8.0 / gates)

    gate_section(0, reset0, True, False)
    gate_section(reset0, hv, False, False)
    gate_section(cand0, width, False, True)

    for i in range(hv // (2 * TILE)):
        wide(9 + i, width, cols_of(r.vpre, 2 * i), cols_of(r.vpre, 2 * i + 1))
    for i in range(len(gate_cols) // 2):
        left, right = gate_cols[2 * i : 2 * i + 2]
        wide(12 + i, 0, cols_of(r.gate, 0, left), cols_of(r.gate, 0, right))

    end_states(r.mpre, True, r.ends)
    adj = jnp.zeros((nstate, width), f32)
    for k in reversed(range(SEG)):
        if k < SEG - 1:
            adj = dec_seg[...] * (keep_seg[k + 1] * adj)
        adj = adj + row_get(r.ends, seg_of(k))
    r.f_recv[me] = adj
    start_f, wait_f = exchange(r.f_recv, r.send2, r.recv2)
    start_f()

    comm.tick(4.0)
    wait_f()
    comm.tick(7.0)

    def adj_step(j, carried):
        k = seq - 1 - j
        new = keep(k * groups) * r.f_recv[k] + dec_all[...] * (keep_block(k) * carried)
        return jnp.where(k > me, new, carried)

    adj = lax.fori_loop(0, seq, adj_step, jnp.zeros((nstate, width), f32))
    for k in reversed(range(SEG)):
        fresh = row_get(r.ends, seg_of(k))
        row_set(r.ends, seg_of(k), adj)
        if k > 0:
            adj = keep_seg[k] * (dec_seg[...] * adj + fresh)

    half = nstate // 2
    for h in range(2):
        states = range(h * half, (h + 1) * half)

        def average_back(d):
            cols = at(d, LANES)
            dec = rows_of(decay, states, cols)
            mix = rows_of(coef, states, cols)

            def ahead(t, state):
                value = r.normed[d, seg_rows(t), :]
                for n in range(half):
                    r.epre[at(t, SEG), n * LANES : (n + 1) * LANES] = state[n]
                return tuple(a * s + value for a, s in zip(dec, state))

            first = tuple(r.starts[d, n * SEG : (n + 1) * SEG, :] for n in states)
            lax.fori_loop(0, seg_len, ahead, first, unroll=4)

            def back(j, carried):
                t = seg_len - 1 - j
                adj, p_sum, q_sum = carried
                grad = r.mpre[d, seg_rows(t), :]
                value = r.normed[d, seg_rows(t), :]
                adj = tuple(a * s + grad for a, s in zip(dec, adj))
                p_sum = tuple(p + a * value for p, a in zip(p_sum, adj))
                q_sum = tuple(
                    q + a * r.epre[at(t, SEG), n * LANES : (n + 1) * LANES]
                    for n, (q, a) in enumerate(zip(q_sum, adj))
                )
                terms = [m * a for m, a in zip(mix, adj)]
                while len(terms) > 1:
                    terms = [a + b for a, b in zip(terms[::2], terms[1::2])]
                r.dnorm[d, seg_rows(t), :] += terms[0]
                return adj, p_sum, q_sum

            zero = (jnp.zeros((SEG, LANES), f32),) * half
            last = tuple(r.ends[d, n * SEG : (n + 1) * SEG, :] for n in states)
            _adj, p_sum, q_sum = lax.fori_loop(0, seg_len, back, (last, zero, zero), unroll=4)
            for n in range(half):
                row = 8 + h * half + n
                r.s768[row : row + 1, cols] = jnp.sum(p_sum[n], axis=0, keepdims=True)
                row = row + nstate
                r.s768[row : row + 1, cols] = jnp.sum(q_sum[n], axis=0, keepdims=True)

        tiles(width // LANES, average_back, 12.0, 6)

    def first_back(i):
        part = at(i, RC)
        grad = row_get(r.dnorm, part)
        n, inv = norm_stats(r.x[part, :])
        add768(0, grad * n)
        add768(1, grad)
        r.dx[part, :] += norm_back(grad * gain0, n, inv)

    tiles(rows // RC, first_back, 3.0)
    dx_copy = pltpu.make_async_copy(r.dx, r.dx_hbm, r.osem.at[1])
    dx_copy.start()

    slot = products(comm.jobs - 1, [(0, r.gate[:, width:reset0])])
    r.tile[slot, 0, :, zd:] = jnp.zeros((BLOCK, TILE - zd), f32)
    place = 0

    def put(value):
        nonlocal place
        count = value.shape[0]
        r.tile[slot, 0, place : place + count, zd:] = value
        place += count

    for d in range(width // LANES):
        put(r.s768[:, d * LANES : (d + 1) * LANES])
    put(r.s_small[...])
    for ref in (r.s_value, r.s_expand, r.s_gates):
        for d in range(ref.shape[1] // LANES):
            put(ref[:, d * LANES : (d + 1) * LANES])
    comm.produced(comm.jobs - 1)
    comm.drain()
    dx_copy.wait()


def finish(sums, alpha, delta, beta, eta, *outs):
    gain, shift, d_alpha, d_delta, d_beta, d_eta, omega, b_output, b_shrink = outs[:9]
    qk, bias, b_value, b_expand, b_gates = outs[9:]
    nstate, width = alpha.shape
    tall_rows = 8 + 2 * nstate
    for d in range(width // LANES):
        cols = slice(d * LANES, (d + 1) * LANES)
        row = d * tall_rows
        for n in range(2):
            gain[n : n + 1, cols] = sums[row + 2 * n : row + 2 * n + 1, :]
            shift[n : n + 1, cols] = sums[row + 2 * n + 1 : row + 2 * n + 2, :]
        for n, target in enumerate((omega, b_output, b_shrink)):
            target[d : d + 1, :] = sums[row + 4 + n : row + 5 + n, :]
        p_sum = sums[row + 8 : row + 8 + nstate, :]
        q_sum = sums[row + 8 + nstate : row + 8 + 2 * nstate, :]
        rate, damping = sigmoid(alpha[:, cols]), sigmoid(delta[:, cols])
        d_inflow = eta[:, cols] * p_sum
        d_eta[:, cols] = rate * beta[:, cols] * p_sum
        d_decay = eta[:, cols] * (rate * beta[:, cols]) * q_sum
        d_rate = d_inflow * beta[:, cols] - d_decay * damping
        d_alpha[:, cols] = d_rate * rate * (1.0 - rate)
        d_delta[:, cols] = -d_decay * rate * damping * (1.0 - damping)
        d_beta[:, cols] = d_inflow * rate
    place = width // LANES * tall_rows
    qk[...] = sums[place : place + 3, :]
    bias[...] = sums[place + 3 : place + 4, :]
    place += 8
    for target in (b_value, b_expand, b_gates):
        target[...] = sums[place : place + target.shape[0], :]
        place += target.shape[0]


def layer(operands, batch, seq):
    rows, width = operands[0].shape
    w_value, w_gates, w_output, w_expand, w_shrink = operands[-5:]
    hv, gates, ff = w_value.shape[1], w_gates.shape[1], w_expand.shape[1]
    zd, group, nstate = operands[15].shape[1], operands[16].shape[1], operands[5].shape[0]
    vmem = pl.BlockSpec(memory_space=pltpu.VMEM)
    smem = pl.BlockSpec(memory_space=pltpu.SMEM)
    hbm = pl.BlockSpec(memory_space=pl.ANY)
    stages, slots = len(stage_orders(batch, seq)[0]), slot_count(seq)

    def shape(*dims, kind=f32):
        return jax.ShapeDtypeStruct(dims, kind)

    return pl.pallas_call(
        functools.partial(kernel, batch, seq),
        out_shape=(
            shape(rows, width),
            shape(rows, width),
            shape(width, hv),
            shape(width, gates),
            shape(hv, width),
            shape(width, ff),
            shape(ff, width),
            shape(BLOCK, TILE - zd),
        ),
        in_specs=[vmem, hbm, smem] + [vmem] * 14 + [hbm] * 5,
        out_specs=(hbm,) * 8,
        scratch_shapes=[
            pltpu.VMEM(w_value.shape, bf16),
            pltpu.VMEM(w_output.shape, bf16),
            pltpu.VMEM(w_gates.shape, bf16),
            pltpu.VMEM((rows, width), f32),
            pltpu.VMEM((rows, width), f32),
            pltpu.VMEM((4, nstate, width), f32),
            pltpu.VMEM((8, width), f32),
            pltpu.VMEM((1, hv), f32),
            pltpu.VMEM((1, gates), f32),
            pltpu.VMEM((1, ff), f32),
            pltpu.VMEM((width // LANES, rows, LANES), f32),
            pltpu.VMEM((rows, hv), f32),
            pltpu.VMEM((rows, gates), f32),
            pltpu.VMEM((rows, hv), f32),
            pltpu.VMEM((rows, width), f32),
            pltpu.VMEM((rows, width), f32),
            pltpu.VMEM((rows, ff), f32),
            pltpu.VMEM((width // LANES, rows, LANES), f32),
            pltpu.VMEM((width // LANES, rows, LANES), f32),
            pltpu.VMEM((rows, group), f32),
            pltpu.VMEM((group, group), f32),
            pltpu.VMEM((rows, max(hv, ff)), bf16),
            pltpu.VMEM((rows, max(hv, ff)), bf16),
            pltpu.VMEM((max(hv, ff), rows), bf16),
            pltpu.VMEM((max(hv, ff), rows), bf16),
            pltpu.VMEM((8 + 2 * nstate, width), f32),
            pltpu.VMEM((1, hv), f32),
            pltpu.VMEM((1, ff), f32),
            pltpu.VMEM((1, gates), f32),
            pltpu.VMEM((8, zd), f32),
            pltpu.VMEM((width // LANES, nstate * SEG, LANES), f32),
            pltpu.VMEM((width // LANES, nstate * SEG, LANES), f32),
            pltpu.VMEM((seq, nstate, width), f32),
            pltpu.VMEM((seq, nstate, width), f32),
            pltpu.SemaphoreType.DMA((8,)),
            pltpu.SemaphoreType.DMA((2,)),
            pltpu.SemaphoreType.DMA((seq,)),
            pltpu.SemaphoreType.DMA((seq,)),
            pltpu.SemaphoreType.DMA((seq,)),
            pltpu.SemaphoreType.DMA((seq,)),
            pltpu.VMEM((TILES, 2, BLOCK, TILE), f32),
            pltpu.SemaphoreType.DMA((stages, slots, 2)),
            pltpu.SemaphoreType.DMA((stages, slots, 2)),
            pltpu.SemaphoreType.REGULAR((stages, slots, 2)),
            pltpu.SemaphoreType.DMA((JOBS, 2)),
            pltpu.SemaphoreType.DMA((JOBS, HALVINGS, 2)),
            pltpu.SemaphoreType.DMA((JOBS, HALVINGS, 2)),
        ]
        + [pltpu.VMEM((slots, 2, count, TILE), f32) for count in stage_rows(stages)],
        compiler_params=pltpu.CompilerParams(
            collective_id=0, has_side_effects=True, vmem_limit_bytes=63 << 20
        ),
        cost_estimate=pl.CostEstimate(
            flops=52_000_000_000, bytes_accessed=60_000_000, transcendentals=20_000_000
        ),
    )(*operands)


def shards(
    batch,
    seq,
    tokens,
    lengths,
    cotangent,
    norm_gain,
    norm_shift,
    alpha_logit,
    delta_logit,
    ema_beta,
    ema_eta,
    ema_omega,
    w_value,
    b_value,
    w_gates,
    b_gates,
    query_key,
    position_bias,
    w_output,
    b_output,
    w_expand,
    b_expand,
    w_shrink,
    b_shrink,
):
    def lines(vector):
        return vector.reshape(-1, LANES)

    averages = (alpha_logit.T, delta_logit.T, ema_beta.T, ema_eta.T)
    operands = (tokens[0], cotangent[0], lengths, norm_gain.T, norm_shift.T) + averages
    operands += (lines(ema_omega), lines(b_output), lines(b_shrink))
    operands += (lines(b_value), lines(b_gates), lines(b_expand))
    operands += (query_key.T, position_bias[None])
    operands += (w_value, w_gates, w_output, w_expand, w_shrink)
    output, grad_tokens, dw_value, dw_gates, dw_output, dw_expand, dw_shrink, sums = layer(
        operands, batch, seq
    )
    like = (norm_gain.T, norm_shift.T) + averages
    like += (lines(ema_omega), lines(b_output), lines(b_shrink), query_key.T)
    like += (position_bias[None], lines(b_value), lines(b_expand), lines(b_gates))
    small = pl.pallas_call(
        finish, out_shape=tuple(jax.ShapeDtypeStruct(a.shape, f32) for a in like)
    )(sums, *averages)
    gain, shift, d_alpha, d_delta, d_beta, d_eta, d_omega, d_output, d_shrink = small[:9]
    d_qk, d_bias, d_value, d_expand, d_gates = small[9:]
    return (
        output[None],
        grad_tokens[None],
        gain.T,
        shift.T,
        d_alpha.T,
        d_delta.T,
        d_beta.T,
        d_eta.T,
        d_omega.reshape(-1),
        dw_value,
        d_value.reshape(-1),
        dw_gates,
        d_gates.reshape(-1),
        d_qk.T,
        d_bias[0],
        dw_output,
        d_output.reshape(-1),
        dw_expand,
        d_expand.reshape(-1),
        dw_shrink,
        d_shrink.reshape(-1),
    )


def solution(mesh):
    token_spec = P("batch", "seq", None)
    return jax.shard_map(
        functools.partial(shards, mesh.shape["batch"], mesh.shape["seq"]),
        mesh=mesh,
        in_specs=(token_spec, P("batch", None), token_spec) + (P(),) * 19,
        out_specs=(token_spec, token_spec) + (P(),) * 19,
        check_vma=False,
    )
```

```python
import functools
import math
import typing

import jax
import jax.numpy as jnp
from jax import lax
from jax.experimental import pallas as pl
from jax.experimental.pallas import tpu as pltpu
from jax.sharding import PartitionSpec as P

f32 = jnp.float32
bf16 = jnp.bfloat16
MESH = pl.DeviceIdType.MESH

SEG = 8
LANES = 128
TILE = 256

NN = (((1,), (0,)), ((), ()))
NT = (((1,), (1,)), ((), ()))


def split(value):
    high = value.astype(bf16)
    return high, (value - high.astype(f32)).astype(bf16)


def dot(a, b, dims=NN):
    return lax.dot_general(a, b, dims, preferred_element_type=f32)


def dot3(a, b, dims=NN):
    a_high, a_low = a
    b_high, b_low = b
    return dot(a_high, b_high, dims) + (dot(a_high, b_low, dims) + dot(a_low, b_high, dims))


def sigmoid(value):
    return 1.0 / (1.0 + jnp.exp(-value))


def silu(value):
    return value * sigmoid(value)


def dsilu(value):
    s = sigmoid(value)
    return s * (1.0 + value * (1.0 - s))


def row_get(ref, part):
    return jnp.concatenate([ref[d, part, :] for d in range(ref.shape[0])], axis=-1)


def row_set(ref, part, value):
    for d in range(ref.shape[0]):
        ref[d, part, :] = value[:, d * LANES : (d + 1) * LANES]


def col_get(ref, i, size=TILE):
    n = size // LANES
    return jnp.concatenate([ref[i * n + k] for k in range(n)], axis=-1)


def col_set(ref, i, value):
    n = value.shape[1] // LANES
    for k in range(n):
        ref[i * n + k] = value[:, k * LANES : (k + 1) * LANES]


def at(i, size):
    return pl.ds(pl.multiple_of(i * size, size), size)


def off(start, i, size):
    return pl.ds(pl.multiple_of(start + i * size, LANES), size)


def bit_of(bit):
    name, step = bit
    return lax.rem(lax.div(lax.axis_index(name), step), 2)


def partner(bit):
    name, step = bit
    where = {"batch": lax.axis_index("batch"), "seq": lax.axis_index("seq")}
    where[name] = where[name] + step * (1 - 2 * bit_of(bit))
    return (where["batch"], where["seq"])


HALVINGS = 5
BLOCK = 768
TILES = 2
SERVICE = 0.5
JOBS = 19
KINDS = ((0, 3), (1, 0), (0, 3), (0, 1), (0, 3), (1, 2), (0, 1), (0, 0), (0, 1), (1, 0), (0, 1), (1, 0), (1, 3), (0, 1), (0, 3), (1, 0), (0, 2), (1, 3), (1, 1))


def slot_count(seq):
    return 8 if seq <= 16 else 4


def bits_of(batch, seq):
    chips = [("batch", 1 << k) for k in range(batch.bit_length() - 1)]
    line = [("seq", 1 << k) for k in range(1, seq.bit_length() - 1)]
    return ("seq", 1), chips, line


def stage_orders(batch, seq):
    core, chips, line = bits_of(batch, seq)
    flipped = chips[::-1]
    return (
        [core] + chips + line,
        [core] + flipped + line,
        [core] + line + chips,
        [core] + line + flipped,
    )


def stage_rows(count):
    return [BLOCK >> (min(s, HALVINGS - 1) + 1) for s in range(count)]


class Links:
    LATENCY = 5.06
    CORE, LINE = 0.6, 0.041

    def __init__(self):
        self.now = 0.0
        self.active = {}
        self.arrived = {}

    def uses(self, bit):
        name, step = bit
        if bit == ("seq", 1):
            return (("core", 1),)
        if name == "batch":
            return ((name + str(step), 1),)
        return (("ends", 1),) if step == 2 else (("ends", 1), ("middle", 2))

    def start(self, key, size, bit):
        self.active[key] = [size, self.uses(bit)]

    def rates(self):
        load = {}
        for _size, uses in self.active.values():
            for link, weight in uses:
                load[link] = load.get(link, 0) + weight
        return {
            key: min((self.CORE if link == "core" else self.LINE) / load[link] for link, _w in uses)
            for key, (_size, uses) in self.active.items()
        }

    def forward(self, until=None):
        while self.active:
            rates = self.rates()
            key = min(self.active, key=lambda k: self.active[k][0] / rates[k])
            step = self.active[key][0] / rates[key]
            if until is not None and self.now + step > until:
                step = until - self.now
                key = None
            for k in self.active:
                self.active[k][0] -= step * rates[k]
            self.now += step
            if key is None:
                return
            del self.active[key]
            self.arrived[key] = self.now + self.LATENCY
            if until is None:
                return
        if until is not None:
            self.now = max(self.now, until)


class Reducer:
    def __init__(self, orders, slots, kinds, pieces, tile, red, sems):
        self.slots = slots
        self.orders, self.kinds, self.pieces = orders, kinds, pieces
        self.subs = [max(p[0] for p in job) + 1 for job in pieces]
        self.tile, self.red = tile, red
        self.send, self.recv, self.credit, self.local, self.gsend, self.grecv = sems
        self.stages = len(orders[0])
        self.halvings = min(HALVINGS, self.stages)
        self.rows = stage_rows(self.stages)
        self.jobs = len(pieces)
        self.links = Links()
        self.due = {}
        self.done = [-1] * self.jobs

    def order(self, j, b):
        return self.orders[self.kinds[j][b]]

    def held(self, j, s):
        if s < 0:
            return self.tile, j % TILES, BLOCK
        return self.red[s], j % self.slots, self.rows[s]

    def keep_start(self, j, b, s):
        return bit_of(self.order(j, b)[s]) * self.rows[s] if s < self.halvings else 0

    def give_start(self, j, b, s):
        return (1 - bit_of(self.order(j, b)[s])) * self.rows[s] if s < self.halvings else 0

    def scatter_copies(self, j, s):
        ref, slot, _rows = self.held(j, s - 1)
        into, into_slot, rows = self.held(j, s)
        copies = []
        for b in range(self.subs[j]):
            start = self.give_start(j, b, s)
            if not isinstance(start, int):
                start = pl.multiple_of(start, 8)
            copies.append(
                pltpu.make_async_remote_copy(
                    src_ref=ref.at[slot, b, pl.ds(start, rows), :],
                    dst_ref=into.at[into_slot, b],
                    send_sem=self.send.at[s, into_slot, b],
                    recv_sem=self.recv.at[s, into_slot, b],
                    device_id=partner(self.order(j, b)[s]),
                    device_id_type=MESH,
                )
            )
        return copies

    def owned(self, j, s, flip=False):
        views = []
        for block, _from, count, target, row, col in self.pieces[j]:
            start = row
            for t in range(s + 1):
                bit = bit_of(self.order(j, block)[t])
                if flip and t == s:
                    bit = 1 - bit
                start = start + bit * self.rows[t]
            views.append(
                target.at[pl.ds(pl.multiple_of(start, 8), self.rows[s]), pl.ds(col, count)]
            )
        return views

    def final(self, j):
        ref, slot, rows = self.held(j, self.stages - 1)
        return [
            ref.at[slot, block, pl.ds(0, rows), pl.ds(from_col, count)]
            for block, from_col, count, _target, _row, _col in self.pieces[j]
        ]

    def gather_copies(self, j, s, arriving=False):
        last = s == self.halvings - 1
        sources = self.final(j) if last else self.owned(j, s)
        blocks = [piece[0] for piece in self.pieces[j]]
        return [
            pltpu.make_async_remote_copy(
                src_ref=source,
                dst_ref=target,
                send_sem=self.gsend.at[j, s, p],
                recv_sem=self.grecv.at[j, s, p],
                device_id=partner(self.order(j, blocks[p])[s]),
                device_id_type=MESH,
            )
            for p, (source, target) in enumerate(zip(sources, self.owned(j, s, flip=arriving)))
        ]

    def local_copies(self, j):
        pairs = zip(self.final(j), self.owned(j, self.halvings - 1))
        return [
            pltpu.make_async_copy(source, target, self.local.at[j, p])
            for p, (source, target) in enumerate(pairs)
        ]

    def sent(self, j, event, s):
        size = self.rows[s] * TILE * 4e-6
        for b in range(self.subs[j]):
            self.links.start((j, event, b), size, self.order(j, b)[s])
        self.due[j] = event

    def arrival(self, j):
        times = [self.links.arrived.get((j, self.due[j], b)) for b in range(self.subs[j])]
        return None if None in times else max(times)

    def first_due(self):
        times = {j: self.arrival(j) for j in self.due}
        times = {j: time for j, time in times.items() if time is not None}
        if not times:
            return None, None
        j = min(times, key=times.get)
        return j, times[j]

    def advance(self, us):
        self.links.forward(self.links.now + us)

    def run(self, j):
        while self.arrival(j) is None:
            self.links.forward()
        self.links.forward(max(self.links.now, self.arrival(j)))
        event = self.due.pop(j)
        for b in range(self.subs[j]):
            self.links.arrived.pop((j, event, b))
        n = self.stages
        if event < n:
            s = event
            for copy in self.scatter_copies(j, s):
                copy.wait_send()
                copy.wait_recv()
            self.add(j, s)
            if s > 0:
                self.give_credit(j, s - 1)
            if s < n - 1:
                self.start_scatter(j, s + 1)
            else:
                for copy in self.local_copies(j) + self.gather_copies(j, self.halvings - 1):
                    copy.start()
                self.sent(j, event + 1, self.halvings - 1)
        else:
            s = self.halvings - 1 - (event - n)
            for copy in self.gather_copies(j, s, True):
                copy.wait_recv()
            if s == self.halvings - 1:
                for copy in self.gather_copies(j, s):
                    copy.wait_send()
                for copy in self.local_copies(j):
                    copy.wait()
                self.give_credit(j, n - 1)
            if s > 0:
                for copy in self.gather_copies(j, s - 1):
                    copy.start()
                self.sent(j, event + 1, s - 1)
        self.done[j] = event
        self.advance(SERVICE)

    def add(self, j, s):
        ref, slot, _rows = self.held(j, s - 1)
        into, into_slot, rows = self.held(j, s)
        starts = [self.keep_start(j, b, s) for b in range(self.subs[j])]
        step = min(48, rows)

        @pl.loop(0, rows // step)
        def _(i):
            for b in range(self.subs[j]):
                here = pl.ds(pl.multiple_of(starts[b] + i * step, 8), step)
                there = pl.ds(pl.multiple_of(i * step, 8), step)
                into[into_slot, b, there, :] += ref[slot, b, here, :]

    def give_credit(self, j, s):
        after = j + self.slots
        if after < self.jobs:
            for b in range(self.subs[after]):
                pl.semaphore_signal(
                    self.credit.at[s, j % self.slots, b],
                    inc=1,
                    device_id=partner(self.order(after, b)[s]),
                    device_id_type=MESH,
                )

    def start_scatter(self, j, s):
        if j >= self.slots:
            self.reach(j - self.slots, s + 1)
            for b in range(self.subs[j]):
                pl.semaphore_wait(self.credit.at[s, j % self.slots, b], 1)
        for copy in self.scatter_copies(j, s):
            copy.start()
        self.sent(j, s, s)

    def reach(self, j, event):
        while self.done[j] < event:
            self.run(j)

    def acquire(self, j):
        if j >= TILES:
            self.reach(j - TILES, 0)
        return j % TILES

    def produced(self, j):
        self.start_scatter(j, 0)

    def tick(self, us=0.0):
        self.advance(us)
        while True:
            j, time = self.first_due()
            if j is None or time > self.links.now:
                break
            self.run(j)

    def drain(self):
        while self.due:
            j, _time = self.first_due()
            if j is None:
                self.links.forward()
            else:
                self.run(j)
        for j in range(self.jobs):
            for s in range(self.halvings - 1):
                for copy in self.gather_copies(j, s):
                    copy.wait_send()


class Refs(typing.NamedTuple):
    x: typing.Any
    cot: typing.Any
    lengths: typing.Any
    norm_gain: typing.Any
    norm_shift: typing.Any
    alpha: typing.Any
    delta: typing.Any
    beta: typing.Any
    eta: typing.Any
    omega_in: typing.Any
    b_output_in: typing.Any
    b_shrink_in: typing.Any
    b_value_in: typing.Any
    b_gates_in: typing.Any
    b_expand_in: typing.Any
    qk: typing.Any
    bias: typing.Any
    w_value: typing.Any
    w_gates: typing.Any
    w_output: typing.Any
    w_expand: typing.Any
    w_shrink: typing.Any
    out_hbm: typing.Any
    dx_hbm: typing.Any
    dw_value: typing.Any
    dw_gates: typing.Any
    dw_output: typing.Any
    dw_expand: typing.Any
    dw_shrink: typing.Any
    sums: typing.Any
    wa: typing.Any
    wb: typing.Any
    wg: typing.Any
    cot_v: typing.Any
    dx: typing.Any
    tables: typing.Any
    gains: typing.Any
    b_value: typing.Any
    b_gates: typing.Any
    b_expand: typing.Any
    normed: typing.Any
    vpre: typing.Any
    gate: typing.Any
    att: typing.Any
    hpre: typing.Any
    mid: typing.Any
    epre: typing.Any
    mpre: typing.Any
    dnorm: typing.Any
    probs: typing.Any
    square: typing.Any
    lh: typing.Any
    ll: typing.Any
    th: typing.Any
    tl: typing.Any
    s768: typing.Any
    s_value: typing.Any
    s_expand: typing.Any
    s_gates: typing.Any
    s_small: typing.Any
    ends: typing.Any
    starts: typing.Any
    e_recv: typing.Any
    f_recv: typing.Any
    wsem: typing.Any
    osem: typing.Any
    send: typing.Any
    recv: typing.Any
    send2: typing.Any
    recv2: typing.Any
    tile: typing.Any
    sems: typing.Any
    red: typing.Any


def kernel(batch, seq, *refs):
    n = len(Refs._fields) - 2
    r = Refs(*refs[:n], refs[n : n + 6], refs[n + 6 :])
    rows, width = r.x.shape
    seg_len = rows // SEG
    me_b, me = lax.axis_index("batch"), lax.axis_index("seq")
    nstate = 16
    hv = r.vpre.shape[1]
    ff = r.epre.shape[1]
    zd = r.qk.shape[1]
    group = r.probs.shape[1]
    groups = rows // group
    reset0 = width + zd
    cand0 = reset0 + hv
    gates = cand0 + width
    scale = 1.0 / math.sqrt(zd)

    sources = (r.w_value, r.w_gates, r.w_output, r.w_expand, r.w_shrink, r.w_output, r.w_value)
    places = (r.wa, r.wg, r.wb, r.wa, r.wb, r.wb, r.wa)
    weights = [
        pltpu.make_async_copy(a, b, r.wsem.at[i]) for i, (a, b) in enumerate(zip(sources, places))
    ]
    cot_copy = pltpu.make_async_copy(r.cot, r.cot_v, r.wsem.at[len(weights)])
    for copy in weights[:3] + [cot_copy]:
        copy.start()

    gate_cols = [i * TILE for i in range(width // TILE)]
    gate_cols += [reset0 + i * TILE for i in range((hv + width) // TILE)]

    def tall_job(ref, i):
        return [(b, 0, TILE, ref, b * BLOCK, i * TILE) for b in range(2)]

    def wide_job(ref, cols):
        return [(b, 0, TILE, ref, 0, cols[b]) for b in range(2)]

    pieces = [tall_job(r.dw_shrink, i) for i in range(width // TILE)]
    pieces += [wide_job(r.dw_expand, (i, i + TILE)) for i in range(0, ff, 2 * TILE)]
    pieces += [tall_job(r.dw_output, i) for i in range(width // TILE)]
    pieces += [wide_job(r.dw_value, (i, i + TILE)) for i in range(0, hv, 2 * TILE)]
    pieces += [wide_job(r.dw_gates, gate_cols[i : i + 2]) for i in range(0, len(gate_cols), 2)]
    pieces.append([(0, 0, zd, r.dw_gates, 0, width), (0, zd, TILE - zd, r.sums, 0, 0)])
    kinds = [KINDS[j % len(KINDS)] for j in range(len(pieces))]
    comm = Reducer(
        stage_orders(batch, seq), slot_count(seq), kinds, pieces, r.tile, r.red, r.sems
    )
    _core, chips, _line = bits_of(batch, seq)

    barrier = pltpu.get_barrier_semaphore()

    def greet(k, _):
        pl.semaphore_signal(
            barrier, inc=1, device_id=(me_b, lax.rem(me + k, seq)), device_id_type=MESH
        )
        return 0

    lax.fori_loop(1, seq, greet, 0)
    for bit in chips:
        pl.semaphore_signal(barrier, inc=1, device_id=partner(bit), device_id_type=MESH)

    alpha, damping = sigmoid(r.alpha[...]), sigmoid(r.delta[...])
    rate = alpha * damping
    series = jnp.full_like(rate, 1.0 / 7.0)
    for n in range(6, 0, -1):
        series = series * rate + 1.0 / n
    log_decay = -rate * series
    for i, value in enumerate(
        (
            1.0 - rate,
            alpha * r.beta[...] * r.eta[...],
            jnp.exp(seg_len * log_decay),
            jnp.exp(rows * log_decay),
        )
    ):
        r.tables[i] = value
    decay, coef, dec_seg, dec_all = (r.tables.at[i] for i in range(4))

    def unfold(source, target, row=0):
        for d in range(source.shape[0]):
            target[row : row + 1, d * LANES : (d + 1) * LANES] = source[d : d + 1, :]

    unfold(r.b_value_in, r.b_value)
    unfold(r.b_gates_in, r.b_gates)
    unfold(r.b_expand_in, r.b_expand)
    for i in range(2):
        r.gains[2 * i : 2 * i + 1, :] = r.norm_gain[i : i + 1, :]
        r.gains[2 * i + 1 : 2 * i + 2, :] = r.norm_shift[i : i + 1, :]
    for i, source in enumerate((r.omega_in, r.b_output_in, r.b_shrink_in)):
        unfold(source, r.gains, 4 + i)
    gain0, shift0, gain1, shift1, omega, b_output, b_shrink = (
        r.gains[i : i + 1, :] for i in range(7)
    )

    first_end = r.lengths[0, 0]
    second_end = first_end + r.lengths[0, 1]

    def keep(group_id):
        starts = (group_id == 0) | (group_id == first_end) | (group_id == second_end)
        return jnp.where(starts, 0.0, 1.0)

    def keep_block(k):
        value = keep(k * groups)
        for g in range(1, groups):
            value = value * keep(k * groups + g)
        return value

    keep_seg = [
        keep(me * groups + k * groups // SEG) if k % (SEG // groups) == 0 else 1.0
        for k in range(SEG)
    ]

    def tiles(count, body, us, parts=1):
        for p in range(parts):
            pl.loop(count * p // parts, count * (p + 1) // parts)(body)
            comm.tick(us / parts)

    def zero_small(i):
        r.s768[i : i + 1, :] = jnp.zeros((1, width), f32)

    for i in range(8):
        zero_small(i)

    def add768(i, value, cols=slice(None)):
        r.s768[i : i + 1, cols] += jnp.sum(value, axis=0, keepdims=True)

    RC = 64

    def norm_stats(value):
        centre = value - jnp.mean(value, axis=-1, keepdims=True)
        inv = lax.rsqrt(jnp.mean(centre * centre, axis=-1, keepdims=True) + 1e-05)
        return centre * inv, inv

    def norm_back(grad, n, inv):
        return inv * (
            grad
            - jnp.mean(grad, axis=-1, keepdims=True)
            - n * jnp.mean(grad * n, axis=-1, keepdims=True)
        )

    @pl.loop(0, rows // RC)
    def _(i):
        part = at(i, RC)
        n, _inv = norm_stats(r.x[part, :])
        value = n * gain0 + shift0
        row_set(r.normed, part, value)
        r.lh[part, :width], r.ll[part, :width] = split(value)

    def seg_rows(t):
        return pl.ds(t, SEG, stride=seg_len)

    def rows_of(ref, count, cols):
        return [jnp.broadcast_to(ref[n : n + 1, cols], (SEG, LANES)) for n in count]

    def end_states(source, reverse, target):
        @pl.loop(0, width // LANES)
        def _(d):
            cols = at(d, LANES)
            dec = rows_of(decay, range(nstate), cols)

            def turn(t, state):
                at_t = seg_len - 1 - t if reverse else t
                value = source[d, seg_rows(at_t), :]
                return tuple(a * s + value for a, s in zip(dec, state))

            zero = jnp.zeros((SEG, LANES), f32)
            state = lax.fori_loop(0, seg_len, turn, (zero,) * nstate, unroll=8)
            for n in range(nstate):
                target[d, n * SEG : (n + 1) * SEG, :] = state[n]

    def seg_of(k):
        return pl.ds(k, nstate, stride=SEG)

    def exchange(buffer, send_sem, recv_sem):
        def copy_to(k):
            peer = lax.rem(me + k, seq)
            return pltpu.make_async_remote_copy(
                src_ref=buffer.at[me],
                dst_ref=buffer.at[me],
                send_sem=send_sem.at[k],
                recv_sem=recv_sem.at[me],
                device_id=(me_b, peer),
                device_id_type=MESH,
            )

        def copy_from(k):
            peer = lax.rem(me + k, seq)
            return pltpu.make_async_remote_copy(
                src_ref=buffer.at[me],
                dst_ref=buffer.at[peer],
                send_sem=send_sem.at[k],
                recv_sem=recv_sem.at[peer],
                device_id=(me_b, peer),
                device_id_type=MESH,
            )

        def start():
            def one(k, _):
                copy_to(k).start()
                return 0

            lax.fori_loop(1, seq, one, 0)

        def wait():
            def one(k, _):
                copy_to(k).wait_send()
                copy_from(k).wait_recv()
                return 0

            lax.fori_loop(1, seq, one, 0)

        return start, wait

    end_states(r.normed, False, r.ends)
    total = jnp.zeros((nstate, width), f32)
    for k in range(SEG):
        total = keep_seg[k] * total * dec_seg[...] + row_get(r.ends, seg_of(k))
    r.e_recv[me] = total
    pl.semaphore_wait(barrier, seq - 1 + len(chips))
    start_e, wait_e = exchange(r.e_recv, r.send, r.recv)
    start_e()

    weights[0].wait()

    @pl.loop(0, hv // TILE)
    def _(i):
        c = at(i, TILE)
        w = r.wa[:, c]
        r.vpre[:, c] = (
            dot(r.lh[:, :width], w) + dot(r.ll[:, :width], w) + r.b_value[:, c]
        )

    weights[3].start()

    wait_e()

    def carry_step(k, carried):
        new = dec_all[...] * (keep_block(k) * carried) + r.e_recv[k]
        return jnp.where(k < me, new, carried)

    state = lax.fori_loop(0, seq, carry_step, jnp.zeros((nstate, width), f32))
    for k in range(SEG):
        state = keep_seg[k] * state
        row_set(r.starts, seg_of(k), state)
        if k < SEG - 1:
            state = dec_seg[...] * state + row_get(r.ends, seg_of(k))

    @pl.loop(0, width // LANES)
    def _(d):
        cols = at(d, LANES)
        dec = rows_of(decay, range(nstate), cols)
        mix = rows_of(coef, range(nstate), cols)

        def turn(t, state):
            value = r.normed[d, seg_rows(t), :]
            state = tuple(a * s + value for a, s in zip(dec, state))
            terms = [m * s for m, s in zip(mix, state)]
            while len(terms) > 1:
                terms = [a + b for a, b in zip(terms[::2], terms[1::2])]
            r.mpre[d, seg_rows(t), :] = terms[0]
            return state

        first = tuple(r.starts[d, n * SEG : (n + 1) * SEG, :] for n in range(nstate))
        lax.fori_loop(0, seg_len, turn, first, unroll=4)

    @pl.loop(0, rows // RC)
    def _(i):
        part = at(i, RC)
        value = row_get(r.mpre, part) + omega * row_get(r.normed, part)
        row_set(r.mpre, part, value)
        r.lh[part, :width], r.ll[part, :width] = split(silu(value))

    weights[1].wait()

    def gate_tile(c):
        w = r.wg[:, c]
        r.gate[:, c] = (
            dot(r.lh[:, :width], w) + dot(r.ll[:, :width], w) + r.b_gates[:, c]
        )

    @pl.loop(0, width // TILE)
    def _(i):
        gate_tile(at(i, TILE))

    gate_tile(pl.ds(width, zd))

    @pl.loop(0, (hv + width) // TILE)
    def _(i):
        gate_tile(off(reset0, i, TILE))

    lag = lax.broadcasted_iota(jnp.int32, (group, group), 0) - lax.broadcasted_iota(
        jnp.int32, (group, group), 1
    )
    row_id = lax.broadcasted_iota(jnp.int32, (group, group), 0)
    causal = lag >= 0
    table = jnp.broadcast_to(r.bias[...], (group, group))
    for b in range(group.bit_length() - 1):
        moved = pltpu.roll(table, 1 << b, 1)
        table = jnp.where((row_id & (1 << b)) != 0, moved, table)
    q_gain, k_gain, q_shift = (r.qk[i : i + 1, :] for i in range(3))
    r.square[...] = table.T

    @pl.loop(0, groups)
    def _(g):
        part = at(g, group)
        shared = silu(r.gate[part, width:reset0])
        q = split(shared * q_gain + q_shift)
        k = split(shared * k_gain)
        scores = dot3(q, k, NT) * scale + r.square[...]
        scores = jnp.where(causal, scores, -1e30)
        p = jnp.exp(scores - jnp.max(scores, axis=-1, keepdims=True))
        p = p / jnp.sum(p, axis=-1, keepdims=True)
        r.probs[part, :] = p
        p = split(p)

        @pl.loop(0, hv // TILE)
        def _(i):
            c = at(i, TILE)
            v = split(silu(r.vpre[part, c]))
            attended = dot3(p, v)
            r.att[part, c] = attended
            gated = attended * silu(r.gate[part, off(reset0, i, TILE)])
            r.lh[part, c], r.ll[part, c] = split(gated)

    weights[2].wait()

    @pl.loop(0, width // TILE)
    def _(i):
        c = at(i, TILE)
        w = r.wb[:, c]
        value = (
            dot(r.lh[...], w)
            + dot(r.ll[...], w)
            + (r.gate[:, off(cand0, i, TILE)] + r.gains[5:6, c])
        )
        r.hpre[:, c] = value
        x = r.x[:, c]
        r.mid[:, c] = x + sigmoid(r.gate[:, c]) * (silu(value) - x)

    weights[4].start()

    @pl.loop(0, rows // RC)
    def _(i):
        part = at(i, RC)
        n, _inv = norm_stats(r.mid[part, :])
        r.lh[part, :width], r.ll[part, :width] = split(n * gain1 + shift1)

    weights[3].wait()

    @pl.loop(0, ff // TILE)
    def _(i):
        c = at(i, TILE)
        w = r.wa[:, c]
        r.epre[:, c] = (
            dot(r.lh[:, :width], w) + dot(r.ll[:, :width], w) + r.b_expand[:, c]
        )

    comm.advance(50.0)
    cot_copy.wait()

    def transposed(source, count, first=0):
        @pl.loop(0, count // LANES)
        def _(i):
            here = off(first, i, LANES)
            r.th[here, :], r.tl[here, :] = split(source(i, at(i, LANES)).T)

    def products(j, pairs):
        slot = comm.acquire(j)
        for b, (first, grad) in enumerate(pairs):
            g = split(grad)
            cols = grad.shape[1]

            @pl.loop(0, BLOCK // TILE)
            def _(k):
                a = off(first, k, TILE)
                value = dot3((r.th[a, :], r.tl[a, :]), g)
                if cols == TILE:
                    r.tile[slot, b, at(k, TILE), :] = value
                else:
                    r.tile[slot, b, at(k, TILE), :cols] = value

        comm.advance(1.0 * len(pairs))
        return slot

    def tall(j, grad):
        products(j, [(0, grad), (BLOCK, grad)])
        comm.produced(j)
        comm.tick()

    def wide(j, first, left, right):
        products(j, [(first, left), (first, right)])
        comm.produced(j)
        comm.tick()

    def cols_of(ref, i, start=0):
        return ref[:, start + i * TILE : start + (i + 1) * TILE]

    transposed(lambda i, c: silu(r.epre[:, c]), ff)
    comm.advance(2.0)
    for i in range(width // TILE):
        tall(i, cols_of(r.cot_v, i))

    def inner_halves(i):
        c = at(i, TILE)
        r.lh[:, c], r.ll[:, c] = split(silu(r.epre[:, c]))

    tiles(ff // TILE, inner_halves, 1.2)
    weights[4].wait()

    def out_tile(i):
        c = at(i, TILE)
        w = r.wb[:, c]
        r.dx[:, c] = r.mid[:, c] + (dot(r.lh[...], w) + dot(r.ll[...], w) + r.gains[6:7, c])

    tiles(width // TILE, out_tile, 3.0)
    out_copy = pltpu.make_async_copy(r.dx, r.out_hbm, r.osem.at[0])
    out_copy.start()

    def cot_halves(i):
        part = at(i, RC)
        value = r.cot_v[part, :]
        add768(6, value)
        r.lh[part, :width], r.ll[part, :width] = split(value)

    tiles(rows // RC, cot_halves, 1.0)

    def inner_back(i):
        c = at(i, TILE)
        w = r.wb[c, :]
        value = (dot(r.lh[:, :width], w, NT) + dot(r.ll[:, :width], w, NT)) * dsilu(
            r.epre[:, c]
        )
        r.epre[:, c] = value
        r.s_expand[:, c] = jnp.sum(value, axis=0, keepdims=True)

    tiles(ff // TILE, inner_back, 3.2)
    weights[5].start()

    def expand_halves(i):
        c = at(i, TILE)
        r.lh[:, c], r.ll[:, c] = split(r.epre[:, c])

    tiles(ff // TILE, expand_halves, 0.8)

    @pl.loop(0, rows // RC)
    def _(i):
        part = at(i, RC)
        n, _inv = norm_stats(r.mid[part, :])
        row_set(r.dnorm, part, n * gain1 + shift1)

    transposed(lambda i, c: r.dnorm[i], width)
    comm.tick(2.0)
    for i in range(ff // (2 * TILE)):
        wide(3 + i, 0, cols_of(r.epre, 2 * i), cols_of(r.epre, 2 * i + 1))

    out_copy.wait()

    @pl.loop(0, width // TILE)
    def _(i):
        c = at(i, TILE)
        w = r.wa[c, :]
        r.dx[:, c] = dot(r.lh[...], w, NT) + dot(r.ll[...], w, NT)

    weights[6].start()
    comm.tick(3.0)

    def middle_back(i):
        part = at(i, RC)
        grad = r.dx[part, :]
        n, inv = norm_stats(r.mid[part, :])
        add768(2, grad * n)
        add768(3, grad)
        dmid = r.cot_v[part, :] + norm_back(grad * gain1, n, inv)
        update = sigmoid(r.gate[part, :width])
        pre = r.hpre[part, :]
        x = r.x[part, :]
        dhpre = dmid * update * dsilu(pre)
        r.dx[part, :] = dmid * (1.0 - update)
        dupdate = dmid * (silu(pre) - x) * (update * (1.0 - update))
        r.gate[part, :width] = dupdate
        r.gate[part, cand0:] = dhpre
        r.lh[part, :width], r.ll[part, :width] = split(dhpre)
        r.s_gates[:, :width] = (
            jnp.where(i == 0, 0.0, r.s_gates[:, :width])
            + jnp.sum(dupdate, axis=0, keepdims=True)
        )
        add768(5, dhpre)

    tiles(rows // RC, middle_back, 5.0, 2)

    transposed(lambda i, c: r.att[:, c] * silu(r.gate[:, off(reset0, i, LANES)]), hv)
    weights[5].wait()
    comm.tick(3.0)
    for i in range(width // TILE):
        tall(6 + i, cols_of(r.gate, i, cand0))

    def attended_back(i):
        c = at(i, TILE)
        w = r.wb[c, :]
        gated = dot(r.lh[:, :width], w, NT) + dot(r.ll[:, :width], w, NT)
        here = off(reset0, i, TILE)
        pre = r.gate[:, here]
        dreset = gated * r.att[:, c] * dsilu(pre)
        r.att[:, c] = gated * silu(pre)
        r.gate[:, here] = dreset
        r.s_gates[:, here] = jnp.sum(dreset, axis=0, keepdims=True)

    tiles(hv // TILE, attended_back, 3.5)

    r.s_small[...] = jnp.zeros_like(r.s_small)
    r.square[...] = jnp.zeros((group, group), f32)

    def attention_back(g):
        part = at(g, group)
        p = r.probs[part, :]
        p_t = split(p.T)

        def value_tile(i, dp):
            c = at(i, TILE)
            pre = r.vpre[part, c]
            d_att = split(r.att[part, c])
            r.vpre[part, c] = dot3(p_t, d_att) * dsilu(pre)
            return dp + dot3(d_att, split(silu(pre)), NT)

        dp = lax.fori_loop(0, hv // TILE, value_tile, jnp.zeros((group, group), f32))
        ds = p * (dp - jnp.sum(dp * p, axis=-1, keepdims=True))
        r.square[...] += ds
        ds = ds * scale
        pre = r.gate[part, width:reset0]
        shared = silu(pre)
        dq = dot3(split(ds), split(shared * k_gain))
        dk = dot3(split(ds.T), split(shared * q_gain + q_shift))
        for n, value in enumerate((dq * shared, dk * shared, dq)):
            r.s_small[n : n + 1, :] += jnp.sum(value, axis=0, keepdims=True)
        r.gate[part, width:reset0] = (dq * q_gain + dk * k_gain) * dsilu(pre)

    tiles(groups, attention_back, 8.4, 4)
    diagonals = r.square[...].T
    for b in range(group.bit_length() - 1):
        moved = pltpu.roll(diagonals, group - (1 << b), 1)
        diagonals = jnp.where((row_id & (1 << b)) != 0, moved, diagonals)
    r.s_small[3:4, :] = jnp.sum(diagonals, axis=0, keepdims=True)
    r.s_gates[:, width:reset0] = jnp.sum(r.gate[:, width:reset0], axis=0, keepdims=True)
    r.s_gates[:, cand0:] = r.s768[5:6, :]

    comm.tick(0.5)
    weights[6].wait()

    @pl.loop(0, hv // TILE)
    def _(i):
        c = at(i, TILE)
        value = r.vpre[:, c]
        r.s_value[:, c] = jnp.sum(value, axis=0, keepdims=True)
        r.lh[:, c], r.ll[:, c] = split(value)

    @pl.loop(0, width // TILE)
    def _(i):
        c = at(i, TILE)
        w = r.wa[c, :]
        col_set(r.dnorm, i, dot(r.lh[...], w, NT) + dot(r.ll[...], w, NT))

    comm.tick(4.2)
    transposed(lambda i, c: r.normed[i], width, width)
    transposed(lambda i, c: silu(r.mpre[i]), width)
    comm.tick(2.5)

    def gate_section(start, size, first, last):
        @pl.loop(0, size // LANES)
        def _(i):
            c = at(i, LANES)
            r.lh[:, c], r.ll[:, c] = split(r.gate[:, off(start, i, LANES)])

        @pl.loop(0, width // TILE)
        def _(i):
            c = at(i, TILE)
            w = r.wg[c, start : start + size]
            value = dot(r.lh[:, :size], w, NT) + dot(r.ll[:, :size], w, NT)
            if not first:
                value += r.att[:, c]
            if last:
                value = value * dsilu(col_get(r.mpre, i))
                col_set(r.mpre, i, value)
                add768(4, value * col_get(r.normed, i), c)
                col_set(r.dnorm, i, col_get(r.dnorm, i) + r.gains[4:5, c] * value)
            else:
                r.att[:, c] = value

        comm.tick(size * 8.0 / gates)

    gate_section(0, reset0, True, False)
    gate_section(reset0, hv, False, False)
    gate_section(cand0, width, False, True)

    for i in range(hv // (2 * TILE)):
        wide(9 + i, width, cols_of(r.vpre, 2 * i), cols_of(r.vpre, 2 * i + 1))
    for i in range(len(gate_cols) // 2):
        left, right = gate_cols[2 * i : 2 * i + 2]
        wide(12 + i, 0, cols_of(r.gate, 0, left), cols_of(r.gate, 0, right))

    end_states(r.mpre, True, r.ends)
    adj = jnp.zeros((nstate, width), f32)
    for k in reversed(range(SEG)):
        if k < SEG - 1:
            adj = dec_seg[...] * (keep_seg[k + 1] * adj)
        adj = adj + row_get(r.ends, seg_of(k))
    r.f_recv[me] = adj
    start_f, wait_f = exchange(r.f_recv, r.send2, r.recv2)
    start_f()

    comm.tick(4.0)
    wait_f()
    comm.tick(7.0)

    def adj_step(j, carried):
        k = seq - 1 - j
        new = keep(k * groups) * r.f_recv[k] + dec_all[...] * (keep_block(k) * carried)
        return jnp.where(k > me, new, carried)

    adj = lax.fori_loop(0, seq, adj_step, jnp.zeros((nstate, width), f32))
    for k in reversed(range(SEG)):
        fresh = row_get(r.ends, seg_of(k))
        row_set(r.ends, seg_of(k), adj)
        if k > 0:
            adj = keep_seg[k] * (dec_seg[...] * adj + fresh)

    half = nstate // 2
    for h in range(2):
        states = range(h * half, (h + 1) * half)

        def average_back(d):
            cols = at(d, LANES)
            dec = rows_of(decay, states, cols)
            mix = rows_of(coef, states, cols)

            def ahead(t, state):
                value = r.normed[d, seg_rows(t), :]
                for n in range(half):
                    r.epre[at(t, SEG), n * LANES : (n + 1) * LANES] = state[n]
                return tuple(a * s + value for a, s in zip(dec, state))

            first = tuple(r.starts[d, n * SEG : (n + 1) * SEG, :] for n in states)
            lax.fori_loop(0, seg_len, ahead, first, unroll=4)

            def back(j, carried):
                t = seg_len - 1 - j
                adj, p_sum, q_sum = carried
                grad = r.mpre[d, seg_rows(t), :]
                value = r.normed[d, seg_rows(t), :]
                adj = tuple(a * s + grad for a, s in zip(dec, adj))
                p_sum = tuple(p + a * value for p, a in zip(p_sum, adj))
                q_sum = tuple(
                    q + a * r.epre[at(t, SEG), n * LANES : (n + 1) * LANES]
                    for n, (q, a) in enumerate(zip(q_sum, adj))
                )
                terms = [m * a for m, a in zip(mix, adj)]
                while len(terms) > 1:
                    terms = [a + b for a, b in zip(terms[::2], terms[1::2])]
                r.dnorm[d, seg_rows(t), :] += terms[0]
                return adj, p_sum, q_sum

            zero = (jnp.zeros((SEG, LANES), f32),) * half
            last = tuple(r.ends[d, n * SEG : (n + 1) * SEG, :] for n in states)
            _adj, p_sum, q_sum = lax.fori_loop(0, seg_len, back, (last, zero, zero), unroll=4)
            for n in range(half):
                row = 8 + h * half + n
                r.s768[row : row + 1, cols] = jnp.sum(p_sum[n], axis=0, keepdims=True)
                row = row + nstate
                r.s768[row : row + 1, cols] = jnp.sum(q_sum[n], axis=0, keepdims=True)

        tiles(width // LANES, average_back, 12.0, 6)

    def first_back(i):
        part = at(i, RC)
        grad = row_get(r.dnorm, part)
        n, inv = norm_stats(r.x[part, :])
        add768(0, grad * n)
        add768(1, grad)
        r.dx[part, :] += norm_back(grad * gain0, n, inv)

    tiles(rows // RC, first_back, 3.0)
    dx_copy = pltpu.make_async_copy(r.dx, r.dx_hbm, r.osem.at[1])
    dx_copy.start()

    slot = products(comm.jobs - 1, [(0, r.gate[:, width:reset0])])
    r.tile[slot, 0, :, zd:] = jnp.zeros((BLOCK, TILE - zd), f32)
    place = 0

    def put(value):
        nonlocal place
        count = value.shape[0]
        r.tile[slot, 0, place : place + count, zd:] = value
        place += count

    for d in range(width // LANES):
        put(r.s768[:, d * LANES : (d + 1) * LANES])
    put(r.s_small[...])
    for ref in (r.s_value, r.s_expand, r.s_gates):
        for d in range(ref.shape[1] // LANES):
            put(ref[:, d * LANES : (d + 1) * LANES])
    comm.produced(comm.jobs - 1)
    comm.drain()
    dx_copy.wait()


def finish(sums, alpha, delta, beta, eta, *outs):
    gain, shift, d_alpha, d_delta, d_beta, d_eta, omega, b_output, b_shrink = outs[:9]
    qk, bias, b_value, b_expand, b_gates = outs[9:]
    nstate, width = alpha.shape
    tall_rows = 8 + 2 * nstate
    for d in range(width // LANES):
        cols = slice(d * LANES, (d + 1) * LANES)
        row = d * tall_rows
        for n in range(2):
            gain[n : n + 1, cols] = sums[row + 2 * n : row + 2 * n + 1, :]
            shift[n : n + 1, cols] = sums[row + 2 * n + 1 : row + 2 * n + 2, :]
        for n, target in enumerate((omega, b_output, b_shrink)):
            target[d : d + 1, :] = sums[row + 4 + n : row + 5 + n, :]
        p_sum = sums[row + 8 : row + 8 + nstate, :]
        q_sum = sums[row + 8 + nstate : row + 8 + 2 * nstate, :]
        rate, damping = sigmoid(alpha[:, cols]), sigmoid(delta[:, cols])
        d_inflow = eta[:, cols] * p_sum
        d_eta[:, cols] = rate * beta[:, cols] * p_sum
        d_decay = eta[:, cols] * (rate * beta[:, cols]) * q_sum
        d_rate = d_inflow * beta[:, cols] - d_decay * damping
        d_alpha[:, cols] = d_rate * rate * (1.0 - rate)
        d_delta[:, cols] = -d_decay * rate * damping * (1.0 - damping)
        d_beta[:, cols] = d_inflow * rate
    place = width // LANES * tall_rows
    qk[...] = sums[place : place + 3, :]
    bias[...] = sums[place + 3 : place + 4, :]
    place += 8
    for target in (b_value, b_expand, b_gates):
        target[...] = sums[place : place + target.shape[0], :]
        place += target.shape[0]


def layer(operands, batch, seq):
    rows, width = operands[0].shape
    w_value, w_gates, w_output, w_expand, w_shrink = operands[-5:]
    hv, gates, ff = w_value.shape[1], w_gates.shape[1], w_expand.shape[1]
    zd, group, nstate = operands[15].shape[1], operands[16].shape[1], operands[5].shape[0]
    vmem = pl.BlockSpec(memory_space=pltpu.VMEM)
    smem = pl.BlockSpec(memory_space=pltpu.SMEM)
    hbm = pl.BlockSpec(memory_space=pl.ANY)
    stages, slots = len(stage_orders(batch, seq)[0]), slot_count(seq)

    def shape(*dims, kind=f32):
        return jax.ShapeDtypeStruct(dims, kind)

    return pl.pallas_call(
        functools.partial(kernel, batch, seq),
        out_shape=(
            shape(rows, width),
            shape(rows, width),
            shape(width, hv),
            shape(width, gates),
            shape(hv, width),
            shape(width, ff),
            shape(ff, width),
            shape(BLOCK, TILE - zd),
        ),
        in_specs=[vmem, hbm, smem] + [vmem] * 14 + [hbm] * 5,
        out_specs=(hbm,) * 8,
        scratch_shapes=[
            pltpu.VMEM(w_value.shape, bf16),
            pltpu.VMEM(w_output.shape, bf16),
            pltpu.VMEM(w_gates.shape, bf16),
            pltpu.VMEM((rows, width), f32),
            pltpu.VMEM((rows, width), f32),
            pltpu.VMEM((4, nstate, width), f32),
            pltpu.VMEM((8, width), f32),
            pltpu.VMEM((1, hv), f32),
            pltpu.VMEM((1, gates), f32),
            pltpu.VMEM((1, ff), f32),
            pltpu.VMEM((width // LANES, rows, LANES), f32),
            pltpu.VMEM((rows, hv), f32),
            pltpu.VMEM((rows, gates), f32),
            pltpu.VMEM((rows, hv), f32),
            pltpu.VMEM((rows, width), f32),
            pltpu.VMEM((rows, width), f32),
            pltpu.VMEM((rows, ff), f32),
            pltpu.VMEM((width // LANES, rows, LANES), f32),
            pltpu.VMEM((width // LANES, rows, LANES), f32),
            pltpu.VMEM((rows, group), f32),
            pltpu.VMEM((group, group), f32),
            pltpu.VMEM((rows, max(hv, ff)), bf16),
            pltpu.VMEM((rows, max(hv, ff)), bf16),
            pltpu.VMEM((max(hv, ff), rows), bf16),
            pltpu.VMEM((max(hv, ff), rows), bf16),
            pltpu.VMEM((8 + 2 * nstate, width), f32),
            pltpu.VMEM((1, hv), f32),
            pltpu.VMEM((1, ff), f32),
            pltpu.VMEM((1, gates), f32),
            pltpu.VMEM((8, zd), f32),
            pltpu.VMEM((width // LANES, nstate * SEG, LANES), f32),
            pltpu.VMEM((width // LANES, nstate * SEG, LANES), f32),
            pltpu.VMEM((seq, nstate, width), f32),
            pltpu.VMEM((seq, nstate, width), f32),
            pltpu.SemaphoreType.DMA((8,)),
            pltpu.SemaphoreType.DMA((2,)),
            pltpu.SemaphoreType.DMA((seq,)),
            pltpu.SemaphoreType.DMA((seq,)),
            pltpu.SemaphoreType.DMA((seq,)),
            pltpu.SemaphoreType.DMA((seq,)),
            pltpu.VMEM((TILES, 2, BLOCK, TILE), f32),
            pltpu.SemaphoreType.DMA((stages, slots, 2)),
            pltpu.SemaphoreType.DMA((stages, slots, 2)),
            pltpu.SemaphoreType.REGULAR((stages, slots, 2)),
            pltpu.SemaphoreType.DMA((JOBS, 2)),
            pltpu.SemaphoreType.DMA((JOBS, HALVINGS, 2)),
            pltpu.SemaphoreType.DMA((JOBS, HALVINGS, 2)),
        ]
        + [pltpu.VMEM((slots, 2, count, TILE), f32) for count in stage_rows(stages)],
        compiler_params=pltpu.CompilerParams(
            collective_id=0, has_side_effects=True, vmem_limit_bytes=63 << 20
        ),
        cost_estimate=pl.CostEstimate(
            flops=52_000_000_000, bytes_accessed=60_000_000, transcendentals=20_000_000
        ),
    )(*operands)


def shards(
    batch,
    seq,
    tokens,
    lengths,
    cotangent,
    norm_gain,
    norm_shift,
    alpha_logit,
    delta_logit,
    ema_beta,
    ema_eta,
    ema_omega,
    w_value,
    b_value,
    w_gates,
    b_gates,
    query_key,
    position_bias,
    w_output,
    b_output,
    w_expand,
    b_expand,
    w_shrink,
    b_shrink,
):
    def lines(vector):
        return vector.reshape(-1, LANES)

    averages = (alpha_logit.T, delta_logit.T, ema_beta.T, ema_eta.T)
    operands = (tokens[0], cotangent[0], lengths, norm_gain.T, norm_shift.T) + averages
    operands += (lines(ema_omega), lines(b_output), lines(b_shrink))
    operands += (lines(b_value), lines(b_gates), lines(b_expand))
    operands += (query_key.T, position_bias[None])
    operands += (w_value, w_gates, w_output, w_expand, w_shrink)
    output, grad_tokens, dw_value, dw_gates, dw_output, dw_expand, dw_shrink, sums = layer(
        operands, batch, seq
    )
    like = (norm_gain.T, norm_shift.T) + averages
    like += (lines(ema_omega), lines(b_output), lines(b_shrink), query_key.T)
    like += (position_bias[None], lines(b_value), lines(b_expand), lines(b_gates))
    small = pl.pallas_call(
        finish, out_shape=tuple(jax.ShapeDtypeStruct(a.shape, f32) for a in like)
    )(sums, *averages)
    gain, shift, d_alpha, d_delta, d_beta, d_eta, d_omega, d_output, d_shrink = small[:9]
    d_qk, d_bias, d_value, d_expand, d_gates = small[9:]
    return (
        output[None],
        grad_tokens[None],
        gain.T,
        shift.T,
        d_alpha.T,
        d_delta.T,
        d_beta.T,
        d_eta.T,
        d_omega.reshape(-1),
        dw_value,
        d_value.reshape(-1),
        dw_gates,
        d_gates.reshape(-1),
        d_qk.T,
        d_bias[0],
        dw_output,
        d_output.reshape(-1),
        dw_expand,
        d_expand.reshape(-1),
        dw_shrink,
        d_shrink.reshape(-1),
    )


def solution(mesh):
    token_spec = P("batch", "seq", None)
    return jax.shard_map(
        functools.partial(shards, mesh.shape["batch"], mesh.shape["seq"]),
        mesh=mesh,
        in_specs=(token_spec, P("batch", None), token_spec) + (P(),) * 19,
        out_specs=(token_spec, token_spec) + (P(),) * 19,
        check_vma=False,
    )
```
